32 devices in a mesh: mob: 2 (over x), imm: 16 (over z, y, core).
Axes of the slice: x: 2, y: 2, z: 4, core: 2. Of those that a mesh axis runs over, the one named last changes fastest.
Arguments:
- mobile_positions: float32 [512, 3, 128], P(('mob', 'imm')), may hold values from 0 to 4
- walk: float32 [2, 512, 3, 128], P(None, ('mob', 'imm')), may hold values from -1.8 to 1.8
- mobile_conc: float32 [512, 8, 128], P(('mob', 'imm')), may hold values from 0 to 2
- matrix_positions: float32 [512, 3, 128], P(('mob', 'imm')), may hold values from 0 to 4
- matrix_conc: float32 [512, 8, 128], P(('mob', 'imm')), may hold values from 0 to 2
- pair_rows: int32 [2, 16, 512], P('mob', 'imm'), may hold values from 0 to 255, as said below
- pair_cols: int32 [2, 16, 512], P('mob', 'imm'), may hold values from 0 to 31
- pair_counts: int32 [2, 16], P('mob', 'imm'), may hold values from 128 to 512, as said below
Outputs:
- mobile_after: float32 [512, 8, 128], P(('mob', 'imm'))
- matrix_after: float32 [512, 8, 128], P(('mob', 'imm'))
The draws below stay inside these ranges and needn't reach their ends.
Inputs may be any that keep to these rules, and one draw needn't show every extreme that they name: Within one device the listed pairs (pair_rows, pair_cols) are distinct. `pair_counts`: in every draw some device uses all 512 slots.
All inputs are finite; a program needn't handle non-finite values.
Results may differ from the reference program's by a relative error of at most 0.0003.
Values sent between devices are 32-bit elements; how exact they have to be, the bound alone decides.
A program may use at most 64 MiB of HBM per device.

```python
import math
import jax
import jax.numpy as jnp
from jax import lax

PART = 128
SOLUTES = 8
MC_DEV = 16
IC_DEV = 16
PAIRS_DEV = 512
MCELLS = 512
ICELLS = 512
N_MOB = 2
N_IMM = 16


def pair_table(key):
    key = jax.random.fold_in(key, 11)
    tiles = N_MOB * N_IMM
    group_m = MC_DEV * N_IMM
    group_i = IC_DEV * N_MOB
    keys = jax.random.split(key, tiles)

    def one_tile(tile_key):
        key_a, key_b = jax.random.split(tile_key)
        order = jax.random.permutation(key_a, jnp.arange(group_m, dtype=jnp.int32))
        offset = jax.random.randint(key_b, (group_m,), 0, group_i, dtype=jnp.int32)
        slot = jnp.arange(PAIRS_DEV, dtype=jnp.int32)
        rows = order[slot % group_m]
        cols = (offset[slot % group_m] + slot // group_m) % group_i
        return (rows, cols)
    rows, cols = jax.vmap(one_tile)(keys)
    return (rows.reshape(N_MOB, N_IMM, PAIRS_DEV), cols.reshape(N_MOB, N_IMM, PAIRS_DEV))


def draw_pair_rows(key, part):
    return pair_table(key)[0]


def draw_pair_cols(key, part):
    return pair_table(key)[1]


def draw_pair_counts(key, part):
    key = jax.random.fold_in(key, 23)
    key_a, key_b, key_c = jax.random.split(key, 3)
    tiles = N_MOB * N_IMM
    base = PAIRS_DEV // 4 + jax.random.randint(key_a, (tiles,), 0, PAIRS_DEV // 4 + 1, dtype=jnp.int32)
    full = jax.random.randint(key_b, (tiles,), 0, 8, dtype=jnp.int32) == 0
    chosen = jax.random.randint(key_c, (), 0, tiles, dtype=jnp.int32)
    full = full | (jnp.arange(tiles, dtype=jnp.int32) == chosen)
    counts = jnp.where(full, PAIRS_DEV, base).astype(jnp.int32)
    return counts.reshape(N_MOB, N_IMM)


def shard_levels(rng, extent, cuts, low, top_value):
    def one(axis_at, parts):
        draws = jax.random.uniform(jax.random.fold_in(jax.random.fold_in(rng, 6), axis_at), (parts,), jnp.float32, low / len(cuts), top_value / len(cuts))
        return jnp.repeat(jnp.exp(draws), extent[axis_at] // parts).reshape((-1,) + (1,) * (len(extent) - axis_at - 1))

    gain = one(*cuts[0])
    for cut in cuts[1:]:
        gain = gain * one(*cut)
    return gain


def centred(stream_key, shape, deviation, bound, cuts=(), kind=jnp.bfloat16):
    result = deviation * jax.random.normal(stream_key, shape, jnp.float32)
    if cuts:
        result = result * shard_levels(stream_key, shape, cuts, -0.22, 0.18)
    return jnp.clip(result, -bound, bound).astype(kind)


def setup_inputs(seed: int = 0) -> dict:
    seeds = jax.random.split(jax.random.key(seed), 9)
    return {
        "mobile_positions": jnp.clip(4.0 * jax.random.uniform(seeds[0], (MCELLS, 3, PART), jnp.float32) ** shard_levels(seeds[0], (MCELLS, 3, PART), ((0, 32),), -0.2, 0.2), 0.0, 4.0),
        "walk": centred(seeds[1], (2, MCELLS, 3, PART), 0.3, 1.8, ((1, 32),), jnp.float32),
        "mobile_conc": jnp.clip(2.0 * jax.random.uniform(seeds[2], (MCELLS, SOLUTES, PART), jnp.float32) ** shard_levels(seeds[2], (MCELLS, SOLUTES, PART), ((0, 32),), -0.2, 0.2), 0.0, 2.0),
        "matrix_positions": jnp.clip(4.0 * jax.random.uniform(seeds[3], (ICELLS, 3, PART), jnp.float32) ** shard_levels(seeds[3], (ICELLS, 3, PART), ((0, 32),), -0.2, 0.2), 0.0, 4.0),
        "matrix_conc": jnp.clip(2.0 * jax.random.uniform(seeds[4], (ICELLS, SOLUTES, PART), jnp.float32) ** shard_levels(seeds[4], (ICELLS, SOLUTES, PART), ((0, 32),), -0.2, 0.2), 0.0, 2.0),
        "pair_rows": draw_pair_rows(jax.random.fold_in(seeds[8], 71), 0),
        "pair_cols": draw_pair_cols(jax.random.fold_in(seeds[8], 71), 0),
        "pair_counts": draw_pair_counts(jax.random.fold_in(seeds[8], 71), 0),
    }


RATE = 1.0 / 512.0


def pair_gains(mob_pos, imm_pos, mob_conc, imm_conc, valid):
    diff_x = mob_pos[:, 0, :, None] - imm_pos[:, 0, None, :]
    diff_y = mob_pos[:, 1, :, None] - imm_pos[:, 1, None, :]
    diff_z = mob_pos[:, 2, :, None] - imm_pos[:, 2, None, :]
    weight = jnp.exp(-0.5 * (diff_x * diff_x + diff_y * diff_y + diff_z * diff_z)) * valid[:, None, None]
    toward_m = jnp.einsum("kab,ksb->ksa", weight, imm_conc, precision=lax.Precision.HIGHEST)
    toward_i = jnp.einsum("kab,ksa->ksb", weight, mob_conc, precision=lax.Precision.HIGHEST)
    gain_m = RATE * (toward_m - jnp.sum(weight, axis=2)[:, None, :] * mob_conc)
    gain_i = RATE * (toward_i - jnp.sum(weight, axis=1)[:, None, :] * imm_conc)
    return gain_m, gain_i


def one_step(positions, mob_conc, imm_pos, imm_conc, mob_cells, imm_cells, valid):
    def scan_fn(carry, blk):
        delta_m, delta_i = carry
        mcell, icell, used = blk
        gain_m, gain_i = pair_gains(positions[mcell], imm_pos[icell], mob_conc[mcell], imm_conc[icell], used)
        return (delta_m.at[mcell].add(gain_m), delta_i.at[icell].add(gain_i)), None

    start = (jnp.zeros_like(mob_conc), jnp.zeros_like(imm_conc))
    (delta_m, delta_i), _ = lax.scan(scan_fn, start, (mob_cells, imm_cells, valid))
    return mob_conc + delta_m, imm_conc + delta_i


def reference(mobile_positions, walk, mobile_conc, matrix_positions, matrix_conc, pair_rows, pair_cols, pair_counts):
    moved_one = mobile_positions + walk[0]
    moved_two = moved_one + walk[1]
    tile_m = jnp.arange(N_MOB).astype(jnp.int32)[:, None, None]
    tile_i = jnp.arange(N_IMM).astype(jnp.int32)[None, :, None]
    mob_cells = tile_m * (N_IMM * MC_DEV) + pair_rows
    imm_cells = ((pair_cols // IC_DEV) * N_IMM + tile_i) * IC_DEV + pair_cols % IC_DEV
    slots = jnp.arange(PAIRS_DEV).astype(jnp.int32)[None, None, :]
    valid = jnp.where(slots < pair_counts[:, :, None], 1.0, 0.0).astype(jnp.float32)
    total = N_MOB * N_IMM * PAIRS_DEV
    blk = math.gcd(total, 512)
    mob_cells = mob_cells.reshape(-1, blk).astype(jnp.int32)
    imm_cells = imm_cells.reshape(-1, blk).astype(jnp.int32)
    valid = valid.reshape(-1, blk)
    mob_c, imm_c = one_step(moved_one, mobile_conc, matrix_positions, matrix_conc, mob_cells, imm_cells, valid)
    mob_c, imm_c = one_step(moved_two, mob_c, matrix_positions, imm_c, mob_cells, imm_cells, valid)
    return mob_c, imm_c
```

```python
import functools
import math

import jax
import jax.numpy as jnp
from jax import lax
from jax.experimental import pallas as pl
from jax.experimental.pallas import tpu as pltpu
from jax.sharding import PartitionSpec as P

RATE = 1.0 / 512.0
SCALE = math.sqrt(0.5 * math.log2(math.e))
CENTRE = 2.0
FAR = -30000.0
MESH = pl.DeviceIdType.MESH
VMEM_LIMIT = 56 * 1024 * 1024
UNROLL = 8
TERMS = 16
F32 = jnp.float32
BF16 = jnp.bfloat16


def sizes(n_mob, n_imm):
    rest = n_imm // 2
    nb = 1
    while nb * nb * 4 <= rest:
        nb *= 2
    return n_mob, nb, rest // nb


class Place:
    def __init__(self, n_mob, n_imm):
        self.nm, self.nb, self.na = sizes(n_mob, n_imm)
        self.p = lax.axis_index("mob")
        q = lax.axis_index("imm")
        self.core = lax.rem(q, 2)
        chip = lax.div(q, 2)
        self.b = lax.rem(chip, self.nb)
        self.a = lax.div(chip, self.nb)

    def am(self, d):
        return lax.rem(self.a + (d + self.na), self.na)

    def bm(self, d):
        return lax.rem(self.b + (d + self.nb), self.nb)

    def pm(self, d):
        return lax.rem(self.p + (d + self.nm), self.nm)

    def dev(self, p, a, b, core):
        return (p, (a * self.nb + b) * 2 + core)

    def along(self, da):
        return self.dev(self.p, self.am(da), self.b, self.core)

    def across(self, dp, db):
        return self.dev(self.pm(dp), self.a, self.bm(db), self.core)

    def sibling(self):
        return self.dev(self.p, self.a, self.b, 1 - self.core)

    def plane(self):
        return [(dp, db) for dp in range(self.nm) for db in range(self.nb) if dp or db]

    def slot(self, dp, db, core):
        return (self.pm(dp) * self.nb + self.bm(db)) * 2 + core

    def greet(self, lists=False):
        sem = pltpu.get_barrier_semaphore()
        peers = [self.sibling()]
        peers += [self.along(d) for d in range(1, self.na)]
        peers += [self.across(dp, db) for dp, db in self.plane()]
        if lists:
            peers += [self.dev(self.p, self.a, self.bm(db), 1 - self.core) for db in range(1, self.nb)]
        for peer in peers:
            pl.semaphore_signal(sem, inc=1, device_id=peer, device_id_type=MESH)
        return sem, len(peers)


def remote(src, dst, sems, index, device):
    copy = pltpu.make_async_remote_copy(
        src_ref=src, dst_ref=dst, send_sem=sems[0].at[index], recv_sem=sems[1].at[index],
        device_id=device, device_id_type=MESH,
    )
    copy.start()
    return copy


def split2(x):
    high = x.astype(BF16).astype(F32)
    return high, x - high


def split3(x):
    high, rest = split2(x)
    mid, low = split2(rest)
    return high, mid, low


def rows_x(x):
    (xh, xm), (yh, ym), (zh, zm) = [split2(x[j]) for j in range(3)]
    norm = split3(-(x[0] * x[0] + x[1] * x[1] + x[2] * x[2]))
    one = jnp.ones_like(x[0])
    return [xh, yh, zh, xh, yh, zh, xm, ym, zm, *norm, one, one, one, jnp.zeros_like(one)]


def rows_y(y):
    (xh, xm), (yh, ym), (zh, zm) = [split2(2.0 * y[j]) for j in range(3)]
    norm = split3(-(y[0] * y[0] + y[1] * y[1] + y[2] * y[2]))
    one = jnp.ones_like(y[0])
    return [xh, yh, zh, xm, ym, zm, xh, yh, zh, one, one, one, *norm, jnp.zeros_like(one)]


def fill(stage, rows):
    cells = rows[0].shape[0]
    for j, row in enumerate(rows):
        stage[pl.ds(j, cells, stride=TERMS), :] = row


def build_y(pos, stage, out, slot):
    cells = pos.shape[1]
    fill(stage, rows_y([pos[j] for j in range(3)]))
    out[pl.ds(slot * cells, cells)] = stage[...].reshape(cells, TERMS, 128).astype(BF16)


def build_x(pos, stage, out, slot):
    cells = pos.shape[1]
    fill(stage, rows_x([pos[j] for j in range(3)]))
    zeros = jnp.zeros((128 - TERMS, 128), F32)
    for cell in range(cells):
        block = jnp.concatenate([stage[cell * TERMS : (cell + 1) * TERMS, :], zeros], axis=0)
        out[slot * cells + cell] = block.T.astype(BF16)


def build_list(at, mc, ic, lists, keep_m, keep_i, keep_rank, out):
    lists_n, chunks = lists.shape[0], lists.shape[0] * 4
    cells_m = at.na * mc
    lines = (out.shape[0] - 8) // 3
    shift_m, shift_i, shift_b = [int(math.log2(n)) for n in (mc, ic, at.nb)]
    lane = lax.broadcasted_iota(jnp.int32, (1, 128), 1)
    mine = lax.broadcasted_iota(jnp.int32, (cells_m, 128), 0)
    upper = jnp.where(
        lax.broadcasted_iota(jnp.int32, (128, 128), 0) <= lax.broadcasted_iota(jnp.int32, (128, 128), 1), 1.0, 0.0
    ).astype(BF16)
    lower = jnp.where(
        lax.broadcasted_iota(jnp.int32, (cells_m, cells_m), 0)
        > lax.broadcasted_iota(jnp.int32, (cells_m, cells_m), 1), 1.0, 0.0
    ).astype(F32)

    def count(chunk, total):
        which, part = lax.div(chunk, 4), lax.rem(chunk, 4)
        r = lists[which, pl.ds(part, 1), :]
        c = lists[which, pl.ds(4 + part, 1), :]
        used = lists[which, 8:9, :]
        owner = jnp.right_shift(r, shift_m)
        ok = (
            (part * 128 + lane < used)
            & (jnp.bitwise_and(owner, 1) == at.core)
            & (jnp.bitwise_and(jnp.right_shift(owner, 1), at.nb - 1) == at.b)
        )
        m = jnp.right_shift(owner, 1 + shift_b) * mc + jnp.bitwise_and(r, mc - 1)
        m = jnp.where(ok, m, -1)
        i = (jnp.right_shift(c, shift_i) * lists_n + which) * ic + jnp.bitwise_and(c, ic - 1)
        hot = jnp.where(mine == m, 1.0, 0.0).astype(F32)
        rank = total + jnp.dot(hot.astype(BF16), upper, preferred_element_type=F32)
        keep_m[pl.ds(chunk, 1), :] = m
        keep_i[pl.ds(chunk, 1), :] = i + 1
        keep_rank[pl.ds(chunk, 1), :] = jnp.sum(hot * rank, axis=0, keepdims=True) - 1.0
        return jnp.broadcast_to(rank[:, 127:128], rank.shape)

    total = lax.fori_loop(0, chunks, count, jnp.zeros((cells_m, 128), F32))
    even = 2.0 * jnp.floor((total + 1.0) * 0.5)
    start = jnp.dot(lower, even, preferred_element_type=F32, precision=lax.Precision.HIGHEST)
    doubles = jnp.sum(even, axis=0, keepdims=True) * 0.5
    line = lax.broadcasted_iota(jnp.int32, (lines, 128), 0)
    column = lax.broadcasted_iota(jnp.int32, (128, 128), 0)

    def place(chunk, acc):
        m = keep_m[pl.ds(chunk, 1), :]
        i = keep_i[pl.ds(chunk, 1), :]
        hot = jnp.where(mine == m, 1.0, 0.0).astype(F32)
        spot = jnp.sum(hot * start, axis=0, keepdims=True) + keep_rank[pl.ds(chunk, 1), :]
        spot = jnp.where(m >= 0, spot.astype(jnp.int32), -1)
        double = jnp.right_shift(spot, 1)
        second = jnp.bitwise_and(spot, 1) == 1
        here = (line == jnp.right_shift(double, 7)) & (m >= 0)
        lane_hot = jnp.where(column == jnp.bitwise_and(double, 127), 1.0, 0.0).astype(BF16)
        high = jnp.right_shift(i, 6).astype(F32)
        low = jnp.bitwise_and(i, 63).astype(F32)
        zero = jnp.zeros((1, 128), F32)
        values = [
            jnp.where(second, zero, m.astype(F32)),
            jnp.where(second, zero, high),
            jnp.where(second, zero, low),
            jnp.where(second, high, zero),
            jnp.where(second, low, zero),
        ]
        left = jnp.concatenate([jnp.where(here, v, 0.0) for v in values], axis=0).astype(BF16)
        return acc + lax.dot_general(left, lane_hot, (((1,), (1,)), ((), ())), preferred_element_type=F32)

    acc = lax.fori_loop(0, chunks, place, jnp.zeros((5 * lines, 128), F32))
    m, high1, low1, high2, low2 = [
        acc[j * lines : (j + 1) * lines].astype(jnp.int32) for j in range(5)
    ]
    dummy = at.nm * lists_n * ic
    out[0:lines, :] = m
    for j, (high, low) in enumerate(((high1, low1), (high2, low2)), 1):
        i = high * 64 + low
        out[j * lines : (j + 1) * lines, :] = jnp.where(i == 0, dummy, i - 1)
    out[3 * lines : 3 * lines + 8, :] = jnp.broadcast_to(doubles.astype(jnp.int32), (8, 128))


def gather_plane_start(at, ref, own, sems):
    return {
        (dp, db): remote(own, ref.at[at.slot(0, 0, at.core)], sems, (dp, db), at.across(dp, db))
        for dp, db in at.plane()
    }


def pass_on(at, ref, sems, dp, db, source=None):
    block = ref.at[at.slot(-dp, -db, at.core)]
    return remote(block if source is None else source, block, sems, (dp, db), at.sibling())


def first_gather(n_mob, n_imm, mpos, walk, mconc, ipos, iconc, rows, cols, count,
                 g_conc, h_conc, x_one, y_all, pair_list, x_two,
                 g_pos, h_pos, lists, in_m, in_w, in_i, in_r, in_c, stage, keep_m, keep_i, keep_rank, *sems):
    at = Place(n_mob, n_imm)
    local, z_pos, z_conc, x_pos, x_conc, c_pos, c_conc, l_sem = (
        sems[0], sems[1:3], sems[3:5], sems[5:7], sems[7:9], sems[9:11], sems[11:13], sems[13:15])
    me = at.slot(0, 0, at.core)
    reads = [
        pltpu.make_async_copy(src, dst, local.at[j])
        for j, (src, dst) in enumerate((
            (mpos, in_m), (walk, in_w), (ipos, in_i), (rows, in_r), (cols, in_c),
            (mconc, g_conc.at[at.a]), (iconc, h_conc.at[me]),
        ))
    ]
    for read in reads:
        read.start()
    sem, peers = at.greet(lists=True)
    reads[0].wait()
    reads[1].wait()
    moved = in_m[...] + in_w[0]
    g_pos[at.a] = (moved - CENTRE) * SCALE
    x_two[...] = ((moved + in_w[1]) - CENTRE) * SCALE
    reads[2].wait()
    h_pos[me] = (in_i[...] - CENTRE) * SCALE
    reads[3].wait()
    reads[4].wait()
    home = at.b * 2 + at.core
    for j in range(4):
        lists[home, j : j + 1, :] = in_r[0, :, j * 128 : (j + 1) * 128]
        lists[home, 4 + j : 5 + j, :] = in_c[0, :, j * 128 : (j + 1) * 128]
    lists[home, 8:16, :] = jnp.full((8, 128), count[0, 0], jnp.int32)
    pl.semaphore_wait(sem, peers)
    order = list(range(1, at.na))
    far = {}
    for da in order:
        far[da] = remote(g_pos.at[at.a], g_pos.at[at.a], z_pos, da, at.along(da))
    share = []
    for db in range(at.nb):
        for dc in range(2):
            if db or dc:
                core = at.core if dc == 0 else 1 - at.core
                share.append(remote(
                    lists.at[home], lists.at[home], l_sem, (db, dc), at.dev(at.p, at.a, at.bm(db), core)))
    p_copies = gather_plane_start(at, h_pos, h_pos.at[me], x_pos)
    for da in order:
        far[at.na + da] = remote(mconc, g_conc.at[at.a], z_conc, da, at.along(da))
    q_copies = gather_plane_start(at, h_conc, iconc, x_conc)
    p_pass = {(0, 0): pass_on(at, h_pos, c_pos, 0, 0)}
    q_pass = {(0, 0): pass_on(at, h_conc, c_conc, 0, 0, iconc)}
    for copy in share:
        copy.wait_recv()
    build_x(g_pos.at[at.a], stage, x_one, at.a)
    build_y(h_pos.at[me], stage, y_all, me)
    build_list(at, mconc.shape[0], iconc.shape[0], lists, keep_m, keep_i, keep_rank, pair_list)
    for dp, db in at.plane():
        p_copies[dp, db].wait_recv()
        p_pass[dp, db] = pass_on(at, h_pos, c_pos, dp, db)
        here = at.slot(-dp, -db, at.core)
        build_y(h_pos.at[here], stage, y_all, here)
    cells_i = y_all.shape[0] - 8
    row = lax.broadcasted_iota(jnp.int32, (8, TERMS, 128), 1)
    y_all[cells_i:, :, :] = jnp.where(row == 12, FAR, 0.0).astype(BF16)
    for dp, db in at.plane():
        q_copies[dp, db].wait_recv()
        q_pass[dp, db] = pass_on(at, h_conc, c_conc, dp, db)
    for (dp, db), copy in p_pass.items():
        copy.wait_recv()
        there = at.slot(-dp, -db, 1 - at.core)
        build_y(h_pos.at[there], stage, y_all, there)
    for da in order:
        far[da].wait_recv()
        build_x(g_pos.at[at.am(-da)], stage, x_one, at.am(-da))
    for copy in q_pass.values():
        copy.wait_recv()
    for da in order:
        far[at.na + da].wait_recv()
    for read in reads[5:]:
        read.wait()
    for group in (far, p_copies, q_copies, p_pass, q_pass):
        for copy in group.values():
            copy.wait_send()
    for copy in share:
        copy.wait_send()


def reduce_start(at, part_m, part_i, land_m, land_c, z_sem, c_sem):
    mc = land_m.shape[1]
    ic = land_c.shape[2]
    z_copies, c_copies = {}, {}
    for da in range(1, at.na):
        z_copies[da] = remote(
            part_m.at[pl.ds(at.am(da) * mc, mc)], land_m.at[da], z_sem, da, at.along(da))
    for dp, db in at.plane() + [(0, 0)]:
        c_copies[dp, db] = remote(
            part_i.at[pl.ds(at.slot(dp, db, 1 - at.core) * ic, ic)], land_c.at[dp, db], c_sem, (dp, db), at.sibling())
    return z_copies, c_copies


def reduce_plane_start(at, part_i, land_c, out_b, land_b, c_copies, b_sem):
    ic = land_c.shape[2]
    b_copies = {}
    for dp, db in at.plane():
        c_copies[dp, db].wait_recv()
        out_b[dp, db] = part_i[pl.ds(at.slot(dp, db, at.core) * ic, ic)] + land_c[dp, db]
        b_copies[dp, db] = remote(out_b.at[dp, db], land_b.at[dp, db], b_sem, (dp, db), at.across(dp, db))
    return b_copies


def reduce_m(at, part_m, land_m, z_copies):
    mc = land_m.shape[1]
    total = part_m[pl.ds(at.a * mc, mc)]
    for da, copy in z_copies.items():
        copy.wait_recv()
        total = total + land_m[da]
    return total


def reduce_i(at, part_i, land_c, land_b, c_copies, b_copies):
    ic = land_c.shape[2]
    c_copies[0, 0].wait_recv()
    total = part_i[pl.ds(at.slot(0, 0, at.core) * ic, ic)] + land_c[0, 0]
    for key, copy in b_copies.items():
        copy.wait_recv()
        total = total + land_b[key]
    return total


def exchange(n_mob, n_imm, part_m, part_i, conc_m, conc_i, x_two, own_m, own_i, g_conc, h_conc, x_all,
             land_m, land_c, out_b, land_b, g_pos, stage, *sems):
    at = Place(n_mob, n_imm)
    z_sem, c_sem, b_sem, z_pos, z_conc, x_conc, c_conc = [sems[j : j + 2] for j in range(0, 14, 2)]
    sem, peers = at.greet()
    build_x(x_two, stage, x_all, at.a)
    pl.semaphore_wait(sem, peers)
    z_copies, c_copies = reduce_start(at, part_m, part_i, land_m, land_c, z_sem, c_sem)
    b_copies = reduce_plane_start(at, part_i, land_c, out_b, land_b, c_copies, b_sem)
    far = {}
    for da in range(1, at.na):
        far[da] = remote(x_two, g_pos.at[da], z_pos, da, at.along(da))
    me = at.slot(0, 0, at.core)
    own_i[...] = conc_i[...] + reduce_i(at, part_i, land_c, land_b, c_copies, b_copies)
    q_copies = gather_plane_start(at, h_conc, own_i, x_conc)
    q_pass = {(0, 0): pass_on(at, h_conc, c_conc, 0, 0, own_i)}
    h_conc[me] = own_i[...]
    own_m[...] = conc_m[...] + reduce_m(at, part_m, land_m, z_copies)
    for da in range(1, at.na):
        far[at.na + da] = remote(own_m, g_conc.at[at.a], z_conc, da, at.along(da))
    g_conc[at.a] = own_m[...]
    for da in range(1, at.na):
        far[da].wait_recv()
        build_x(g_pos.at[da], stage, x_all, at.am(-da))
    for dp, db in at.plane():
        q_copies[dp, db].wait_recv()
        q_pass[dp, db] = pass_on(at, h_conc, c_conc, dp, db)
    for copy in q_pass.values():
        copy.wait_recv()
    for da in range(1, at.na):
        far[at.na + da].wait_recv()
    for group in (z_copies, c_copies, b_copies, far, q_copies, q_pass):
        for copy in group.values():
            copy.wait_send()


def last_reduce(n_mob, n_imm, part_m, part_i, conc_m, conc_i, own_m, own_i,
                land_m, land_c, out_b, land_b, *sems):
    at = Place(n_mob, n_imm)
    z_sem, c_sem, b_sem = [sems[j : j + 2] for j in range(0, 6, 2)]
    sem, peers = at.greet()
    pl.semaphore_wait(sem, peers)
    z_copies, c_copies = reduce_start(at, part_m, part_i, land_m, land_c, z_sem, c_sem)
    b_copies = reduce_plane_start(at, part_i, land_c, out_b, land_b, c_copies, b_sem)
    own_i[...] = conc_i[...] + reduce_i(at, part_i, land_c, land_b, c_copies, b_copies)
    own_m[...] = conc_m[...] + reduce_m(at, part_m, land_m, z_copies)
    for group in (z_copies, c_copies, b_copies):
        for copy in group.values():
            copy.wait_send()


def conc_rows(conc):
    conc = conc * RATE
    high = conc.astype(BF16).astype(F32)
    ones = jnp.full_like(conc, RATE)
    return jnp.concatenate([high, conc - high, ones, ones], axis=0).astype(BF16)


def pair_loop(pair_list, x_all, y_all, x_conc, y_conc, gain_m, gain_i, lst, w_even, w_odd, m_rows, i_rows, sem):
    read = pltpu.make_async_copy(pair_list, lst, sem)
    read.start()
    gain_m[...] = jnp.zeros_like(gain_m)
    gain_i[...] = jnp.zeros_like(gain_i)
    w_odd[...] = jnp.zeros_like(w_odd)
    cells_i = y_conc.shape[0]

    def prepare_m(c, carry):
        m_rows[c] = conc_rows(x_conc[c])
        return carry

    def prepare_i(c, carry):
        i_rows[c] = conc_rows(y_conc[c])
        return carry

    lax.fori_loop(0, x_conc.shape[0], prepare_m, 0, unroll=8)
    lax.fori_loop(0, cells_i, prepare_i, 0, unroll=8)
    i_rows[cells_i] = jnp.zeros((32, 128), BF16)
    read.wait()
    lines = (lst.shape[0] - 8) // 3
    used = lst[3 * lines, 0]

    def entry(block, u):
        spot = block * UNROLL
        line, lane = lax.div(spot, 128), lax.rem(spot, 128) + u
        return lst[line, lane], lst[lines + line, lane], lst[2 * lines + line, lane]

    def weigh(block, u, out):
        m, i, k = entry(block, u)
        right = jnp.concatenate([y_all[i], y_all[k]], axis=1)
        power = jnp.dot(x_all[m][:, :TERMS], right, preferred_element_type=F32)
        out[u] = jnp.exp2(power).astype(BF16)

    def transfer(block, u, weights):
        m, i, k = entry(block, u)
        weight = weights[u]
        to_i = jnp.dot(m_rows[m], weight, preferred_element_type=F32)
        right = jnp.concatenate([i_rows[i], i_rows[k]], axis=1)
        to_m = lax.dot_general(right, weight, (((1,), (1,)), ((), ())), preferred_element_type=F32)
        return m, i, k, to_i, to_m

    def finish(m, i, k, to_i, to_m):
        gain_m[m] += to_m[0:8] + to_m[8:16] - to_m[16:24] * x_conc[m]
        add_i = to_i[0:8, :128] + to_i[8:16, :128] - to_i[16:24, :128] * y_conc[jnp.minimum(i, cells_i - 1)]
        add_k = to_i[0:8, 128:] + to_i[8:16, 128:] - to_i[16:24, 128:] * y_conc[jnp.minimum(k, cells_i - 1)]
        gain_i[i] += add_i
        gain_i[k] += add_k

    def half(block, out, weights):
        before = jnp.maximum(block - 1, 0)
        moved = []
        for u in range(UNROLL):
            moved.append(transfer(before, u, weights))
            weigh(block, u, out)
        for item in moved:
            finish(*item)

    def body(t, carry):
        half(2 * t, w_even, w_odd)
        half(2 * t + 1, w_odd, w_even)
        return carry

    blocks = lax.div(used + (UNROLL - 1), UNROLL)
    lax.fori_loop(0, lax.div(blocks + 2, 2), body, 0)


def on_device(n_mob, n_imm, mpos, walk, mconc, ipos, iconc, rows, cols, counts):
    nm, nb, na = sizes(n_mob, n_imm)
    mc, solutes, part = mconc.shape
    ic = iconc.shape[0]
    slots = nm * nb * 2
    cells_m, cells_i = na * mc, slots * ic
    tiles = nb * 2
    chunks = tiles * 4
    lines = -(-(chunks * 64 + cells_m // 2 + 4 * UNROLL) // 128)
    lines = -(-lines // 16) * 16
    vmem = pl.BlockSpec(memory_space=pltpu.VMEM)
    smem = pl.BlockSpec(memory_space=pltpu.SMEM)
    anywhere = pl.BlockSpec(memory_space=pl.ANY)
    dma = pltpu.SemaphoreType.DMA

    def params(ident):
        return pltpu.CompilerParams(collective_id=ident, has_side_effects=True, vmem_limit_bytes=VMEM_LIMIT)

    def shape(dims, dtype=F32):
        return jax.ShapeDtypeStruct(dims, dtype)

    def pairs(*dims):
        return [dma(dims)] * 2

    cell_m, cell_i = (mc, solutes, part), (ic, solutes, part)
    all_m, all_i = (na,) + cell_m, (slots,) + cell_i
    pos_m, pos_i = (3, mc, part), (3, ic, part)
    stage = pltpu.VMEM((max(mc, ic) * TERMS, part), F32)
    x_shape = shape((cells_m, part, 128), BF16)
    g_conc, h_conc, x_one, y_all, pair_list, x_two = pl.pallas_call(
        functools.partial(first_gather, n_mob, n_imm),
        out_shape=(
            shape(all_m), shape(all_i), x_shape, shape((cells_i + 8, TERMS, part), BF16),
            shape((3 * lines + 8, 128), jnp.int32), shape(pos_m),
        ),
        in_specs=[anywhere] * 7 + [smem],
        out_specs=(vmem,) * 6,
        scratch_shapes=[
            pltpu.VMEM((na,) + pos_m, F32), pltpu.VMEM((slots,) + pos_i, F32),
            pltpu.VMEM((tiles, 16, 128), jnp.int32),
            pltpu.VMEM(pos_m, F32), pltpu.VMEM((2,) + pos_m, F32), pltpu.VMEM(pos_i, F32),
            pltpu.VMEM(rows.shape, jnp.int32), pltpu.VMEM(cols.shape, jnp.int32), stage,
            pltpu.VMEM((chunks, 128), jnp.int32), pltpu.VMEM((chunks, 128), jnp.int32),
            pltpu.VMEM((chunks, 128), F32),
            dma((7,)), *pairs(na), *pairs(na), *pairs(nm, nb), *pairs(nm, nb), *pairs(nm, nb), *pairs(nm, nb),
            *pairs(nb, 2),
        ],
        compiler_params=params(0),
    )(jnp.transpose(mpos, (1, 0, 2)), jnp.transpose(walk, (0, 2, 1, 3)), mconc,
      jnp.transpose(ipos, (1, 0, 2)), iconc, rows, cols, counts)

    def gains(x_all, x_conc, y_conc):
        return pl.pallas_call(
            pair_loop,
            out_shape=(shape((cells_m, solutes, part)), shape((cells_i + 1, solutes, part))),
            in_specs=[anywhere] + [vmem] * 4,
            out_specs=(vmem,) * 2,
            scratch_shapes=[
                pltpu.SMEM(pair_list.shape, jnp.int32),
                pltpu.VMEM((UNROLL, part, 256), BF16), pltpu.VMEM((UNROLL, part, 256), BF16),
                pltpu.VMEM((cells_m, 32, part), BF16), pltpu.VMEM((cells_i + 1, 32, part), BF16),
                dma,
            ],
            compiler_params=pltpu.CompilerParams(vmem_limit_bytes=VMEM_LIMIT),
        )(pair_list, x_all, y_all,
          x_conc.reshape((cells_m, solutes, part)), y_conc.reshape((cells_i, solutes, part)))

    lands = [
        pltpu.VMEM((na,) + cell_m, F32),
        pltpu.VMEM((nm, nb) + cell_i, F32), pltpu.VMEM((nm, nb) + cell_i, F32), pltpu.VMEM((nm, nb) + cell_i, F32),
    ]
    reduce_sems = [*pairs(na), *pairs(nm, nb), *pairs(nm, nb)]
    own = (shape(cell_m), shape(cell_i))
    part_m, part_i = gains(x_one, g_conc, h_conc)
    own_m, own_i, g_conc, h_conc, x_all = pl.pallas_call(
        functools.partial(exchange, n_mob, n_imm),
        out_shape=own + (shape(all_m), shape(all_i), x_shape),
        in_specs=[vmem] * 5,
        out_specs=(vmem,) * 5,
        scratch_shapes=lands + [pltpu.VMEM((na,) + pos_m, F32), stage] + reduce_sems + [
            *pairs(na), *pairs(na), *pairs(nm, nb), *pairs(nm, nb)],
        compiler_params=params(1),
    )(part_m, part_i, mconc, iconc, x_two)
    part_m, part_i = gains(x_all, g_conc, h_conc)
    return pl.pallas_call(
        functools.partial(last_reduce, n_mob, n_imm),
        out_shape=own,
        in_specs=[vmem] * 4,
        out_specs=(vmem,) * 2,
        scratch_shapes=lands + reduce_sems,
        compiler_params=params(2),
    )(part_m, part_i, own_m, own_i)


def solution(mesh):
    return jax.shard_map(
        functools.partial(on_device, mesh.shape["mob"], mesh.shape["imm"]),
        mesh=mesh,
        in_specs=(
            P(("mob", "imm"), None, None),
            P(None, ("mob", "imm"), None, None),
            P(("mob", "imm"), None, None),
            P(("mob", "imm"), None, None),
            P(("mob", "imm"), None, None),
            P("mob", "imm", None),
            P("mob", "imm", None),
            P("mob", "imm"),
        ),
        out_specs=(P(("mob", "imm"), None, None), P(("mob", "imm"), None, None)),
        check_vma=False,
    )
```

```python
import functools
import math

import jax
import jax.numpy as jnp
from jax import lax
from jax.experimental import pallas as pl
from jax.experimental.pallas import tpu as pltpu
from jax.sharding import PartitionSpec as P

RATE = 1.0 / 512.0
SCALE = math.sqrt(0.5 * math.log2(math.e))
CENTRE = 2.0
FAR = -30000.0
MESH = pl.DeviceIdType.MESH
VMEM_LIMIT = 20 * 1024 * 1024
UNROLL = 8
TERMS = 16
F32 = jnp.float32
BF16 = jnp.bfloat16


def sizes(n_mob, n_imm):
    rest = n_imm // 2
    nb = 1
    while nb * nb * 4 <= rest:
        nb *= 2
    return n_mob, nb, rest // nb


class Place:
    def __init__(self, n_mob, n_imm):
        self.nm, self.nb, self.na = sizes(n_mob, n_imm)
        self.p = lax.axis_index("mob")
        q = lax.axis_index("imm")
        self.core = lax.rem(q, 2)
        chip = lax.div(q, 2)
        self.b = lax.rem(chip, self.nb)
        self.a = lax.div(chip, self.nb)

    def am(self, d):
        return lax.rem(self.a + (d + self.na), self.na)

    def bm(self, d):
        return lax.rem(self.b + (d + self.nb), self.nb)

    def pm(self, d):
        return lax.rem(self.p + (d + self.nm), self.nm)

    def dev(self, p, a, b, core):
        return (p, (a * self.nb + b) * 2 + core)

    def along(self, da):
        return self.dev(self.p, self.am(da), self.b, self.core)

    def across(self, dp, db):
        return self.dev(self.pm(dp), self.a, self.bm(db), self.core)

    def sibling(self):
        return self.dev(self.p, self.a, self.b, 1 - self.core)

    def plane(self):
        return [(dp, db) for dp in range(self.nm) for db in range(self.nb) if dp or db]

    def slot(self, dp, db, core):
        return (self.pm(dp) * self.nb + self.bm(db)) * 2 + core

    def greet(self, lists=False):
        sem = pltpu.get_barrier_semaphore()
        peers = [self.sibling()]
        peers += [self.along(d) for d in range(1, self.na)]
        peers += [self.across(dp, db) for dp, db in self.plane()]
        if lists:
            peers += [self.dev(self.p, self.a, self.bm(db), 1 - self.core) for db in range(1, self.nb)]
        for peer in peers:
            pl.semaphore_signal(sem, inc=1, device_id=peer, device_id_type=MESH)
        return sem, len(peers)


def remote(src, dst, sems, index, device):
    copy = pltpu.make_async_remote_copy(
        src_ref=src, dst_ref=dst, send_sem=sems[0].at[index], recv_sem=sems[1].at[index],
        device_id=device, device_id_type=MESH,
    )
    copy.start()
    return copy


def split2(x):
    high = x.astype(BF16).astype(F32)
    return high, x - high


def split3(x):
    high, rest = split2(x)
    mid, low = split2(rest)
    return high, mid, low


def rows_x(x):
    (xh, xm), (yh, ym), (zh, zm) = [split2(x[j]) for j in range(3)]
    norm = split3(-(x[0] * x[0] + x[1] * x[1] + x[2] * x[2]))
    one = jnp.ones_like(x[0])
    return [xh, yh, zh, xh, yh, zh, xm, ym, zm, *norm, one, one, one, jnp.zeros_like(one)]


def rows_y(y):
    (xh, xm), (yh, ym), (zh, zm) = [split2(2.0 * y[j]) for j in range(3)]
    norm = split3(-(y[0] * y[0] + y[1] * y[1] + y[2] * y[2]))
    one = jnp.ones_like(y[0])
    return [xh, yh, zh, xm, ym, zm, xh, yh, zh, one, one, one, *norm, jnp.zeros_like(one)]


def fill(stage, rows):
    cells = rows[0].shape[0]
    for j, row in enumerate(rows):
        stage[pl.ds(j, cells, stride=TERMS), :] = row


def build_y(pos, stage, out, slot):
    cells = pos.shape[1]
    fill(stage, rows_y([pos[j] for j in range(3)]))
    out[pl.ds(slot * cells, cells)] = stage[...].reshape(cells, TERMS, 128).astype(BF16)


def build_x(pos, stage, out, slot):
    cells = pos.shape[1]
    fill(stage, rows_x([pos[j] for j in range(3)]))
    zeros = jnp.zeros((128 - TERMS, 128), F32)
    for cell in range(cells):
        block = jnp.concatenate([stage[cell * TERMS : (cell + 1) * TERMS, :], zeros], axis=0)
        out[slot * cells + cell] = block.T.astype(BF16)


def build_list(at, mc, ic, lists, keep_m, keep_i, keep_rank, out):
    lists_n, chunks = lists.shape[0], lists.shape[0] * 4
    cells_m = at.na * mc
    lines = (out.shape[0] - 8) // 3
    shift_m, shift_i, shift_b = [int(math.log2(n)) for n in (mc, ic, at.nb)]
    lane = lax.broadcasted_iota(jnp.int32, (1, 128), 1)
    mine = lax.broadcasted_iota(jnp.int32, (cells_m, 128), 0)
    upper = jnp.where(
        lax.broadcasted_iota(jnp.int32, (128, 128), 0) <= lax.broadcasted_iota(jnp.int32, (128, 128), 1), 1.0, 0.0
    ).astype(BF16)
    lower = jnp.where(
        lax.broadcasted_iota(jnp.int32, (cells_m, cells_m), 0)
        > lax.broadcasted_iota(jnp.int32, (cells_m, cells_m), 1), 1.0, 0.0
    ).astype(F32)

    def count(chunk, total):
        which, part = lax.div(chunk, 4), lax.rem(chunk, 4)
        r = lists[which, pl.ds(part, 1), :]
        c = lists[which, pl.ds(4 + part, 1), :]
        used = lists[which, 8:9, :]
        owner = jnp.right_shift(r, shift_m)
        ok = (
            (part * 128 + lane < used)
            & (jnp.bitwise_and(owner, 1) == at.core)
            & (jnp.bitwise_and(jnp.right_shift(owner, 1), at.nb - 1) == at.b)
        )
        m = jnp.right_shift(owner, 1 + shift_b) * mc + jnp.bitwise_and(r, mc - 1)
        m = jnp.where(ok, m, -1)
        i = (jnp.right_shift(c, shift_i) * lists_n + which) * ic + jnp.bitwise_and(c, ic - 1)
        hot = jnp.where(mine == m, 1.0, 0.0).astype(F32)
        rank = total + jnp.dot(hot.astype(BF16), upper, preferred_element_type=F32)
        keep_m[pl.ds(chunk, 1), :] = m
        keep_i[pl.ds(chunk, 1), :] = i + 1
        keep_rank[pl.ds(chunk, 1), :] = jnp.sum(hot * rank, axis=0, keepdims=True) - 1.0
        return jnp.broadcast_to(rank[:, 127:128], rank.shape)

    total = lax.fori_loop(0, chunks, count, jnp.zeros((cells_m, 128), F32))
    even = 2.0 * jnp.floor((total + 1.0) * 0.5)
    start = jnp.dot(lower, even, preferred_element_type=F32, precision=lax.Precision.HIGHEST)
    doubles = jnp.sum(even, axis=0, keepdims=True) * 0.5
    line = lax.broadcasted_iota(jnp.int32, (lines, 128), 0)
    column = lax.broadcasted_iota(jnp.int32, (128, 128), 0)

    def place(chunk, acc):
        m = keep_m[pl.ds(chunk, 1), :]
        i = keep_i[pl.ds(chunk, 1), :]
        hot = jnp.where(mine == m, 1.0, 0.0).astype(F32)
        spot = jnp.sum(hot * start, axis=0, keepdims=True) + keep_rank[pl.ds(chunk, 1), :]
        spot = jnp.where(m >= 0, spot.astype(jnp.int32), -1)
        double = jnp.right_shift(spot, 1)
        second = jnp.bitwise_and(spot, 1) == 1
        here = (line == jnp.right_shift(double, 7)) & (m >= 0)
        lane_hot = jnp.where(column == jnp.bitwise_and(double, 127), 1.0, 0.0).astype(BF16)
        high = jnp.right_shift(i, 6).astype(F32)
        low = jnp.bitwise_and(i, 63).astype(F32)
        zero = jnp.zeros((1, 128), F32)
        values = [
            jnp.where(second, zero, m.astype(F32)),
            jnp.where(second, zero, high),
            jnp.where(second, zero, low),
            jnp.where(second, high, zero),
            jnp.where(second, low, zero),
        ]
        left = jnp.concatenate([jnp.where(here, v, 0.0) for v in values], axis=0).astype(BF16)
        return acc + lax.dot_general(left, lane_hot, (((1,), (1,)), ((), ())), preferred_element_type=F32)

    acc = lax.fori_loop(0, chunks, place, jnp.zeros((5 * lines, 128), F32))
    m, high1, low1, high2, low2 = [
        acc[j * lines : (j + 1) * lines].astype(jnp.int32) for j in range(5)
    ]
    dummy = at.nm * lists_n * ic
    out[0:lines, :] = m
    for j, (high, low) in enumerate(((high1, low1), (high2, low2)), 1):
        i = high * 64 + low
        out[j * lines : (j + 1) * lines, :] = jnp.where(i == 0, dummy, i - 1)
    out[3 * lines : 3 * lines + 8, :] = jnp.broadcast_to(doubles.astype(jnp.int32), (8, 128))


def gather_plane_start(at, ref, own, sems):
    return {
        (dp, db): remote(own, ref.at[at.slot(0, 0, at.core)], sems, (dp, db), at.across(dp, db))
        for dp, db in at.plane()
    }


def pass_on(at, ref, sems, dp, db, source=None):
    block = ref.at[at.slot(-dp, -db, at.core)]
    return remote(block if source is None else source, block, sems, (dp, db), at.sibling())


def first_gather(n_mob, n_imm, mpos, walk, mconc, ipos, iconc, rows, cols, count,
                 g_conc, h_conc, x_one, y_all, pair_list, x_two,
                 g_pos, h_pos, lists, in_m, in_w, in_i, in_r, in_c, stage, keep_m, keep_i, keep_rank, *sems):
    at = Place(n_mob, n_imm)
    local, z_pos, z_conc, x_pos, x_conc, c_pos, c_conc, l_sem = (
        sems[0], sems[1:3], sems[3:5], sems[5:7], sems[7:9], sems[9:11], sems[11:13], sems[13:15])
    me = at.slot(0, 0, at.core)
    reads = [
        pltpu.make_async_copy(src, dst, local.at[j])
        for j, (src, dst) in enumerate((
            (mpos, in_m), (walk, in_w), (ipos, in_i), (rows, in_r), (cols, in_c),
            (mconc, g_conc.at[at.a]), (iconc, h_conc.at[me]),
        ))
    ]
    for read in reads:
        read.start()
    sem, peers = at.greet(lists=True)
    reads[0].wait()
    reads[1].wait()
    moved = in_m[...] + in_w[0]
    g_pos[at.a] = (moved - CENTRE) * SCALE
    x_two[...] = ((moved + in_w[1]) - CENTRE) * SCALE
    reads[2].wait()
    h_pos[me] = (in_i[...] - CENTRE) * SCALE
    reads[3].wait()
    reads[4].wait()
    home = at.b * 2 + at.core
    for j in range(4):
        lists[home, j : j + 1, :] = in_r[0, :, j * 128 : (j + 1) * 128]
        lists[home, 4 + j : 5 + j, :] = in_c[0, :, j * 128 : (j + 1) * 128]
    lists[home, 8:16, :] = jnp.full((8, 128), count[0, 0], jnp.int32)
    pl.semaphore_wait(sem, peers)
    order = list(range(1, at.na))
    far = {}
    for da in order:
        far[da] = remote(g_pos.at[at.a], g_pos.at[at.a], z_pos, da, at.along(da))
    share = []
    for db in range(at.nb):
        for dc in range(2):
            if db or dc:
                core = at.core if dc == 0 else 1 - at.core
                share.append(remote(
                    lists.at[home], lists.at[home], l_sem, (db, dc), at.dev(at.p, at.a, at.bm(db), core)))
    p_copies = gather_plane_start(at, h_pos, h_pos.at[me], x_pos)
    for da in order:
        far[at.na + da] = remote(mconc, g_conc.at[at.a], z_conc, da, at.along(da))
    q_copies = gather_plane_start(at, h_conc, iconc, x_conc)
    p_pass = {(0, 0): pass_on(at, h_pos, c_pos, 0, 0)}
    q_pass = {(0, 0): pass_on(at, h_conc, c_conc, 0, 0, iconc)}
    for copy in share:
        copy.wait_recv()
    build_x(g_pos.at[at.a], stage, x_one, at.a)
    build_y(h_pos.at[me], stage, y_all, me)
    build_list(at, mconc.shape[0], iconc.shape[0], lists, keep_m, keep_i, keep_rank, pair_list)
    for dp, db in at.plane():
        p_copies[dp, db].wait_recv()
        p_pass[dp, db] = pass_on(at, h_pos, c_pos, dp, db)
        here = at.slot(-dp, -db, at.core)
        build_y(h_pos.at[here], stage, y_all, here)
    cells_i = y_all.shape[0] - 8
    row = lax.broadcasted_iota(jnp.int32, (8, TERMS, 128), 1)
    y_all[cells_i:, :, :] = jnp.where(row == 12, FAR, 0.0).astype(BF16)
    for dp, db in at.plane():
        q_copies[dp, db].wait_recv()
        q_pass[dp, db] = pass_on(at, h_conc, c_conc, dp, db)
    for (dp, db), copy in p_pass.items():
        copy.wait_recv()
        there = at.slot(-dp, -db, 1 - at.core)
        build_y(h_pos.at[there], stage, y_all, there)
    for da in order:
        far[da].wait_recv()
        build_x(g_pos.at[at.am(-da)], stage, x_one, at.am(-da))
    for copy in q_pass.values():
        copy.wait_recv()
    for da in order:
        far[at.na + da].wait_recv()
    for read in reads[5:]:
        read.wait()
    for group in (far, p_copies, q_copies, p_pass, q_pass):
        for copy in group.values():
            copy.wait_send()
    for copy in share:
        copy.wait_send()


def reduce_start(at, part_m, part_i, land_m, land_c, z_sem, c_sem):
    mc = land_m.shape[1]
    ic = land_c.shape[2]
    z_copies, c_copies = {}, {}
    for da in range(1, at.na):
        z_copies[da] = remote(
            part_m.at[pl.ds(at.am(da) * mc, mc)], land_m.at[da], z_sem, da, at.along(da))
    for dp, db in at.plane() + [(0, 0)]:
        c_copies[dp, db] = remote(
            part_i.at[pl.ds(at.slot(dp, db, 1 - at.core) * ic, ic)], land_c.at[dp, db], c_sem, (dp, db), at.sibling())
    return z_copies, c_copies


def reduce_plane_start(at, part_i, land_c, out_b, land_b, c_copies, b_sem):
    ic = land_c.shape[2]
    b_copies = {}
    for dp, db in at.plane():
        c_copies[dp, db].wait_recv()
        out_b[dp, db] = part_i[pl.ds(at.slot(dp, db, at.core) * ic, ic)] + land_c[dp, db]
        b_copies[dp, db] = remote(out_b.at[dp, db], land_b.at[dp, db], b_sem, (dp, db), at.across(dp, db))
    return b_copies


def reduce_m(at, part_m, land_m, z_copies):
    mc = land_m.shape[1]
    total = part_m[pl.ds(at.a * mc, mc)]
    for da, copy in z_copies.items():
        copy.wait_recv()
        total = total + land_m[da]
    return total


def reduce_i(at, part_i, land_c, land_b, c_copies, b_copies):
    ic = land_c.shape[2]
    c_copies[0, 0].wait_recv()
    total = part_i[pl.ds(at.slot(0, 0, at.core) * ic, ic)] + land_c[0, 0]
    for key, copy in b_copies.items():
        copy.wait_recv()
        total = total + land_b[key]
    return total


def exchange(n_mob, n_imm, part_m, part_i, conc_m, conc_i, x_two, own_m, own_i, g_conc, h_conc, x_all,
             land_m, land_c, out_b, land_b, g_pos, stage, *sems):
    at = Place(n_mob, n_imm)
    z_sem, c_sem, b_sem, z_pos, z_conc, x_conc, c_conc = [sems[j : j + 2] for j in range(0, 14, 2)]
    sem, peers = at.greet()
    build_x(x_two, stage, x_all, at.a)
    pl.semaphore_wait(sem, peers)
    z_copies, c_copies = reduce_start(at, part_m, part_i, land_m, land_c, z_sem, c_sem)
    b_copies = reduce_plane_start(at, part_i, land_c, out_b, land_b, c_copies, b_sem)
    far = {}
    for da in range(1, at.na):
        far[da] = remote(x_two, g_pos.at[da], z_pos, da, at.along(da))
    me = at.slot(0, 0, at.core)
    own_i[...] = conc_i[...] + reduce_i(at, part_i, land_c, land_b, c_copies, b_copies)
    q_copies = gather_plane_start(at, h_conc, own_i, x_conc)
    q_pass = {(0, 0): pass_on(at, h_conc, c_conc, 0, 0, own_i)}
    h_conc[me] = own_i[...]
    own_m[...] = conc_m[...] + reduce_m(at, part_m, land_m, z_copies)
    for da in range(1, at.na):
        far[at.na + da] = remote(own_m, g_conc.at[at.a], z_conc, da, at.along(da))
    g_conc[at.a] = own_m[...]
    for da in range(1, at.na):
        far[da].wait_recv()
        build_x(g_pos.at[da], stage, x_all, at.am(-da))
    for dp, db in at.plane():
        q_copies[dp, db].wait_recv()
        q_pass[dp, db] = pass_on(at, h_conc, c_conc, dp, db)
    for copy in q_pass.values():
        copy.wait_recv()
    for da in range(1, at.na):
        far[at.na + da].wait_recv()
    for group in (z_copies, c_copies, b_copies, far, q_copies, q_pass):
        for copy in group.values():
            copy.wait_send()


def last_reduce(n_mob, n_imm, part_m, part_i, conc_m, conc_i, own_m, own_i,
                land_m, land_c, out_b, land_b, *sems):
    at = Place(n_mob, n_imm)
    z_sem, c_sem, b_sem = [sems[j : j + 2] for j in range(0, 6, 2)]
    sem, peers = at.greet()
    pl.semaphore_wait(sem, peers)
    z_copies, c_copies = reduce_start(at, part_m, part_i, land_m, land_c, z_sem, c_sem)
    b_copies = reduce_plane_start(at, part_i, land_c, out_b, land_b, c_copies, b_sem)
    own_i[...] = conc_i[...] + reduce_i(at, part_i, land_c, land_b, c_copies, b_copies)
    own_m[...] = conc_m[...] + reduce_m(at, part_m, land_m, z_copies)
    for group in (z_copies, c_copies, b_copies):
        for copy in group.values():
            copy.wait_send()


def conc_rows(conc):
    conc = conc * RATE
    high = conc.astype(BF16).astype(F32)
    ones = jnp.full_like(conc, RATE)
    return jnp.concatenate([high, conc - high, ones, ones], axis=0).astype(BF16)


def pair_loop(pair_list, x_all, y_all, x_conc, y_conc, gain_m, gain_i, lst, w_even, w_odd, m_rows, i_rows, sem):
    read = pltpu.make_async_copy(pair_list, lst, sem)
    read.start()
    gain_m[...] = jnp.zeros_like(gain_m)
    gain_i[...] = jnp.zeros_like(gain_i)
    w_odd[...] = jnp.zeros_like(w_odd)
    cells_i = y_conc.shape[0]

    def prepare_m(c, carry):
        m_rows[c] = conc_rows(x_conc[c])
        return carry

    def prepare_i(c, carry):
        i_rows[c] = conc_rows(y_conc[c])
        return carry

    lax.fori_loop(0, x_conc.shape[0], prepare_m, 0, unroll=8)
    lax.fori_loop(0, cells_i, prepare_i, 0, unroll=8)
    i_rows[cells_i] = jnp.zeros((32, 128), BF16)
    read.wait()
    lines = (lst.shape[0] - 8) // 3
    used = lst[3 * lines, 0]

    def entry(block, u):
        spot = block * UNROLL
        line, lane = lax.div(spot, 128), lax.rem(spot, 128) + u
        return lst[line, lane], lst[lines + line, lane], lst[2 * lines + line, lane]

    def weigh(block, u, out):
        m, i, k = entry(block, u)
        right = jnp.concatenate([y_all[i], y_all[k]], axis=1)
        power = jnp.dot(x_all[m][:, :TERMS], right, preferred_element_type=F32)
        out[u] = jnp.exp2(power).astype(BF16)

    def transfer(block, u, weights):
        m, i, k = entry(block, u)
        weight = weights[u]
        to_i = jnp.dot(m_rows[m], weight, preferred_element_type=F32)
        right = jnp.concatenate([i_rows[i], i_rows[k]], axis=1)
        to_m = lax.dot_general(right, weight, (((1,), (1,)), ((), ())), preferred_element_type=F32)
        return m, i, k, to_i, to_m

    def finish(m, i, k, to_i, to_m):
        gain_m[m] += to_m[0:8] + to_m[8:16] - to_m[16:24] * x_conc[m]
        add_i = to_i[0:8, :128] + to_i[8:16, :128] - to_i[16:24, :128] * y_conc[jnp.minimum(i, cells_i - 1)]
        add_k = to_i[0:8, 128:] + to_i[8:16, 128:] - to_i[16:24, 128:] * y_conc[jnp.minimum(k, cells_i - 1)]
        gain_i[i] += add_i
        gain_i[k] += add_k

    def half(block, out, weights):
        before = jnp.maximum(block - 1, 0)
        moved = []
        for u in range(UNROLL):
            moved.append(transfer(before, u, weights))
            weigh(block, u, out)
        for item in moved:
            finish(*item)

    def body(t, carry):
        half(2 * t, w_even, w_odd)
        half(2 * t + 1, w_odd, w_even)
        return carry

    blocks = lax.div(used + (UNROLL - 1), UNROLL)
    lax.fori_loop(0, lax.div(blocks + 2, 2), body, 0)


def on_device(n_mob, n_imm, mpos, walk, mconc, ipos, iconc, rows, cols, counts):
    nm, nb, na = sizes(n_mob, n_imm)
    mc, solutes, part = mconc.shape
    ic = iconc.shape[0]
    slots = nm * nb * 2
    cells_m, cells_i = na * mc, slots * ic
    tiles = nb * 2
    chunks = tiles * 4
    lines = -(-(chunks * 64 + cells_m // 2 + 4 * UNROLL) // 128)
    lines = -(-lines // 16) * 16
    vmem = pl.BlockSpec(memory_space=pltpu.VMEM)
    smem = pl.BlockSpec(memory_space=pltpu.SMEM)
    anywhere = pl.BlockSpec(memory_space=pl.ANY)
    hbm = pl.BlockSpec(memory_space=pltpu.HBM)
    dma = pltpu.SemaphoreType.DMA

    def params(ident):
        return pltpu.CompilerParams(collective_id=ident, has_side_effects=True, vmem_limit_bytes=VMEM_LIMIT)

    def shape(dims, dtype=F32):
        return jax.ShapeDtypeStruct(dims, dtype)

    def pairs(*dims):
        return [dma(dims)] * 2

    cell_m, cell_i = (mc, solutes, part), (ic, solutes, part)
    all_m, all_i = (na,) + cell_m, (slots,) + cell_i
    pos_m, pos_i = (3, mc, part), (3, ic, part)
    stage = pltpu.VMEM((max(mc, ic) * TERMS, part), F32)
    x_shape = shape((cells_m, part, 128), BF16)
    g_conc, h_conc, x_one, y_all, pair_list, x_two = pl.pallas_call(
        functools.partial(first_gather, n_mob, n_imm),
        out_shape=(
            shape(all_m), shape(all_i), x_shape, shape((cells_i + 8, TERMS, part), BF16),
            shape((3 * lines + 8, 128), jnp.int32), shape(pos_m),
        ),
        in_specs=[hbm] * 7 + [smem],
        out_specs=(vmem,) * 6,
        scratch_shapes=[
            pltpu.VMEM((na,) + pos_m, F32), pltpu.VMEM((slots,) + pos_i, F32),
            pltpu.VMEM((tiles, 16, 128), jnp.int32),
            pltpu.VMEM(pos_m, F32), pltpu.VMEM((2,) + pos_m, F32), pltpu.VMEM(pos_i, F32),
            pltpu.VMEM(rows.shape, jnp.int32), pltpu.VMEM(cols.shape, jnp.int32), stage,
            pltpu.VMEM((chunks, 128), jnp.int32), pltpu.VMEM((chunks, 128), jnp.int32),
            pltpu.VMEM((chunks, 128), F32),
            dma((7,)), *pairs(na), *pairs(na), *pairs(nm, nb), *pairs(nm, nb), *pairs(nm, nb), *pairs(nm, nb),
            *pairs(nb, 2),
        ],
        compiler_params=params(0),
    )(*[
        pltpu.with_memory_space_constraint(x, pltpu.HBM)
        for x in (jnp.transpose(mpos, (1, 0, 2)), jnp.transpose(walk, (0, 2, 1, 3)), mconc,
                  jnp.transpose(ipos, (1, 0, 2)), iconc, rows, cols)
    ], counts)

    def gains(x_all, x_conc, y_conc):
        return pl.pallas_call(
            pair_loop,
            out_shape=(shape((cells_m, solutes, part)), shape((cells_i + 1, solutes, part))),
            in_specs=[anywhere] + [vmem] * 4,
            out_specs=(vmem,) * 2,
            scratch_shapes=[
                pltpu.SMEM(pair_list.shape, jnp.int32),
                pltpu.VMEM((UNROLL, part, 256), BF16), pltpu.VMEM((UNROLL, part, 256), BF16),
                pltpu.VMEM((cells_m, 32, part), BF16), pltpu.VMEM((cells_i + 1, 32, part), BF16),
                dma,
            ],
            compiler_params=pltpu.CompilerParams(vmem_limit_bytes=VMEM_LIMIT),
        )(pair_list, x_all, y_all,
          x_conc.reshape((cells_m, solutes, part)), y_conc.reshape((cells_i, solutes, part)))

    lands = [
        pltpu.VMEM((na,) + cell_m, F32),
        pltpu.VMEM((nm, nb) + cell_i, F32), pltpu.VMEM((nm, nb) + cell_i, F32), pltpu.VMEM((nm, nb) + cell_i, F32),
    ]
    reduce_sems = [*pairs(na), *pairs(nm, nb), *pairs(nm, nb)]
    own = (shape(cell_m), shape(cell_i))
    part_m, part_i = gains(x_one, g_conc, h_conc)
    own_m, own_i, g_conc, h_conc, x_all = pl.pallas_call(
        functools.partial(exchange, n_mob, n_imm),
        out_shape=own + (shape(all_m), shape(all_i), x_shape),
        in_specs=[vmem] * 5,
        out_specs=(vmem,) * 5,
        scratch_shapes=lands + [pltpu.VMEM((na,) + pos_m, F32), stage] + reduce_sems + [
            *pairs(na), *pairs(na), *pairs(nm, nb), *pairs(nm, nb)],
        compiler_params=params(1),
    )(part_m, part_i, mconc, iconc, x_two)
    part_m, part_i = gains(x_all, g_conc, h_conc)
    return pl.pallas_call(
        functools.partial(last_reduce, n_mob, n_imm),
        out_shape=own,
        in_specs=[vmem] * 4,
        out_specs=(vmem,) * 2,
        scratch_shapes=lands + reduce_sems,
        compiler_params=params(2),
    )(part_m, part_i, own_m, own_i)


def solution(mesh):
    return jax.shard_map(
        functools.partial(on_device, mesh.shape["mob"], mesh.shape["imm"]),
        mesh=mesh,
        in_specs=(
            P(("mob", "imm"), None, None),
            P(None, ("mob", "imm"), None, None),
            P(("mob", "imm"), None, None),
            P(("mob", "imm"), None, None),
            P(("mob", "imm"), None, None),
            P("mob", "imm", None),
            P("mob", "imm", None),
            P("mob", "imm"),
        ),
        out_specs=(P(("mob", "imm"), None, None), P(("mob", "imm"), None, None)),
        check_vma=False,
    )
```

```python
import functools
import math

import jax
import jax.numpy as jnp
from jax import lax
from jax.experimental import pallas as pl
from jax.experimental.pallas import tpu as pltpu
from jax.sharding import PartitionSpec as P

RATE = 1.0 / 512.0
SCALE = math.sqrt(0.5 * math.log2(math.e))
CENTRE = 2.0
FAR = -30000.0
MESH = pl.DeviceIdType.MESH
VMEM_LIMIT = 20 * 1024 * 1024
UNROLL = 8
TERMS = 16
F32 = jnp.float32
BF16 = jnp.bfloat16


def sizes(n_mob, n_imm):
    rest = n_imm // 2
    nb = 1
    while nb * nb * 4 <= rest:
        nb *= 2
    return n_mob, nb, rest // nb


class Place:
    def __init__(self, n_mob, n_imm):
        self.nm, self.nb, self.na = sizes(n_mob, n_imm)
        self.p = lax.axis_index("mob")
        q = lax.axis_index("imm")
        self.core = lax.rem(q, 2)
        chip = lax.div(q, 2)
        self.b = lax.rem(chip, self.nb)
        self.a = lax.div(chip, self.nb)

    def am(self, d):
        return lax.rem(self.a + (d + self.na), self.na)

    def bm(self, d):
        return lax.rem(self.b + (d + self.nb), self.nb)

    def pm(self, d):
        return lax.rem(self.p + (d + self.nm), self.nm)

    def dev(self, p, a, b, core):
        return (p, (a * self.nb + b) * 2 + core)

    def along(self, da):
        return self.dev(self.p, self.am(da), self.b, self.core)

    def other(self, dc):
        return 1 - self.core if dc else self.core

    def across(self, dp, db, dc):
        return self.dev(self.pm(dp), self.a, self.bm(db), self.other(dc))

    def plane(self):
        keys = [(dp, db) for dp in range(self.nm) for db in range(self.nb)]
        return sorted((key for key in keys if any(key)), key=lambda key: -bool(key[0]) - bool(key[1]))

    def mates(self):
        return [(db, dc) for db in range(self.nb) for dc in range(2) if db or dc]

    def slot(self, dp, db, dc):
        return (self.pm(dp) * self.nb + self.bm(db)) * 2 + self.other(dc)

    def greet(self, lists=False):
        sem = pltpu.get_barrier_semaphore()
        peers = [self.along(d) for d in range(1, self.na)] + [self.across(0, 0, 1)]
        peers += [self.across(dp, db, 0) for dp, db in self.plane()]
        if lists:
            peers += [self.across(0, db, 1) for db in range(1, self.nb)]
        for peer in peers:
            pl.semaphore_signal(sem, inc=1, device_id=peer, device_id_type=MESH)
        return sem, len(peers)


def remote(src, dst, sems, index, device):
    copy = pltpu.make_async_remote_copy(
        src_ref=src, dst_ref=dst, send_sem=sems[0].at[index], recv_sem=sems[1].at[index],
        device_id=device, device_id_type=MESH,
    )
    copy.start()
    return copy


def split2(x):
    high = x.astype(BF16).astype(F32)
    return high, x - high


def split3(x):
    high, rest = split2(x)
    mid, low = split2(rest)
    return high, mid, low


def rows_x(x):
    (xh, xm), (yh, ym), (zh, zm) = [split2(x[j]) for j in range(3)]
    norm = split3(-(x[0] * x[0] + x[1] * x[1] + x[2] * x[2]))
    one = jnp.ones_like(x[0])
    return [xh, yh, zh, xh, yh, zh, xm, ym, zm, *norm, one, one, one, jnp.zeros_like(one)]


def rows_y(y):
    (xh, xm), (yh, ym), (zh, zm) = [split2(2.0 * y[j]) for j in range(3)]
    norm = split3(-(y[0] * y[0] + y[1] * y[1] + y[2] * y[2]))
    one = jnp.ones_like(y[0])
    return [xh, yh, zh, xm, ym, zm, xh, yh, zh, one, one, one, *norm, jnp.zeros_like(one)]


def fill(stage, rows):
    cells = rows[0].shape[0]
    for j, row in enumerate(rows):
        stage[pl.ds(j, cells, stride=TERMS), :] = row


def build_y(pos, stage, out, slot):
    cells = pos.shape[1]
    fill(stage, rows_y([pos[j] for j in range(3)]))
    out[pl.ds(slot * cells, cells)] = stage[...].reshape(cells, TERMS, 128).astype(BF16)


def build_x(pos, stage, out, slot):
    cells = pos.shape[1]
    fill(stage, rows_x([pos[j] for j in range(3)]))
    for group in range(0, cells, 128 // TERMS):
        block = stage[group * TERMS : group * TERMS + 128, :].T.astype(BF16)
        for j in range(128 // TERMS):
            out[slot * cells + group + j, :, :TERMS] = block[:, j * TERMS : (j + 1) * TERMS]


def count_list(at, mc, ic, lists, keep_m, keep_i, keep_rank, first, last, total):
    lists_n = lists.shape[0]
    cells_m = at.na * mc
    shift_m, shift_i, shift_b = [int(math.log2(n)) for n in (mc, ic, at.nb)]
    lane = lax.broadcasted_iota(jnp.int32, (1, 128), 1)
    mine = lax.broadcasted_iota(jnp.int32, (cells_m, 128), 0)
    upper = jnp.where(
        lax.broadcasted_iota(jnp.int32, (128, 128), 0) <= lax.broadcasted_iota(jnp.int32, (128, 128), 1), 1.0, 0.0
    ).astype(BF16)
    home = at.b * 2 + at.core

    def count(chunk, total):
        which, part = lax.rem(lax.div(chunk, 4) + home, lists_n), lax.rem(chunk, 4)
        r = lists[which, pl.ds(part, 1), :]
        c = lists[which, pl.ds(4 + part, 1), :]
        used = lists[which, 8:9, :]
        owner = jnp.right_shift(r, shift_m)
        ok = (
            (part * 128 + lane < used)
            & (jnp.bitwise_and(owner, 1) == at.core)
            & (jnp.bitwise_and(jnp.right_shift(owner, 1), at.nb - 1) == at.b)
        )
        m = jnp.right_shift(owner, 1 + shift_b) * mc + jnp.bitwise_and(r, mc - 1)
        m = jnp.where(ok, m, -1)
        i = (jnp.right_shift(c, shift_i) * lists_n + which) * ic + jnp.bitwise_and(c, ic - 1)
        hot = jnp.where(mine == m, 1.0, 0.0).astype(F32)
        rank = total + jnp.dot(hot.astype(BF16), upper, preferred_element_type=F32)
        keep_m[pl.ds(chunk, 1), :] = m
        keep_i[pl.ds(chunk, 1), :] = i + 1
        keep_rank[pl.ds(chunk, 1), :] = jnp.sum(hot * rank, axis=0, keepdims=True) - 1.0
        return jnp.broadcast_to(rank[:, 127:128], rank.shape)

    return lax.fori_loop(first, last, count, total, unroll=4)


def place_list(at, mc, ic, lists, keep_m, keep_i, keep_rank, total, out):
    lists_n, chunks = lists.shape[0], lists.shape[0] * 4
    cells_m = at.na * mc
    lines = -(-(out.shape[0] // 3) // 16) * 16
    mine = lax.broadcasted_iota(jnp.int32, (cells_m, 128), 0)
    lower = jnp.where(
        lax.broadcasted_iota(jnp.int32, (cells_m, cells_m), 0)
        > lax.broadcasted_iota(jnp.int32, (cells_m, cells_m), 1), 1.0, 0.0
    ).astype(F32)
    even = 2.0 * jnp.floor((total + 1.0) * 0.5)
    start = jnp.dot(lower, even, preferred_element_type=F32, precision=lax.Precision.HIGHEST)
    doubles = jnp.sum(even, axis=0, keepdims=True) * 0.5
    line = lax.broadcasted_iota(jnp.int32, (lines, 128), 0)
    column = lax.broadcasted_iota(jnp.int32, (128, 128), 0)

    def place(chunk, acc):
        m = keep_m[pl.ds(chunk, 1), :]
        i = keep_i[pl.ds(chunk, 1), :]
        hot = jnp.where(mine == m, 1.0, 0.0).astype(F32)
        spot = jnp.sum(hot * start, axis=0, keepdims=True) + keep_rank[pl.ds(chunk, 1), :]
        spot = jnp.where(m >= 0, spot.astype(jnp.int32), -1)
        double = jnp.right_shift(spot, 1)
        second = jnp.bitwise_and(spot, 1) == 1
        here = (line == jnp.right_shift(double, 7)) & (m >= 0)
        lane_hot = jnp.where(column == jnp.bitwise_and(double, 127), 1.0, 0.0).astype(BF16)
        high = jnp.right_shift(i, 6).astype(F32)
        low = jnp.bitwise_and(i, 63).astype(F32)
        zero = jnp.zeros((1, 128), F32)
        values = [
            jnp.where(second, zero, m.astype(F32)),
            jnp.where(second, zero, high),
            jnp.where(second, zero, low),
            jnp.where(second, high, zero),
            jnp.where(second, low, zero),
        ]
        left = jnp.concatenate([jnp.where(here, v, 0.0) for v in values], axis=0).astype(BF16)
        return acc + lax.dot_general(left, lane_hot, (((1,), (1,)), ((), ())), preferred_element_type=F32)

    acc = lax.fori_loop(0, chunks, place, jnp.zeros((5 * lines, 128), F32), unroll=4)
    m, high1, low1, high2, low2 = [
        acc[j * lines : (j + 1) * lines].astype(jnp.int32) for j in range(5)
    ]
    dummy = at.nm * lists_n * ic
    size = out.shape[0] // 3
    out[0:size, :] = m[0:size]
    for j, (high, low) in enumerate(((high1, low1), (high2, low2)), 1):
        i = (high * 64 + low)[0:size]
        out[j * size : (j + 1) * size, :] = jnp.where(i == 0, dummy, i - 1)
    out[out.shape[0] - 1 :, :] = doubles.astype(jnp.int32)


def conc_rows(conc):
    conc = conc * RATE
    high = conc.astype(BF16).astype(F32)
    ones = jnp.full_like(conc, RATE)
    return jnp.concatenate([high, conc - high, ones, ones], axis=1).astype(BF16)


def fill_rows(conc, rows, slot):
    cells = conc.shape[1]
    rows[pl.ds(slot * cells, cells)] = conc_rows(conc[slot])


def share_plane(at, src, dst, sems, pass_sems):
    me = at.slot(0, 0, 0)
    copies = {
        (dp, db): remote(src, dst.at[me], sems, (dp, db), at.across(dp, db, 0)) for dp, db in at.plane()
    }
    return copies, {(0, 0): remote(src, dst.at[me], pass_sems, (0, 0), at.across(0, 0, 1))}


def pass_on(at, copies, passed, dst, pass_sems):
    for (dp, db), copy in copies.items():
        copy.wait_recv()
        block = dst.at[at.slot(-dp, -db, 0)]
        passed[dp, db] = remote(block, block, pass_sems, (dp, db), at.across(0, 0, 1))


def share_along(at, src, dst, sems):
    return {da: remote(src, dst.at[at.a], sems, da, at.along(da)) for da in range(1, at.na)}


def take_plane(at, copies, passed, conc, rows):
    for dp, db in copies:
        fill_rows(conc, rows, at.slot(-dp, -db, 0))
    for (dp, db), copy in passed.items():
        copy.wait_recv()
        fill_rows(conc, rows, at.slot(-dp, -db, 1))


def take_along(at, copies, conc, rows):
    for da, copy in copies.items():
        copy.wait_recv()
        fill_rows(conc, rows, at.am(-da))


def finish_sends(*groups):
    for group in groups:
        for copy in group.values():
            copy.wait_send()


def first_gather(n_mob, n_imm, mpos, walk, mconc, ipos, iconc, rows, cols, count,
                 g_conc, h_conc, m_rows, i_rows, x_one, y_all, pair_list, x_two,
                 g_pos, h_pos, lists, in_m, in_w, in_i, in_r, in_c, in_n, stage, keep_m, keep_i, keep_rank, *sems):
    at = Place(n_mob, n_imm)
    local = sems[0]
    z_pos, z_conc, p_pos, p_conc, c_pos, c_conc, l_sem = [sems[j : j + 2] for j in range(1, 15, 2)]
    me = at.slot(0, 0, 0)
    reads = [
        pltpu.make_async_copy(src, dst, local.at[j])
        for j, (src, dst) in enumerate((
            (mpos, in_m), (walk, in_w), (ipos, in_i), (rows, in_r), (cols, in_c), (count, in_n),
            (mconc, g_conc.at[at.a]), (iconc, h_conc.at[me]),
        ))
    ]
    for read in reads:
        read.start()
    sem, peers = at.greet(lists=True)
    h_conc[h_conc.shape[0] - 1] = jnp.zeros(h_conc.shape[1:], F32)
    i_rows[i_rows.shape[0] - 16 :] = jnp.zeros((16,) + i_rows.shape[1:], BF16)
    cells_i = y_all.shape[0] - 8
    row = lax.broadcasted_iota(jnp.int32, (8, TERMS, 128), 1)
    y_all[cells_i:, :, :] = jnp.where(row == 12, FAR, 0.0).astype(BF16)
    reads[0].wait()
    reads[1].wait()
    moved = in_m[...] + in_w[0]
    g_pos[at.a] = (moved - CENTRE) * SCALE
    x_two[...] = ((moved + in_w[1]) - CENTRE) * SCALE
    reads[2].wait()
    h_pos[me] = (in_i[...] - CENTRE) * SCALE
    for read in reads[3:6]:
        read.wait()
    home = at.b * 2 + at.core
    for j in range(4):
        lists[home, j : j + 1, :] = in_r[0, :, j * 128 : (j + 1) * 128]
        lists[home, 4 + j : 5 + j, :] = in_c[0, :, j * 128 : (j + 1) * 128]
    lists[home, 8:16, :] = jnp.broadcast_to(in_n[...], (8, 128))
    build_x(g_pos.at[at.a], stage, x_one, at.a)
    build_y(h_pos.at[me], stage, y_all, me)
    for read in reads[6:]:
        read.wait()
    fill_rows(g_conc, m_rows, at.a)
    fill_rows(h_conc, i_rows, me)
    mc, ic = mconc.shape[0], iconc.shape[0]
    total = count_list(at, mc, ic, lists, keep_m, keep_i, keep_rank, 0, 4, jnp.zeros((at.na * mc, 128), F32))
    pl.semaphore_wait(sem, peers)
    z_far = share_along(at, g_pos.at[at.a], g_pos, z_pos)
    z_conc = share_along(at, g_conc.at[at.a], g_conc, z_conc)
    shared = {
        (db, dc): remote(lists.at[home], lists.at[home], l_sem, (db, dc), at.across(0, db, dc))
        for db, dc in at.mates()
    }
    p_far, p_near = share_plane(at, h_pos.at[me], h_pos, p_pos, c_pos)
    p_conc, p_near_conc = share_plane(at, h_conc.at[me], h_conc, p_conc, c_conc)
    for copy in shared.values():
        copy.wait_recv()
    total = count_list(at, mc, ic, lists, keep_m, keep_i, keep_rank, 4, lists.shape[0] * 4, total)
    place_list(at, mc, ic, lists, keep_m, keep_i, keep_rank, total, pair_list)
    pass_on(at, p_far, p_near, h_pos, c_pos)
    pass_on(at, p_conc, p_near_conc, h_conc, c_conc)
    for dp, db in p_far:
        here = at.slot(-dp, -db, 0)
        build_y(h_pos.at[here], stage, y_all, here)
    for (dp, db), copy in p_near.items():
        copy.wait_recv()
        here = at.slot(-dp, -db, 1)
        build_y(h_pos.at[here], stage, y_all, here)
    for da, copy in z_far.items():
        copy.wait_recv()
        build_x(g_pos.at[at.am(-da)], stage, x_one, at.am(-da))
    take_plane(at, p_conc, p_near_conc, h_conc, i_rows)
    take_along(at, z_conc, g_conc, m_rows)
    finish_sends(z_far, z_conc, shared, p_far, p_near, p_conc, p_near_conc)


def reduce_start(at, part_m, part_i, land_m, land_c, out_b, land_b, z_sem, c_sem, b_sem):
    mc, ic = land_m.shape[1], land_c.shape[2]
    c_copies = {
        (dp, db): remote(
            part_i.at[pl.ds(at.slot(dp, db, 1) * ic, ic)], land_c.at[dp, db], c_sem, (dp, db), at.across(0, 0, 1))
        for dp, db in at.plane() + [(0, 0)]
    }
    z_copies = {
        da: remote(part_m.at[pl.ds(at.am(da) * mc, mc)], land_m.at[da], z_sem, da, at.along(da))
        for da in range(1, at.na)
    }
    b_copies = {}
    for dp, db in at.plane():
        c_copies[dp, db].wait_recv()
        out_b[dp, db] = part_i[pl.ds(at.slot(dp, db, 0) * ic, ic)] + land_c[dp, db]
        b_copies[dp, db] = remote(out_b.at[dp, db], land_b.at[dp, db], b_sem, (dp, db), at.across(dp, db, 0))
    return z_copies, c_copies, b_copies


def reduce_end(base, part, slot, land, copies):
    cells = base.shape[0]
    total = base[...] + part[pl.ds(slot * cells, cells)]
    for key, copy in copies.items():
        copy.wait_recv()
        total = total + land[key]
    return total


def reduce_plane_end(at, base, part, land_c, land_b, c_copies, b_copies):
    c_copies[0, 0].wait_recv()
    return reduce_end(base, part, at.slot(0, 0, 0), land_b, b_copies) + land_c[0, 0]


def exchange(n_mob, n_imm, part_m, part_i, conc_m, conc_i, x_two, own_m, own_i, g_conc, h_conc, m_rows, i_rows,
             x_all, land_m, land_c, out_b, land_b, g_pos, stage, *sems):
    at = Place(n_mob, n_imm)
    z_sem, c_sem, b_sem, z_pos, z_conc, p_conc, c_conc = [sems[j : j + 2] for j in range(0, 14, 2)]
    sem, peers = at.greet()
    h_conc[h_conc.shape[0] - 1] = jnp.zeros(h_conc.shape[1:], F32)
    i_rows[i_rows.shape[0] - 16 :] = jnp.zeros((16,) + i_rows.shape[1:], BF16)
    pl.semaphore_wait(sem, peers)
    z_copies, c_copies, b_copies = reduce_start(
        at, part_m, part_i, land_m, land_c, out_b, land_b, z_sem, c_sem, b_sem)
    z_far = share_along(at, x_two, g_pos, z_pos)
    build_x(x_two, stage, x_all, at.a)
    me = at.slot(0, 0, 0)
    own_i[...] = reduce_plane_end(at, conc_i, part_i, land_c, land_b, c_copies, b_copies)
    p_conc, p_near = share_plane(at, own_i, h_conc, p_conc, c_conc)
    own_m[...] = reduce_end(conc_m, part_m, at.a, land_m, z_copies)
    z_conc = share_along(at, own_m, g_conc, z_conc)
    g_conc[at.a] = own_m[...]
    h_conc[me] = own_i[...]
    fill_rows(g_conc, m_rows, at.a)
    fill_rows(h_conc, i_rows, me)
    for da, copy in z_far.items():
        copy.wait_recv()
        build_x(g_pos.at[at.am(-da)], stage, x_all, at.am(-da))
    pass_on(at, p_conc, p_near, h_conc, c_conc)
    take_plane(at, p_conc, p_near, h_conc, i_rows)
    take_along(at, z_conc, g_conc, m_rows)
    finish_sends(z_copies, c_copies, b_copies, z_far, z_conc, p_conc, p_near)


def last_reduce(n_mob, n_imm, part_m, part_i, conc_m, conc_i, own_m, own_i, land_m, land_c, out_b, land_b, *sems):
    at = Place(n_mob, n_imm)
    sem, peers = at.greet()
    pl.semaphore_wait(sem, peers)
    z_copies, c_copies, b_copies = reduce_start(
        at, part_m, part_i, land_m, land_c, out_b, land_b, sems[0:2], sems[2:4], sems[4:6])
    own_i[...] = reduce_plane_end(at, conc_i, part_i, land_c, land_b, c_copies, b_copies)
    own_m[...] = reduce_end(conc_m, part_m, at.a, land_m, z_copies)
    finish_sends(z_copies, c_copies, b_copies)


def pair_loop(pair_list, x_all, y_all, x_conc, y_conc, m_rows, i_rows, gain_m, gain_i,
              lst, p_even, p_odd, w_even, w_odd, sem):
    read = pltpu.make_async_copy(pair_list, lst, sem)
    read.start()
    gain_m[...] = jnp.zeros_like(gain_m)
    gain_i[...] = jnp.zeros_like(gain_i)
    read.wait()
    size = lst.shape[0] // 3 // 128 * 128
    used = lst[lst.shape[0] - 128]

    def entry(block, u):
        spot = block * UNROLL
        return lst[spot + u], lst[spot + (size + u)], lst[spot + (2 * size + u)]

    def measure(block, u, powers):
        m, i, k = entry(block, u)
        right = jnp.concatenate([y_all[i], y_all[k]], axis=1)
        powers[u] = jnp.dot(x_all[m][:, :TERMS], right, preferred_element_type=F32)

    def weigh(u, powers, weights):
        weights[u] = jnp.exp2(powers[u]).astype(BF16)

    def transfer(block, u, weights):
        m, i, k = entry(block, u)
        weight = weights[u]
        to_i = jnp.dot(m_rows[m], weight, preferred_element_type=F32)
        right = jnp.concatenate([i_rows[i], i_rows[k]], axis=1)
        to_m = lax.dot_general(right, weight, (((1,), (1,)), ((), ())), preferred_element_type=F32)
        return m, i, k, to_i, to_m

    def finish(m, i, k, to_i, to_m):
        gain_m[m] += to_m[0:8] + to_m[8:16] - to_m[16:24] * x_conc[m]
        gain_i[i] += to_i[0:8, :128] + to_i[8:16, :128] - to_i[16:24, :128] * y_conc[i]
        gain_i[k] += to_i[0:8, 128:] + to_i[8:16, 128:] - to_i[16:24, 128:] * y_conc[k]

    def step(block, first=None, second=None, third=None):
        moved = []
        for u in range(UNROLL):
            if second is not None:
                weigh(u, *second)
            if first is not None:
                measure(block, u, first)
            if third is not None:
                moved.append(transfer(block - 2, u, third))
        for item in moved:
            finish(*item)

    pairs = jnp.maximum(lax.div(used + (2 * UNROLL - 1), 2 * UNROLL), 1)
    step(0, p_even)
    step(1, p_odd, (p_even, w_even))

    def body(t, carry):
        step(2 * t, p_even, (p_odd, w_odd), w_even)
        step(2 * t + 1, p_odd, (p_even, w_even), w_odd)
        return carry

    lax.fori_loop(1, pairs, body, 0)
    step(2 * pairs, None, (p_odd, w_odd), w_even)
    step(2 * pairs + 1, None, None, w_odd)


def on_device(n_mob, n_imm, mpos, walk, mconc, ipos, iconc, rows, cols, counts):
    nm, nb, na = sizes(n_mob, n_imm)
    mc, solutes, part = mconc.shape
    ic = iconc.shape[0]
    slots = nm * nb * 2
    cells_m, cells_i = na * mc, slots * ic
    tiles = nb * 2
    chunks = tiles * 4
    lines = -(-(chunks * 64 + cells_m // 2 + 2 * UNROLL) // 128)
    list_rows = -(-(3 * lines + 1) // 8) * 8
    vmem = pl.BlockSpec(memory_space=pltpu.VMEM)
    anywhere = pl.BlockSpec(memory_space=pl.ANY)
    hbm = pl.BlockSpec(memory_space=pltpu.HBM)
    dma = pltpu.SemaphoreType.DMA

    def params(ident):
        return pltpu.CompilerParams(collective_id=ident, has_side_effects=True, vmem_limit_bytes=VMEM_LIMIT)

    def shape(dims, dtype=F32):
        return jax.ShapeDtypeStruct(dims, dtype)

    def pairs(*dims):
        return [dma(dims)] * 2

    cell_m, cell_i = (mc, solutes, part), (ic, solutes, part)
    all_m, all_i = (na,) + cell_m, (slots + 1,) + cell_i
    pos_m, pos_i = (3, mc, part), (3, ic, part)
    stage = pltpu.VMEM((max(mc, ic) * TERMS, part), F32)
    x_shape = shape((cells_m, part, 128), BF16)
    concs = (
        shape(all_m), shape(all_i),
        shape((cells_m, 4 * solutes, part), BF16), shape((cells_i + 16, 4 * solutes, part), BF16),
    )
    plane = (nm, nb)
    *concs_one, x_one, y_all, pair_list, x_two = pl.pallas_call(
        functools.partial(first_gather, n_mob, n_imm),
        out_shape=concs + (
            x_shape, shape((cells_i + 8, TERMS, part), BF16), shape((list_rows, 128), jnp.int32), shape(pos_m),
        ),
        in_specs=[hbm] * 8,
        out_specs=(vmem,) * 8,
        scratch_shapes=[
            pltpu.VMEM((na,) + pos_m, F32), pltpu.VMEM((slots,) + pos_i, F32),
            pltpu.VMEM((tiles, 16, 128), jnp.int32),
            pltpu.VMEM(pos_m, F32), pltpu.VMEM((2,) + pos_m, F32), pltpu.VMEM(pos_i, F32),
            pltpu.VMEM(rows.shape, jnp.int32), pltpu.VMEM(cols.shape, jnp.int32), pltpu.VMEM((1, 1), jnp.int32),
            stage, pltpu.VMEM((chunks, 128), jnp.int32), pltpu.VMEM((chunks, 128), jnp.int32),
            pltpu.VMEM((chunks, 128), F32),
            dma((8,)), *pairs(na), *pairs(na), *pairs(*plane), *pairs(*plane), *pairs(*plane), *pairs(*plane),
            *pairs(nb, 2),
        ],
        compiler_params=params(0),
    )(*[
        pltpu.with_memory_space_constraint(x, pltpu.HBM)
        for x in (jnp.transpose(mpos, (1, 0, 2)), jnp.transpose(walk, (0, 2, 1, 3)), mconc,
                  jnp.transpose(ipos, (1, 0, 2)), iconc, rows, cols)
    ], counts)
    flat_list = pair_list.reshape(-1)

    def gains(x_all, x_conc, y_conc, m_rows, i_rows):
        return pl.pallas_call(
            pair_loop,
            out_shape=(shape((cells_m, solutes, part)), shape((cells_i + 1, solutes, part))),
            in_specs=[anywhere] + [vmem] * 6,
            out_specs=(vmem,) * 2,
            scratch_shapes=[
                pltpu.SMEM((flat_list.shape[0],), jnp.int32),
                pltpu.VMEM((UNROLL, part, 256), F32), pltpu.VMEM((UNROLL, part, 256), F32),
                pltpu.VMEM((UNROLL, part, 256), BF16), pltpu.VMEM((UNROLL, part, 256), BF16),
                dma,
            ],
            compiler_params=pltpu.CompilerParams(vmem_limit_bytes=VMEM_LIMIT),
        )(flat_list, x_all, y_all, x_conc.reshape((cells_m, solutes, part)),
          y_conc.reshape((cells_i + ic, solutes, part)), m_rows, i_rows)

    lands = [pltpu.VMEM((na,) + cell_m, F32)] + [pltpu.VMEM(plane + cell_i, F32)] * 3
    own = (shape(cell_m), shape(cell_i))
    part_m, part_i = gains(x_one, *concs_one)
    own_m, own_i, *concs_two, x_all = pl.pallas_call(
        functools.partial(exchange, n_mob, n_imm),
        out_shape=own + concs + (x_shape,),
        in_specs=[vmem] * 5,
        out_specs=(vmem,) * 7,
        scratch_shapes=lands + [pltpu.VMEM((na,) + pos_m, F32), stage, *pairs(na), *pairs(*plane), *pairs(*plane),
                                *pairs(na), *pairs(na), *pairs(*plane), *pairs(*plane)],
        compiler_params=params(1),
    )(part_m, part_i, mconc, iconc, x_two)
    part_m, part_i = gains(x_all, *concs_two)
    return pl.pallas_call(
        functools.partial(last_reduce, n_mob, n_imm),
        out_shape=own,
        in_specs=[vmem] * 4,
        out_specs=(vmem,) * 2,
        scratch_shapes=lands + [*pairs(na), *pairs(*plane), *pairs(*plane)],
        compiler_params=params(2),
    )(part_m, part_i, own_m, own_i)


def solution(mesh):
    return jax.shard_map(
        functools.partial(on_device, mesh.shape["mob"], mesh.shape["imm"]),
        mesh=mesh,
        in_specs=(
            P(("mob", "imm"), None, None),
            P(None, ("mob", "imm"), None, None),
            P(("mob", "imm"), None, None),
            P(("mob", "imm"), None, None),
            P(("mob", "imm"), None, None),
            P("mob", "imm", None),
            P("mob", "imm", None),
            P("mob", "imm"),
        ),
        out_specs=(P(("mob", "imm"), None, None), P(("mob", "imm"), None, None)),
        check_vma=False,
    )
```

```python
import functools
import math

import jax
import jax.numpy as jnp
from jax import lax
from jax.experimental import pallas as pl
from jax.experimental.pallas import tpu as pltpu
from jax.sharding import PartitionSpec as P

RATE = 1.0 / 512.0
SCALE = math.sqrt(0.5 * math.log2(math.e))
CENTRE = 2.0
FAR = -30000.0
MESH = pl.DeviceIdType.MESH
VMEM_LIMIT = 20 * 1024 * 1024
UNROLL = 16
TERMS = 16
F32 = jnp.float32
BF16 = jnp.bfloat16


def sizes(n_mob, n_imm):
    rest = n_imm // 2
    nb = 1
    while nb * nb * 4 <= rest:
        nb *= 2
    return n_mob, nb, rest // nb


class Place:
    def __init__(self, n_mob, n_imm):
        self.nm, self.nb, self.na = sizes(n_mob, n_imm)
        self.p = lax.axis_index("mob")
        q = lax.axis_index("imm")
        self.core = lax.rem(q, 2)
        chip = lax.div(q, 2)
        self.b = lax.rem(chip, self.nb)
        self.a = lax.div(chip, self.nb)

    def am(self, d):
        return lax.rem(self.a + (d + self.na), self.na)

    def bm(self, d):
        return lax.rem(self.b + (d + self.nb), self.nb)

    def pm(self, d):
        return lax.rem(self.p + (d + self.nm), self.nm)

    def dev(self, p, a, b, core):
        return (p, (a * self.nb + b) * 2 + core)

    def along(self, da):
        return self.dev(self.p, self.am(da), self.b, self.core)

    def other(self, dc):
        return 1 - self.core if dc else self.core

    def across(self, dp, db, dc):
        return self.dev(self.pm(dp), self.a, self.bm(db), self.other(dc))

    def plane(self):
        keys = [(dp, db) for dp in range(self.nm) for db in range(self.nb)]
        return sorted((key for key in keys if any(key)), key=lambda key: -bool(key[0]) - bool(key[1]))

    def mates(self):
        return [(db, dc) for db in range(self.nb) for dc in range(2) if db or dc]

    def slot(self, dp, db, dc):
        return (self.pm(dp) * self.nb + self.bm(db)) * 2 + self.other(dc)

    def greet(self, lists=False):
        sem = pltpu.get_barrier_semaphore()
        peers = [self.along(d) for d in range(1, self.na)] + [self.across(0, 0, 1)]
        peers += [self.across(dp, db, 0) for dp, db in self.plane()]
        if lists:
            peers += [self.across(0, db, 1) for db in range(1, self.nb)]
        for peer in peers:
            pl.semaphore_signal(sem, inc=1, device_id=peer, device_id_type=MESH)
        return sem, len(peers)


def remote(src, dst, sems, index, device):
    copy = pltpu.make_async_remote_copy(
        src_ref=src, dst_ref=dst, send_sem=sems[0].at[index], recv_sem=sems[1].at[index],
        device_id=device, device_id_type=MESH,
    )
    copy.start()
    return copy


def split2(x):
    high = x.astype(BF16).astype(F32)
    return high, x - high


def split3(x):
    high, rest = split2(x)
    mid, low = split2(rest)
    return high, mid, low


def rows_x(x):
    (xh, xm), (yh, ym), (zh, zm) = [split2(x[j]) for j in range(3)]
    norm = split3(-(x[0] * x[0] + x[1] * x[1] + x[2] * x[2]))
    one = jnp.ones_like(x[0])
    return [xh, yh, zh, xh, yh, zh, xm, ym, zm, *norm, one, one, one, jnp.zeros_like(one)]


def rows_y(y):
    (xh, xm), (yh, ym), (zh, zm) = [split2(2.0 * y[j]) for j in range(3)]
    norm = split3(-(y[0] * y[0] + y[1] * y[1] + y[2] * y[2]))
    one = jnp.ones_like(y[0])
    return [xh, yh, zh, xm, ym, zm, xh, yh, zh, one, one, one, *norm, jnp.zeros_like(one)]


def fill(stage, rows):
    cells = rows[0].shape[0]
    for j, row in enumerate(rows):
        stage[pl.ds(j, cells, stride=TERMS), :] = row


def build_y(pos, stage, out, slot):
    cells = pos.shape[1]
    fill(stage, rows_y([pos[j] for j in range(3)]))
    out[pl.ds(slot * cells, cells)] = stage[...].reshape(cells, TERMS, 128).astype(BF16)


def build_x(pos, stage, out, slot):
    cells = pos.shape[1]
    fill(stage, rows_x([pos[j] for j in range(3)]))
    for group in range(0, cells, 128 // TERMS):
        block = stage[group * TERMS : group * TERMS + 128, :].T.astype(BF16)
        for j in range(128 // TERMS):
            out[slot * cells + group + j, :, :TERMS] = block[:, j * TERMS : (j + 1) * TERMS]


def count_list(at, mc, ic, lists, keep_m, keep_i, keep_rank, first, last, total):
    lists_n = lists.shape[0]
    cells_m = at.na * mc
    shift_m, shift_i, shift_b = [int(math.log2(n)) for n in (mc, ic, at.nb)]
    lane = lax.broadcasted_iota(jnp.int32, (1, 128), 1)
    mine = lax.broadcasted_iota(jnp.int32, (cells_m, 128), 0)
    upper = jnp.where(
        lax.broadcasted_iota(jnp.int32, (128, 128), 0) <= lax.broadcasted_iota(jnp.int32, (128, 128), 1), 1.0, 0.0
    ).astype(BF16)
    home = at.b * 2 + at.core

    def count(chunk, total):
        which, part = lax.rem(lax.div(chunk, 4) + home, lists_n), lax.rem(chunk, 4)
        r = lists[which, pl.ds(part, 1), :]
        c = lists[which, pl.ds(4 + part, 1), :]
        used = lists[which, 8:9, :]
        owner = jnp.right_shift(r, shift_m)
        ok = (
            (part * 128 + lane < used)
            & (jnp.bitwise_and(owner, 1) == at.core)
            & (jnp.bitwise_and(jnp.right_shift(owner, 1), at.nb - 1) == at.b)
        )
        m = jnp.right_shift(owner, 1 + shift_b) * mc + jnp.bitwise_and(r, mc - 1)
        m = jnp.where(ok, m, -1)
        i = (jnp.right_shift(c, shift_i) * lists_n + which) * ic + jnp.bitwise_and(c, ic - 1)
        hot = jnp.where(mine == m, 1.0, 0.0).astype(F32)
        rank = total + jnp.dot(hot.astype(BF16), upper, preferred_element_type=F32)
        keep_m[pl.ds(chunk, 1), :] = m
        keep_i[pl.ds(chunk, 1), :] = i + 1
        keep_rank[pl.ds(chunk, 1), :] = jnp.sum(hot * rank, axis=0, keepdims=True) - 1.0
        return jnp.broadcast_to(rank[:, 127:128], rank.shape)

    return lax.fori_loop(first, last, count, total, unroll=4)


def place_list(at, mc, ic, lists, keep_m, keep_i, keep_rank, total, out):
    lists_n, chunks = lists.shape[0], lists.shape[0] * 4
    cells_m = at.na * mc
    lines = -(-(out.shape[0] // 3) // 16) * 16
    mine = lax.broadcasted_iota(jnp.int32, (cells_m, 128), 0)
    lower = jnp.where(
        lax.broadcasted_iota(jnp.int32, (cells_m, cells_m), 0)
        > lax.broadcasted_iota(jnp.int32, (cells_m, cells_m), 1), 1.0, 0.0
    ).astype(F32)
    even = 2.0 * jnp.floor((total + 1.0) * 0.5)
    start = jnp.dot(lower, even, preferred_element_type=F32, precision=lax.Precision.HIGHEST)
    doubles = jnp.sum(even, axis=0, keepdims=True) * 0.5
    line = lax.broadcasted_iota(jnp.int32, (lines, 128), 0)
    column = lax.broadcasted_iota(jnp.int32, (128, 128), 0)

    def place(chunk, acc):
        m = keep_m[pl.ds(chunk, 1), :]
        i = keep_i[pl.ds(chunk, 1), :]
        hot = jnp.where(mine == m, 1.0, 0.0).astype(F32)
        spot = jnp.sum(hot * start, axis=0, keepdims=True) + keep_rank[pl.ds(chunk, 1), :]
        spot = jnp.where(m >= 0, spot.astype(jnp.int32), -1)
        double = jnp.right_shift(spot, 1)
        second = jnp.bitwise_and(spot, 1) == 1
        here = (line == jnp.right_shift(double, 7)) & (m >= 0)
        lane_hot = jnp.where(column == jnp.bitwise_and(double, 127), 1.0, 0.0).astype(BF16)
        high = jnp.right_shift(i, 6).astype(F32)
        low = jnp.bitwise_and(i, 63).astype(F32)
        zero = jnp.zeros((1, 128), F32)
        values = [
            jnp.where(second, zero, m.astype(F32)),
            jnp.where(second, zero, high),
            jnp.where(second, zero, low),
            jnp.where(second, high, zero),
            jnp.where(second, low, zero),
        ]
        left = jnp.concatenate([jnp.where(here, v, 0.0) for v in values], axis=0).astype(BF16)
        return acc + lax.dot_general(left, lane_hot, (((1,), (1,)), ((), ())), preferred_element_type=F32)

    acc = lax.fori_loop(0, chunks, place, jnp.zeros((5 * lines, 128), F32), unroll=4)
    m, high1, low1, high2, low2 = [
        acc[j * lines : (j + 1) * lines].astype(jnp.int32) for j in range(5)
    ]
    dummy = at.nm * lists_n * ic
    size = out.shape[0] // 3
    out[0:size, :] = m[0:size]
    for j, (high, low) in enumerate(((high1, low1), (high2, low2)), 1):
        i = (high * 64 + low)[0:size]
        out[j * size : (j + 1) * size, :] = jnp.where(i == 0, dummy, i - 1)
    out[out.shape[0] - 1 :, :] = doubles.astype(jnp.int32)


def conc_rows(conc):
    conc = conc * RATE
    high = conc.astype(BF16).astype(F32)
    ones = jnp.full_like(conc, RATE)
    return jnp.concatenate([high, conc - high, ones, ones], axis=1).astype(BF16)


def fill_rows(conc, rows, slot):
    cells = conc.shape[1]
    rows[pl.ds(slot * cells, cells)] = conc_rows(conc[slot])


def share_plane(at, src, dst, sems, pass_sems):
    me = at.slot(0, 0, 0)
    copies = {
        (dp, db): remote(src, dst.at[me], sems, (dp, db), at.across(dp, db, 0)) for dp, db in at.plane()
    }
    return copies, {(0, 0): remote(src, dst.at[me], pass_sems, (0, 0), at.across(0, 0, 1))}


def pass_on(at, copies, passed, dst, pass_sems):
    for (dp, db), copy in copies.items():
        copy.wait_recv()
        block = dst.at[at.slot(-dp, -db, 0)]
        passed[dp, db] = remote(block, block, pass_sems, (dp, db), at.across(0, 0, 1))


def share_along(at, src, dst, sems):
    return {da: remote(src, dst.at[at.a], sems, da, at.along(da)) for da in range(1, at.na)}


def take_plane(at, copies, passed, conc, rows):
    for dp, db in copies:
        fill_rows(conc, rows, at.slot(-dp, -db, 0))
    for (dp, db), copy in passed.items():
        copy.wait_recv()
        fill_rows(conc, rows, at.slot(-dp, -db, 1))


def take_along(at, copies, conc, rows):
    for da, copy in copies.items():
        copy.wait_recv()
        fill_rows(conc, rows, at.am(-da))


def finish_sends(*groups):
    for group in groups:
        for copy in group.values():
            copy.wait_send()


def first_gather(n_mob, n_imm, mpos, walk, mconc, ipos, iconc, rows, cols, count,
                 g_conc, h_conc, m_rows, i_rows, x_one, y_all, pair_list, x_two,
                 g_pos, h_pos, lists, in_m, in_w, in_i, in_r, in_c, in_n, stage, keep_m, keep_i, keep_rank, *sems):
    at = Place(n_mob, n_imm)
    local = sems[0]
    z_pos, z_conc, p_pos, p_conc, c_pos, c_conc, l_sem = [sems[j : j + 2] for j in range(1, 15, 2)]
    me = at.slot(0, 0, 0)
    reads = [
        pltpu.make_async_copy(src, dst, local.at[j])
        for j, (src, dst) in enumerate((
            (mpos, in_m), (walk, in_w), (ipos, in_i), (rows, in_r), (cols, in_c), (count, in_n),
            (mconc, g_conc.at[at.a]), (iconc, h_conc.at[me]),
        ))
    ]
    for read in reads:
        read.start()
    sem, peers = at.greet(lists=True)
    h_conc[h_conc.shape[0] - 1] = jnp.zeros(h_conc.shape[1:], F32)
    i_rows[i_rows.shape[0] - 16 :] = jnp.zeros((16,) + i_rows.shape[1:], BF16)
    cells_i = y_all.shape[0] - 8
    row = lax.broadcasted_iota(jnp.int32, (8, TERMS, 128), 1)
    y_all[cells_i:, :, :] = jnp.where(row == 12, FAR, 0.0).astype(BF16)
    reads[0].wait()
    reads[1].wait()
    moved = in_m[...] + in_w[0]
    g_pos[at.a] = (moved - CENTRE) * SCALE
    x_two[...] = ((moved + in_w[1]) - CENTRE) * SCALE
    reads[2].wait()
    h_pos[me] = (in_i[...] - CENTRE) * SCALE
    for read in reads[3:6]:
        read.wait()
    home = at.b * 2 + at.core
    for j in range(4):
        lists[home, j : j + 1, :] = in_r[0, :, j * 128 : (j + 1) * 128]
        lists[home, 4 + j : 5 + j, :] = in_c[0, :, j * 128 : (j + 1) * 128]
    lists[home, 8:16, :] = jnp.broadcast_to(in_n[...], (8, 128))
    build_x(g_pos.at[at.a], stage, x_one, at.a)
    build_y(h_pos.at[me], stage, y_all, me)
    for read in reads[6:]:
        read.wait()
    fill_rows(g_conc, m_rows, at.a)
    fill_rows(h_conc, i_rows, me)
    mc, ic = mconc.shape[0], iconc.shape[0]
    total = count_list(at, mc, ic, lists, keep_m, keep_i, keep_rank, 0, 4, jnp.zeros((at.na * mc, 128), F32))
    pl.semaphore_wait(sem, peers)
    z_far = share_along(at, g_pos.at[at.a], g_pos, z_pos)
    z_conc = share_along(at, g_conc.at[at.a], g_conc, z_conc)
    shared = {
        (db, dc): remote(lists.at[home], lists.at[home], l_sem, (db, dc), at.across(0, db, dc))
        for db, dc in at.mates()
    }
    p_far, p_near = share_plane(at, h_pos.at[me], h_pos, p_pos, c_pos)
    p_conc, p_near_conc = share_plane(at, h_conc.at[me], h_conc, p_conc, c_conc)
    for copy in shared.values():
        copy.wait_recv()
    total = count_list(at, mc, ic, lists, keep_m, keep_i, keep_rank, 4, lists.shape[0] * 4, total)
    place_list(at, mc, ic, lists, keep_m, keep_i, keep_rank, total, pair_list)
    pass_on(at, p_far, p_near, h_pos, c_pos)
    pass_on(at, p_conc, p_near_conc, h_conc, c_conc)
    for dp, db in p_far:
        here = at.slot(-dp, -db, 0)
        build_y(h_pos.at[here], stage, y_all, here)
    for (dp, db), copy in p_near.items():
        copy.wait_recv()
        here = at.slot(-dp, -db, 1)
        build_y(h_pos.at[here], stage, y_all, here)
    for da, copy in z_far.items():
        copy.wait_recv()
        build_x(g_pos.at[at.am(-da)], stage, x_one, at.am(-da))
    take_plane(at, p_conc, p_near_conc, h_conc, i_rows)
    take_along(at, z_conc, g_conc, m_rows)
    finish_sends(z_far, z_conc, shared, p_far, p_near, p_conc, p_near_conc)


def reduce_start(at, part_m, part_i, land_m, land_c, out_b, land_b, z_sem, c_sem, b_sem):
    mc, ic = land_m.shape[1], land_c.shape[2]
    c_copies = {
        (dp, db): remote(
            part_i.at[pl.ds(at.slot(dp, db, 1) * ic, ic)], land_c.at[dp, db], c_sem, (dp, db), at.across(0, 0, 1))
        for dp, db in at.plane() + [(0, 0)]
    }
    z_copies = {
        da: remote(part_m.at[pl.ds(at.am(da) * mc, mc)], land_m.at[da], z_sem, da, at.along(da))
        for da in range(1, at.na)
    }
    b_copies = {}
    for dp, db in at.plane():
        c_copies[dp, db].wait_recv()
        out_b[dp, db] = part_i[pl.ds(at.slot(dp, db, 0) * ic, ic)] + land_c[dp, db]
        b_copies[dp, db] = remote(out_b.at[dp, db], land_b.at[dp, db], b_sem, (dp, db), at.across(dp, db, 0))
    return z_copies, c_copies, b_copies


def reduce_end(base, part, slot, land, copies):
    cells = base.shape[0]
    total = base[...] + part[pl.ds(slot * cells, cells)]
    for key, copy in copies.items():
        copy.wait_recv()
        total = total + land[key]
    return total


def reduce_plane_end(at, base, part, land_c, land_b, c_copies, b_copies):
    c_copies[0, 0].wait_recv()
    return reduce_end(base, part, at.slot(0, 0, 0), land_b, b_copies) + land_c[0, 0]


def exchange(n_mob, n_imm, part_m, part_i, conc_m, conc_i, x_two, own_m, own_i, g_conc, h_conc, m_rows, i_rows,
             x_all, land_m, land_c, out_b, land_b, g_pos, stage, *sems):
    at = Place(n_mob, n_imm)
    z_sem, c_sem, b_sem, z_pos, z_conc, p_conc, c_conc = [sems[j : j + 2] for j in range(0, 14, 2)]
    sem, peers = at.greet()
    h_conc[h_conc.shape[0] - 1] = jnp.zeros(h_conc.shape[1:], F32)
    i_rows[i_rows.shape[0] - 16 :] = jnp.zeros((16,) + i_rows.shape[1:], BF16)
    pl.semaphore_wait(sem, peers)
    z_copies, c_copies, b_copies = reduce_start(
        at, part_m, part_i, land_m, land_c, out_b, land_b, z_sem, c_sem, b_sem)
    z_far = share_along(at, x_two, g_pos, z_pos)
    build_x(x_two, stage, x_all, at.a)
    me = at.slot(0, 0, 0)
    own_i[...] = reduce_plane_end(at, conc_i, part_i, land_c, land_b, c_copies, b_copies)
    p_conc, p_near = share_plane(at, own_i, h_conc, p_conc, c_conc)
    own_m[...] = reduce_end(conc_m, part_m, at.a, land_m, z_copies)
    z_conc = share_along(at, own_m, g_conc, z_conc)
    g_conc[at.a] = own_m[...]
    h_conc[me] = own_i[...]
    fill_rows(g_conc, m_rows, at.a)
    fill_rows(h_conc, i_rows, me)
    for da, copy in z_far.items():
        copy.wait_recv()
        build_x(g_pos.at[at.am(-da)], stage, x_all, at.am(-da))
    pass_on(at, p_conc, p_near, h_conc, c_conc)
    take_plane(at, p_conc, p_near, h_conc, i_rows)
    take_along(at, z_conc, g_conc, m_rows)
    finish_sends(z_copies, c_copies, b_copies, z_far, z_conc, p_conc, p_near)


def last_reduce(n_mob, n_imm, part_m, part_i, conc_m, conc_i, own_m, own_i, land_m, land_c, out_b, land_b, *sems):
    at = Place(n_mob, n_imm)
    sem, peers = at.greet()
    pl.semaphore_wait(sem, peers)
    z_copies, c_copies, b_copies = reduce_start(
        at, part_m, part_i, land_m, land_c, out_b, land_b, sems[0:2], sems[2:4], sems[4:6])
    own_i[...] = reduce_plane_end(at, conc_i, part_i, land_c, land_b, c_copies, b_copies)
    own_m[...] = reduce_end(conc_m, part_m, at.a, land_m, z_copies)
    finish_sends(z_copies, c_copies, b_copies)


def pair_loop(pair_list, x_all, y_all, x_conc, y_conc, m_rows, i_rows, gain_m, gain_i,
              lst, p_even, p_odd, w_even, w_odd, sem):
    read = pltpu.make_async_copy(pair_list, lst, sem)
    read.start()
    gain_m[...] = jnp.zeros_like(gain_m)
    gain_i[...] = jnp.zeros_like(gain_i)
    read.wait()
    size = lst.shape[0] // 3 // 128 * 128
    used = lst[lst.shape[0] - 128]

    def entry(block, u):
        spot = block * UNROLL
        return lst[spot + u], lst[spot + (size + u)], lst[spot + (2 * size + u)]

    def measure(block, u, powers):
        m, i, k = entry(block, u)
        right = jnp.concatenate([y_all[i], y_all[k]], axis=1)
        powers[u] = jnp.dot(x_all[m][:, :TERMS], right, preferred_element_type=F32)

    def weigh(u, powers, weights):
        weights[u] = jnp.exp2(powers[u]).astype(BF16)

    def transfer(block, u, weights):
        m, i, k = entry(block, u)
        weight = weights[u]
        to_i = jnp.dot(m_rows[m], weight, preferred_element_type=F32)
        right = jnp.concatenate([i_rows[i], i_rows[k]], axis=1)
        to_m = lax.dot_general(right, weight, (((1,), (1,)), ((), ())), preferred_element_type=F32)
        return m, i, k, to_i, to_m

    def finish(m, i, k, to_i, to_m):
        gain_m[m] += to_m[0:8] + to_m[8:16] - to_m[16:24] * x_conc[m]
        gain_i[i] += to_i[0:8, :128] + to_i[8:16, :128] - to_i[16:24, :128] * y_conc[i]
        gain_i[k] += to_i[0:8, 128:] + to_i[8:16, 128:] - to_i[16:24, 128:] * y_conc[k]

    def step(block, first=None, second=None, third=None):
        moved = []
        for u in range(UNROLL):
            if second is not None:
                weigh(u, *second)
            if first is not None:
                measure(block, u, first)
            if third is not None:
                moved.append(transfer(block - 2, u, third))
        for item in moved:
            finish(*item)

    pairs = jnp.maximum(lax.div(used + (2 * UNROLL - 1), 2 * UNROLL), 1)
    step(0, p_even)
    step(1, p_odd, (p_even, w_even))

    def body(t, carry):
        step(2 * t, p_even, (p_odd, w_odd), w_even)
        step(2 * t + 1, p_odd, (p_even, w_even), w_odd)
        return carry

    lax.fori_loop(1, pairs, body, 0)
    step(2 * pairs, None, (p_odd, w_odd), w_even)
    step(2 * pairs + 1, None, None, w_odd)


def write_out(own_m, own_i, out_m, out_i, sems):
    copies = [
        pltpu.make_async_copy(src, dst, sems.at[j]) for j, (src, dst) in enumerate(((own_m, out_m), (own_i, out_i)))
    ]
    for copy in copies:
        copy.start()
    for copy in copies:
        copy.wait()


def on_device(n_mob, n_imm, mpos, walk, mconc, ipos, iconc, rows, cols, counts):
    nm, nb, na = sizes(n_mob, n_imm)
    mc, solutes, part = mconc.shape
    ic = iconc.shape[0]
    slots = nm * nb * 2
    cells_m, cells_i = na * mc, slots * ic
    tiles = nb * 2
    chunks = tiles * 4
    lines = -(-(chunks * 64 + cells_m // 2 + 2 * UNROLL) // 128)
    list_rows = -(-(3 * lines + 1) // 8) * 8
    vmem = pl.BlockSpec(memory_space=pltpu.VMEM)
    anywhere = pl.BlockSpec(memory_space=pl.ANY)
    hbm = pl.BlockSpec(memory_space=pltpu.HBM)
    dma = pltpu.SemaphoreType.DMA

    def params(ident):
        return pltpu.CompilerParams(collective_id=ident, has_side_effects=True, vmem_limit_bytes=VMEM_LIMIT)

    def shape(dims, dtype=F32):
        return jax.ShapeDtypeStruct(dims, dtype)

    def pairs(*dims):
        return [dma(dims)] * 2

    cell_m, cell_i = (mc, solutes, part), (ic, solutes, part)
    all_m, all_i = (na,) + cell_m, (slots + 1,) + cell_i
    pos_m, pos_i = (3, mc, part), (3, ic, part)
    stage = pltpu.VMEM((max(mc, ic) * TERMS, part), F32)
    x_shape = shape((cells_m, part, 128), BF16)
    concs = (
        shape(all_m), shape(all_i),
        shape((cells_m, 4 * solutes, part), BF16), shape((cells_i + 16, 4 * solutes, part), BF16),
    )
    plane = (nm, nb)
    *concs_one, x_one, y_all, pair_list, x_two = pl.pallas_call(
        functools.partial(first_gather, n_mob, n_imm),
        out_shape=concs + (
            x_shape, shape((cells_i + 8, TERMS, part), BF16), shape((list_rows, 128), jnp.int32), shape(pos_m),
        ),
        in_specs=[hbm] * 8,
        out_specs=(vmem,) * 8,
        scratch_shapes=[
            pltpu.VMEM((na,) + pos_m, F32), pltpu.VMEM((slots,) + pos_i, F32),
            pltpu.VMEM((tiles, 16, 128), jnp.int32),
            pltpu.VMEM(pos_m, F32), pltpu.VMEM((2,) + pos_m, F32), pltpu.VMEM(pos_i, F32),
            pltpu.VMEM(rows.shape, jnp.int32), pltpu.VMEM(cols.shape, jnp.int32), pltpu.VMEM((1, 1), jnp.int32),
            stage, pltpu.VMEM((chunks, 128), jnp.int32), pltpu.VMEM((chunks, 128), jnp.int32),
            pltpu.VMEM((chunks, 128), F32),
            dma((8,)), *pairs(na), *pairs(na), *pairs(*plane), *pairs(*plane), *pairs(*plane), *pairs(*plane),
            *pairs(nb, 2),
        ],
        compiler_params=params(0),
    )(*[
        pltpu.with_memory_space_constraint(x, pltpu.HBM)
        for x in (jnp.transpose(mpos, (1, 0, 2)), jnp.transpose(walk, (0, 2, 1, 3)), mconc,
                  jnp.transpose(ipos, (1, 0, 2)), iconc, rows, cols)
    ], counts)
    flat_list = pair_list.reshape(-1)

    def gains(x_all, x_conc, y_conc, m_rows, i_rows):
        return pl.pallas_call(
            pair_loop,
            out_shape=(shape((cells_m, solutes, part)), shape((cells_i + 1, solutes, part))),
            in_specs=[anywhere] + [vmem] * 6,
            out_specs=(vmem,) * 2,
            scratch_shapes=[
                pltpu.SMEM((flat_list.shape[0],), jnp.int32),
                pltpu.VMEM((UNROLL, part, 256), F32), pltpu.VMEM((UNROLL, part, 256), F32),
                pltpu.VMEM((UNROLL, part, 256), BF16), pltpu.VMEM((UNROLL, part, 256), BF16),
                dma,
            ],
            compiler_params=pltpu.CompilerParams(vmem_limit_bytes=VMEM_LIMIT),
        )(flat_list, x_all, y_all, x_conc.reshape((cells_m, solutes, part)),
          y_conc.reshape((cells_i + ic, solutes, part)), m_rows, i_rows)

    lands = [pltpu.VMEM((na,) + cell_m, F32)] + [pltpu.VMEM(plane + cell_i, F32)] * 3
    own = (shape(cell_m), shape(cell_i))
    part_m, part_i = gains(x_one, *concs_one)
    own_m, own_i, *concs_two, x_all = pl.pallas_call(
        functools.partial(exchange, n_mob, n_imm),
        out_shape=own + concs + (x_shape,),
        in_specs=[vmem] * 5,
        out_specs=(vmem,) * 7,
        scratch_shapes=lands + [pltpu.VMEM((na,) + pos_m, F32), stage, *pairs(na), *pairs(*plane), *pairs(*plane),
                                *pairs(na), *pairs(na), *pairs(*plane), *pairs(*plane)],
        compiler_params=params(1),
    )(part_m, part_i, mconc, iconc, x_two)
    part_m, part_i = gains(x_all, *concs_two)
    own_m, own_i = pl.pallas_call(
        functools.partial(last_reduce, n_mob, n_imm),
        out_shape=own,
        in_specs=[vmem] * 4,
        out_specs=(vmem,) * 2,
        scratch_shapes=lands + [*pairs(na), *pairs(*plane), *pairs(*plane)],
        compiler_params=params(2),
    )(part_m, part_i, own_m, own_i)
    return pl.pallas_call(
        write_out,
        out_shape=own,
        in_specs=[vmem] * 2,
        out_specs=(anywhere,) * 2,
        scratch_shapes=[dma((2,))],
        compiler_params=pltpu.CompilerParams(vmem_limit_bytes=VMEM_LIMIT),
    )(own_m, own_i)


def solution(mesh):
    return jax.shard_map(
        functools.partial(on_device, mesh.shape["mob"], mesh.shape["imm"]),
        mesh=mesh,
        in_specs=(
            P(("mob", "imm"), None, None),
            P(None, ("mob", "imm"), None, None),
            P(("mob", "imm"), None, None),
            P(("mob", "imm"), None, None),
            P(("mob", "imm"), None, None),
            P("mob", "imm", None),
            P("mob", "imm", None),
            P("mob", "imm"),
        ),
        out_specs=(P(("mob", "imm"), None, None), P(("mob", "imm"), None, None)),
        check_vma=False,
    )
```

```python
import functools
import math

import jax
import jax.numpy as jnp
from jax import lax
from jax.experimental import pallas as pl
from jax.experimental.pallas import tpu as pltpu
from jax.sharding import PartitionSpec as P

RATE = 1.0 / 512.0
SCALE = math.sqrt(0.5 * math.log2(math.e))
CENTRE = 2.0
FAR = -30000.0
MESH = pl.DeviceIdType.MESH
VMEM_LIMIT = 20 * 1024 * 1024
UNROLL = 16
TERMS = 16
F32 = jnp.float32
BF16 = jnp.bfloat16


def sizes(n_mob, n_imm):
    rest = n_imm // 2
    nb = 1
    while nb * nb * 4 <= rest:
        nb *= 2
    return n_mob, nb, rest // nb


class Place:
    def __init__(self, n_mob, n_imm):
        self.nm, self.nb, self.na = sizes(n_mob, n_imm)
        self.p = lax.axis_index("mob")
        q = lax.axis_index("imm")
        self.core = lax.rem(q, 2)
        chip = lax.div(q, 2)
        self.b = lax.rem(chip, self.nb)
        self.a = lax.div(chip, self.nb)

    def am(self, d):
        return lax.rem(self.a + (d + self.na), self.na)

    def bm(self, d):
        return lax.rem(self.b + (d + self.nb), self.nb)

    def pm(self, d):
        return lax.rem(self.p + (d + self.nm), self.nm)

    def dev(self, p, a, b, core):
        return (p, (a * self.nb + b) * 2 + core)

    def along(self, da):
        return self.dev(self.p, self.am(da), self.b, self.core)

    def other(self, dc):
        return 1 - self.core if dc else self.core

    def across(self, dp, db, dc):
        return self.dev(self.pm(dp), self.a, self.bm(db), self.other(dc))

    def plane(self):
        keys = [(dp, db) for dp in range(self.nm) for db in range(self.nb)]
        return sorted((key for key in keys if any(key)), key=lambda key: -bool(key[0]) - bool(key[1]))

    def mates(self):
        return [(dp, da) for dp in range(self.nm) for da in range(self.na) if dp or da]

    def mate(self, dp, da):
        return self.dev(self.pm(dp), self.am(da), self.b, self.core)

    def slot(self, dp, db, dc):
        return (self.pm(dp) * self.nb + self.bm(db)) * 2 + self.other(dc)

    def greet(self, lists=False):
        sem = pltpu.get_barrier_semaphore()
        peers = [self.along(d) for d in range(1, self.na)] + [self.across(0, 0, 1)]
        peers += [self.across(dp, db, 0) for dp, db in self.plane()]
        if lists:
            peers += [self.mate(dp, da) for dp, da in self.mates() if dp and da]
        for peer in peers:
            pl.semaphore_signal(sem, inc=1, device_id=peer, device_id_type=MESH)
        return sem, len(peers)


def remote(src, dst, sems, index, device):
    copy = pltpu.make_async_remote_copy(
        src_ref=src, dst_ref=dst, send_sem=sems[0].at[index], recv_sem=sems[1].at[index],
        device_id=device, device_id_type=MESH,
    )
    copy.start()
    return copy


def split2(x):
    high = x.astype(BF16).astype(F32)
    return high, x - high


def split3(x):
    high, rest = split2(x)
    mid, low = split2(rest)
    return high, mid, low


def rows_x(x):
    (xh, xm), (yh, ym), (zh, zm) = [split2(x[j]) for j in range(3)]
    norm = split3(-(x[0] * x[0] + x[1] * x[1] + x[2] * x[2]))
    one = jnp.ones_like(x[0])
    return [xh, yh, zh, xh, yh, zh, xm, ym, zm, *norm, one, one, one, jnp.zeros_like(one)]


def rows_y(y):
    (xh, xm), (yh, ym), (zh, zm) = [split2(2.0 * y[j]) for j in range(3)]
    norm = split3(-(y[0] * y[0] + y[1] * y[1] + y[2] * y[2]))
    one = jnp.ones_like(y[0])
    return [xh, yh, zh, xm, ym, zm, xh, yh, zh, one, one, one, *norm, jnp.zeros_like(one)]


def fill(stage, rows):
    cells = rows[0].shape[0]
    for j, row in enumerate(rows):
        stage[pl.ds(j, cells, stride=TERMS), :] = row


def build_y(pos, stage, out, slot):
    cells = pos.shape[1]
    fill(stage, rows_y([pos[j] for j in range(3)]))
    out[pl.ds(slot * cells, cells)] = stage[...].reshape(cells, TERMS, 128).astype(BF16)


def build_x(pos, stage, out, slot):
    cells = pos.shape[1]
    fill(stage, rows_x([pos[j] for j in range(3)]))
    for group in range(0, cells, 128 // TERMS):
        block = stage[group * TERMS : group * TERMS + 128, :].T.astype(BF16)
        for j in range(128 // TERMS):
            out[slot * cells + group + j, :, :TERMS] = block[:, j * TERMS : (j + 1) * TERMS]


def count_list(at, mc, ic, lists, keep_m, keep_i, keep_rank, first, last, total):
    lists_n = lists.shape[0]
    cells_m = at.na * mc
    shift_m, shift_i, shift_b = [int(math.log2(n)) for n in (mc, ic, at.nb)]
    mine = lax.broadcasted_iota(jnp.int32, (cells_m, 128), 0)
    column = lax.broadcasted_iota(jnp.int32, (128, 256), 1)
    upper = jnp.where(
        (lax.broadcasted_iota(jnp.int32, (128, 256), 0) <= column) | (column >= 128), 1.0, 0.0
    ).astype(BF16)
    home = at.p * at.na + at.a

    def count(chunk, total):
        which, part = lax.rem(lax.div(chunk, 4) + home, lists_n), lax.rem(chunk, 4)
        r = lists[which, pl.ds(part, 1), :]
        c = lists[which, pl.ds(4 + part, 1), :]
        owner = jnp.right_shift(r, shift_i)
        ok = (
            (r >= 0)
            & (jnp.right_shift(owner, 1 + shift_b) == at.a)
            & (jnp.right_shift(c, shift_m) == at.p)
        )
        m = lax.rem(which, at.na) * mc + jnp.bitwise_and(c, mc - 1)
        m = jnp.where(ok, m, -1)
        spot = lax.div(which, at.na) * (at.nb * 2) + jnp.bitwise_and(owner, at.nb * 2 - 1)
        i = spot * ic + jnp.bitwise_and(r, ic - 1)
        hot = jnp.where(mine == m, 1.0, 0.0).astype(F32)
        rank = jnp.dot(hot.astype(BF16), upper, preferred_element_type=F32)
        keep_m[pl.ds(chunk, 1), :] = m
        keep_i[pl.ds(chunk, 1), :] = i + 1
        keep_rank[pl.ds(chunk, 1), :] = jnp.sum(hot * (rank[:, :128] + total), axis=0, keepdims=True) - 1.0
        return total + rank[:, 128:]

    return lax.fori_loop(first, last, count, total, unroll=7)


def place_list(at, mc, ic, lists, keep_m, keep_i, keep_rank, total, out):
    lists_n, chunks = lists.shape[0], lists.shape[0] * 4
    cells_m = at.na * mc
    lines = -(-(out.shape[0] // 3) // 8) * 8
    dummy = at.nm * at.nb * 2 * ic
    wide = dummy > 255
    groups = 5 if wide else 3
    mine = lax.broadcasted_iota(jnp.int32, (cells_m, 128), 0)
    lower = jnp.where(
        lax.broadcasted_iota(jnp.int32, (cells_m, cells_m), 0)
        > lax.broadcasted_iota(jnp.int32, (cells_m, cells_m), 1), 1.0, 0.0
    ).astype(F32)
    even = 2.0 * jnp.floor((total + 1.0) * 0.5)
    start = jnp.dot(lower, even, preferred_element_type=F32, precision=lax.Precision.HIGHEST)
    doubles = jnp.sum(even, axis=0, keepdims=True) * 0.5
    line = lax.broadcasted_iota(jnp.int32, (lines, 128), 0)
    column = lax.broadcasted_iota(jnp.int32, (128, 128), 0)

    def place(chunk, acc):
        m = keep_m[pl.ds(chunk, 1), :]
        i = keep_i[pl.ds(chunk, 1), :]
        hot = jnp.where(mine == m, 1.0, 0.0).astype(F32)
        spot = jnp.sum(hot * start, axis=0, keepdims=True) + keep_rank[pl.ds(chunk, 1), :]
        spot = jnp.where(m >= 0, spot.astype(jnp.int32), -1)
        double = jnp.right_shift(spot, 1)
        second = jnp.bitwise_and(spot, 1) == 1
        here = (line == jnp.right_shift(double, 7)) & (m >= 0)
        lane_hot = jnp.where(column == jnp.bitwise_and(double, 127), 1.0, 0.0).astype(BF16)
        zero = jnp.zeros((1, 128), F32)
        parts = [jnp.bitwise_and(i, 63), jnp.right_shift(i, 6)] if wide else [i]
        parts = [x.astype(F32) for x in parts]
        values = [jnp.where(second, zero, m.astype(F32))]
        values += [jnp.where(second, zero, x) for x in parts] + [jnp.where(second, x, zero) for x in parts]
        left = jnp.concatenate([jnp.where(here, v, 0.0) for v in values], axis=0).astype(BF16)
        return acc + lax.dot_general(left, lane_hot, (((1,), (1,)), ((), ())), preferred_element_type=F32)

    acc = lax.fori_loop(0, chunks, place, jnp.zeros((groups * lines, 128), F32), unroll=8)
    found = [acc[j * lines : (j + 1) * lines].astype(jnp.int32) for j in range(groups)]
    size = out.shape[0] // 3
    out[0:size, :] = found[0][0:size]
    for j in range(2):
        i = found[1 + 2 * j] + 64 * found[2 + 2 * j] if wide else found[1 + j]
        out[(j + 1) * size : (j + 2) * size, :] = jnp.where(i == 0, dummy, i - 1)[0:size]
    out[out.shape[0] - 1 :, :] = doubles.astype(jnp.int32)


def conc_rows(conc):
    conc = conc * RATE
    high = conc.astype(BF16).astype(F32)
    ones = jnp.full_like(conc, RATE)
    return jnp.concatenate([high, conc - high, ones, ones], axis=1).astype(BF16)


def fill_rows(conc, rows, slot):
    cells = conc.shape[1]
    rows[pl.ds(slot * cells, cells)] = conc_rows(conc[slot])


def share_plane(at, src, dst, sems, pass_sems):
    me = at.slot(0, 0, 0)
    copies = {
        (dp, db): remote(src, dst.at[me], sems, (dp, db), at.across(dp, db, 0)) for dp, db in at.plane()
    }
    return copies, {(0, 0): remote(src, dst.at[me], pass_sems, (0, 0), at.across(0, 0, 1))}


def pass_on(at, copies, passed, dst, pass_sems):
    for (dp, db), copy in copies.items():
        copy.wait_recv()
        block = dst.at[at.slot(-dp, -db, 0)]
        passed[dp, db] = remote(block, block, pass_sems, (dp, db), at.across(0, 0, 1))


def share_along(at, src, dst, sems):
    return {da: remote(src, dst.at[at.a], sems, da, at.along(da)) for da in range(1, at.na)}


def take_plane(at, copies, passed, conc, rows):
    for dp, db in copies:
        fill_rows(conc, rows, at.slot(-dp, -db, 0))
    for (dp, db), copy in passed.items():
        copy.wait_recv()
        fill_rows(conc, rows, at.slot(-dp, -db, 1))


def take_along(at, copies, conc, rows):
    for da, copy in copies.items():
        copy.wait_recv()
        fill_rows(conc, rows, at.am(-da))


def finish_sends(*groups):
    for group in groups:
        for copy in group.values():
            copy.wait_send()


def first_gather(n_mob, n_imm, mpos, walk, mconc, ipos, iconc, rows, cols, count,
                 g_conc, h_conc, m_rows, i_rows, x_all, y_one, pair_list, h_pos,
                 g_pos, lists, in_m, in_w, in_i, in_r, in_c, in_n, stage, keep_m, keep_i, keep_rank, *sems):
    at = Place(n_mob, n_imm)
    local = sems[0]
    z_pos, z_conc, p_pos, p_conc, c_pos, c_conc, l_sem = [sems[j : j + 2] for j in range(1, 15, 2)]
    me = at.slot(0, 0, 0)
    reads = [
        pltpu.make_async_copy(src, dst, local.at[j])
        for j, (src, dst) in enumerate((
            (mpos, in_m), (walk, in_w), (ipos, in_i), (rows, in_r), (cols, in_c), (count, in_n),
            (iconc, g_conc.at[at.a]), (mconc, h_conc.at[me]),
        ))
    ]
    for read in reads:
        read.start()
    sem, peers = at.greet(lists=True)
    clear_spare(h_conc, i_rows, y_one)
    reads[0].wait()
    reads[1].wait()
    moved = in_m[...] + in_w[0]
    h_pos[me, 0] = (moved - CENTRE) * SCALE
    h_pos[me, 1] = ((moved + in_w[1]) - CENTRE) * SCALE
    reads[2].wait()
    g_pos[at.a] = (in_i[...] - CENTRE) * SCALE
    for read in reads[3:6]:
        read.wait()
    home = at.p * at.na + at.a
    lane = lax.broadcasted_iota(jnp.int32, (1, 128), 1)
    for j in range(4):
        r = in_r[0, :, j * 128 : (j + 1) * 128]
        lists[home, j : j + 1, :] = jnp.where(j * 128 + lane < in_n[...], r, -1)
        lists[home, 4 + j : 5 + j, :] = in_c[0, :, j * 128 : (j + 1) * 128]
    build_x(g_pos.at[at.a], stage, x_all, at.a)
    build_y(h_pos.at[me, 0], stage, y_one, me)
    for read in reads[6:]:
        read.wait()
    fill_rows(g_conc, m_rows, at.a)
    fill_rows(h_conc, i_rows, me)
    mc, ic = iconc.shape[0], mconc.shape[0]
    total = count_list(at, mc, ic, lists, keep_m, keep_i, keep_rank, 0, 4, jnp.zeros((at.na * mc, 128), F32))
    pl.semaphore_wait(sem, peers)
    shared = {
        (dp, da): remote(lists.at[home], lists.at[home], l_sem, (dp, da), at.mate(dp, da)) for dp, da in at.mates()
    }
    z_far = share_along(at, g_pos.at[at.a], g_pos, z_pos)
    z_conc = share_along(at, g_conc.at[at.a], g_conc, z_conc)
    p_far, p_near = share_plane(at, h_pos.at[me], h_pos, p_pos, c_pos)
    p_conc, p_near_conc = share_plane(at, h_conc.at[me], h_conc, p_conc, c_conc)
    for copy in shared.values():
        copy.wait_recv()
    total = count_list(at, mc, ic, lists, keep_m, keep_i, keep_rank, 4, lists.shape[0] * 4, total)
    pass_on(at, p_far, p_near, h_pos, c_pos)
    pass_on(at, p_conc, p_near_conc, h_conc, c_conc)
    place_list(at, mc, ic, lists, keep_m, keep_i, keep_rank, total, pair_list)
    for dp, db in p_far:
        here = at.slot(-dp, -db, 0)
        build_y(h_pos.at[here, 0], stage, y_one, here)
    for (dp, db), copy in p_near.items():
        copy.wait_recv()
        here = at.slot(-dp, -db, 1)
        build_y(h_pos.at[here, 0], stage, y_one, here)
    for da, copy in z_far.items():
        copy.wait_recv()
        build_x(g_pos.at[at.am(-da)], stage, x_all, at.am(-da))
    take_plane(at, p_conc, p_near_conc, h_conc, i_rows)
    take_along(at, z_conc, g_conc, m_rows)
    finish_sends(z_far, z_conc, shared, p_far, p_near, p_conc, p_near_conc)


def clear_spare(h_conc, i_rows, y_all):
    h_conc[h_conc.shape[0] - 1] = jnp.zeros(h_conc.shape[1:], F32)
    i_rows[i_rows.shape[0] - 16 :] = jnp.zeros((16,) + i_rows.shape[1:], BF16)
    row = lax.broadcasted_iota(jnp.int32, (8, TERMS, 128), 1)
    y_all[y_all.shape[0] - 8 :] = jnp.where(row == 12, FAR, 0.0).astype(BF16)


def reduce_start(at, part_m, part_i, land_m, land_c, out_b, land_b, z_sem, c_sem, b_sem):
    mc, ic = land_m.shape[1], land_c.shape[2]
    c_copies = {
        (dp, db): remote(
            part_i.at[pl.ds(at.slot(dp, db, 1) * ic, ic)], land_c.at[dp, db], c_sem, (dp, db), at.across(0, 0, 1))
        for dp, db in at.plane() + [(0, 0)]
    }
    z_copies = {
        da: remote(part_m.at[pl.ds(at.am(da) * mc, mc)], land_m.at[da], z_sem, da, at.along(da))
        for da in range(1, at.na)
    }
    b_copies = {}
    for dp, db in at.plane():
        c_copies[dp, db].wait_recv()
        out_b[dp, db] = part_i[pl.ds(at.slot(dp, db, 0) * ic, ic)] + land_c[dp, db]
        b_copies[dp, db] = remote(out_b.at[dp, db], land_b.at[dp, db], b_sem, (dp, db), at.across(dp, db, 0))
    return z_copies, c_copies, b_copies


def reduce_end(base, part, slot, land, copies):
    cells = base.shape[0]
    total = base[...] + part[pl.ds(slot * cells, cells)]
    for key, copy in copies.items():
        copy.wait_recv()
        total = total + land[key]
    return total


def reduce_plane_end(at, base, part, land_c, land_b, c_copies, b_copies):
    c_copies[0, 0].wait_recv()
    return reduce_end(base, part, at.slot(0, 0, 0), land_b, b_copies) + land_c[0, 0]


def exchange(n_mob, n_imm, part_m, part_i, conc_m, conc_i, h_pos, own_m, own_i, g_conc, h_conc, m_rows, i_rows,
             y_two, land_m, land_c, out_b, land_b, stage, *sems):
    at = Place(n_mob, n_imm)
    z_sem, c_sem, b_sem, z_conc, p_conc, c_conc = [sems[j : j + 2] for j in range(0, 12, 2)]
    sem, peers = at.greet()
    clear_spare(h_conc, i_rows, y_two)
    pl.semaphore_wait(sem, peers)
    z_copies, c_copies, b_copies = reduce_start(
        at, part_m, part_i, land_m, land_c, out_b, land_b, z_sem, c_sem, b_sem)
    for slot in range(h_pos.shape[0]):
        build_y(h_pos.at[slot, 1], stage, y_two, slot)
    me = at.slot(0, 0, 0)
    own_i[...] = reduce_plane_end(at, conc_i, part_i, land_c, land_b, c_copies, b_copies)
    p_conc, p_near = share_plane(at, own_i, h_conc, p_conc, c_conc)
    own_m[...] = reduce_end(conc_m, part_m, at.a, land_m, z_copies)
    z_conc = share_along(at, own_m, g_conc, z_conc)
    g_conc[at.a] = own_m[...]
    h_conc[me] = own_i[...]
    fill_rows(g_conc, m_rows, at.a)
    fill_rows(h_conc, i_rows, me)
    pass_on(at, p_conc, p_near, h_conc, c_conc)
    take_plane(at, p_conc, p_near, h_conc, i_rows)
    take_along(at, z_conc, g_conc, m_rows)
    finish_sends(z_copies, c_copies, b_copies, z_conc, p_conc, p_near)


def last_reduce(n_mob, n_imm, part_m, part_i, conc_m, conc_i, own_m, own_i, land_m, land_c, out_b, land_b, *sems):
    at = Place(n_mob, n_imm)
    sem, peers = at.greet()
    pl.semaphore_wait(sem, peers)
    z_copies, c_copies, b_copies = reduce_start(
        at, part_m, part_i, land_m, land_c, out_b, land_b, sems[0:2], sems[2:4], sems[4:6])
    own_i[...] = reduce_plane_end(at, conc_i, part_i, land_c, land_b, c_copies, b_copies)
    own_m[...] = reduce_end(conc_m, part_m, at.a, land_m, z_copies)
    finish_sends(z_copies, c_copies, b_copies)


def pair_loop(pair_list, x_all, y_all, x_conc, y_conc, m_rows, i_rows, gain_m, gain_i,
              lst, p_even, p_odd, w_even, w_odd, sem):
    read = pltpu.make_async_copy(pair_list, lst, sem)
    read.start()
    gain_m[...] = jnp.zeros_like(gain_m)
    gain_i[...] = jnp.zeros_like(gain_i)
    read.wait()
    size = lst.shape[0] // 3 // 128 * 128
    used = lst[lst.shape[0] - 128]

    def entry(block, u):
        spot = block * UNROLL
        return lst[spot + u], lst[spot + (size + u)], lst[spot + (2 * size + u)]

    def measure(block, u, powers):
        m, i, k = entry(block, u)
        right = jnp.concatenate([y_all[i], y_all[k]], axis=1)
        powers[u] = jnp.dot(x_all[m][:, :TERMS], right, preferred_element_type=F32)

    def weigh(u, powers, weights):
        weights[u] = jnp.exp2(powers[u]).astype(BF16)

    def transfer(block, u, weights):
        m, i, k = entry(block, u)
        weight = weights[u]
        to_i = jnp.dot(m_rows[m], weight, preferred_element_type=F32)
        right = jnp.concatenate([i_rows[i], i_rows[k]], axis=1)
        to_m = lax.dot_general(right, weight, (((1,), (1,)), ((), ())), preferred_element_type=F32)
        return m, i, k, to_i, to_m

    def finish(m, i, k, to_i, to_m):
        gain_m[m] += to_m[0:8] + to_m[8:16] - to_m[16:24] * x_conc[m]
        gain_i[i] += to_i[0:8, :128] + to_i[8:16, :128] - to_i[16:24, :128] * y_conc[i]
        gain_i[k] += to_i[0:8, 128:] + to_i[8:16, 128:] - to_i[16:24, 128:] * y_conc[k]

    def step(block, first=None, second=None, third=None):
        moved = []
        for u in range(UNROLL):
            if second is not None:
                weigh(u, *second)
            if first is not None:
                measure(block, u, first)
            if third is not None:
                moved.append(transfer(block - 2, u, third))
        for item in moved:
            finish(*item)

    pairs = jnp.maximum(lax.div(used + (2 * UNROLL - 1), 2 * UNROLL), 1)
    step(0, p_even)
    step(1, p_odd, (p_even, w_even))

    def body(t, carry):
        step(2 * t, p_even, (p_odd, w_odd), w_even)
        step(2 * t + 1, p_odd, (p_even, w_even), w_odd)
        return carry

    lax.fori_loop(1, pairs, body, 0)
    step(2 * pairs, None, (p_odd, w_odd), w_even)
    step(2 * pairs + 1, None, None, w_odd)


def write_out(own_m, own_i, out_m, out_i, sems):
    copies = [
        pltpu.make_async_copy(src, dst, sems.at[j]) for j, (src, dst) in enumerate(((own_m, out_m), (own_i, out_i)))
    ]
    for copy in copies:
        copy.start()
    for copy in copies:
        copy.wait()


def on_device(n_mob, n_imm, mpos, walk, mconc, ipos, iconc, rows, cols, counts):
    nm, nb, na = sizes(n_mob, n_imm)
    mc, solutes, part = iconc.shape
    ic = mconc.shape[0]
    slots = nm * nb * 2
    cells_m, cells_i = na * mc, slots * ic
    tiles = nm * na
    chunks = tiles * 4
    lines = -(-(chunks * 64 + cells_m // 2 + 2 * UNROLL) // 128)
    list_rows = -(-(3 * lines + 1) // 8) * 8
    vmem = pl.BlockSpec(memory_space=pltpu.VMEM)
    anywhere = pl.BlockSpec(memory_space=pl.ANY)
    hbm = pl.BlockSpec(memory_space=pltpu.HBM)
    dma = pltpu.SemaphoreType.DMA

    def params(ident):
        return pltpu.CompilerParams(collective_id=ident, has_side_effects=True, vmem_limit_bytes=VMEM_LIMIT)

    def shape(dims, dtype=F32):
        return jax.ShapeDtypeStruct(dims, dtype)

    def pairs(*dims):
        return [dma(dims)] * 2

    cell_m, cell_i = (mc, solutes, part), (ic, solutes, part)
    all_m, all_i = (na,) + cell_m, (slots + 1,) + cell_i
    pos_m, pos_i = (3, mc, part), (3, ic, part)
    stage = pltpu.VMEM((max(mc, ic) * TERMS, part), F32)
    x_shape = shape((cells_m, part, 128), BF16)
    concs = (
        shape(all_m), shape(all_i),
        shape((cells_m, 4 * solutes, part), BF16), shape((cells_i + 16, 4 * solutes, part), BF16),
    )
    plane = (nm, nb)
    y_shape = shape((cells_i + 8, TERMS, part), BF16)
    *concs_one, x_all, y_one, pair_list, h_pos = pl.pallas_call(
        functools.partial(first_gather, n_mob, n_imm),
        out_shape=concs + (
            x_shape, y_shape, shape((list_rows, 128), jnp.int32), shape((slots, 2) + pos_i),
        ),
        in_specs=[hbm] * 8,
        out_specs=(vmem,) * 8,
        scratch_shapes=[
            pltpu.VMEM((na,) + pos_m, F32), pltpu.VMEM((tiles, 8, 128), jnp.int32),
            pltpu.VMEM(pos_i, F32), pltpu.VMEM((2,) + pos_i, F32), pltpu.VMEM(pos_m, F32),
            pltpu.VMEM(rows.shape, jnp.int32), pltpu.VMEM(cols.shape, jnp.int32), pltpu.VMEM((1, 1), jnp.int32),
            stage, pltpu.VMEM((chunks, 128), jnp.int32), pltpu.VMEM((chunks, 128), jnp.int32),
            pltpu.VMEM((chunks, 128), F32),
            dma((8,)), *pairs(na), *pairs(na), *pairs(*plane), *pairs(*plane), *pairs(*plane), *pairs(*plane),
            *pairs(nm, na),
        ],
        compiler_params=params(0),
    )(*[
        pltpu.with_memory_space_constraint(x, pltpu.HBM)
        for x in (jnp.transpose(mpos, (1, 0, 2)), jnp.transpose(walk, (0, 2, 1, 3)), mconc,
                  jnp.transpose(ipos, (1, 0, 2)), iconc, rows, cols)
    ], counts)
    flat_list = pair_list.reshape(-1)

    def gains(y_all, x_conc, y_conc, m_rows, i_rows):
        return pl.pallas_call(
            pair_loop,
            out_shape=(shape((cells_m, solutes, part)), shape((cells_i + 1, solutes, part))),
            in_specs=[anywhere] + [vmem] * 6,
            out_specs=(vmem,) * 2,
            scratch_shapes=[
                pltpu.SMEM((flat_list.shape[0],), jnp.int32),
                pltpu.VMEM((UNROLL, part, 256), F32), pltpu.VMEM((UNROLL, part, 256), F32),
                pltpu.VMEM((UNROLL, part, 256), BF16), pltpu.VMEM((UNROLL, part, 256), BF16),
                dma,
            ],
            compiler_params=pltpu.CompilerParams(vmem_limit_bytes=VMEM_LIMIT),
        )(flat_list, x_all, y_all, x_conc.reshape((cells_m, solutes, part)),
          y_conc.reshape((cells_i + ic, solutes, part)), m_rows, i_rows)

    lands = [pltpu.VMEM((na,) + cell_m, F32)] + [pltpu.VMEM(plane + cell_i, F32)] * 3
    own = (shape(cell_m), shape(cell_i))
    part_m, part_i = gains(y_one, *concs_one)
    own_m, own_i, *concs_two, y_two = pl.pallas_call(
        functools.partial(exchange, n_mob, n_imm),
        out_shape=own + concs + (y_shape,),
        in_specs=[vmem] * 5,
        out_specs=(vmem,) * 7,
        scratch_shapes=lands + [stage, *pairs(na), *pairs(*plane), *pairs(*plane),
                                *pairs(na), *pairs(*plane), *pairs(*plane)],
        compiler_params=params(1),
    )(part_m, part_i, iconc, mconc, h_pos)
    part_m, part_i = gains(y_two, *concs_two)
    own_m, own_i = pl.pallas_call(
        functools.partial(last_reduce, n_mob, n_imm),
        out_shape=own,
        in_specs=[vmem] * 4,
        out_specs=(vmem,) * 2,
        scratch_shapes=lands + [*pairs(na), *pairs(*plane), *pairs(*plane)],
        compiler_params=params(2),
    )(part_m, part_i, own_m, own_i)
    return pl.pallas_call(
        write_out,
        out_shape=own[::-1],
        in_specs=[vmem] * 2,
        out_specs=(anywhere,) * 2,
        scratch_shapes=[dma((2,))],
        compiler_params=pltpu.CompilerParams(vmem_limit_bytes=VMEM_LIMIT),
    )(own_i, own_m)


def solution(mesh):
    return jax.shard_map(
        functools.partial(on_device, mesh.shape["mob"], mesh.shape["imm"]),
        mesh=mesh,
        in_specs=(
            P(("mob", "imm"), None, None),
            P(None, ("mob", "imm"), None, None),
            P(("mob", "imm"), None, None),
            P(("mob", "imm"), None, None),
            P(("mob", "imm"), None, None),
            P("mob", "imm", None),
            P("mob", "imm", None),
            P("mob", "imm"),
        ),
        out_specs=(P(("mob", "imm"), None, None), P(("mob", "imm"), None, None)),
        check_vma=False,
    )
```

```python
import functools
import math

import jax
import jax.numpy as jnp
from jax import lax
from jax.experimental import pallas as pl
from jax.experimental.pallas import tpu as pltpu
from jax.sharding import PartitionSpec as P

RATE = 1.0 / 512.0
SCALE = math.sqrt(0.5 * math.log2(math.e))
CENTRE = 2.0
FAR = -30000.0
MESH = pl.DeviceIdType.MESH
VMEM_LIMIT = 20 * 1024 * 1024
UNROLL = 16
TERMS = 16
F32 = jnp.float32
BF16 = jnp.bfloat16


def sizes(n_mob, n_imm):
    rest = n_imm // 2
    nb = 1
    while nb * nb * 4 <= rest:
        nb *= 2
    return n_mob, nb, rest // nb


class Place:
    def __init__(self, n_mob, n_imm):
        self.nm, self.nb, self.na = sizes(n_mob, n_imm)
        self.p = lax.axis_index("mob")
        q = lax.axis_index("imm")
        self.core = lax.rem(q, 2)
        chip = lax.div(q, 2)
        self.b = lax.rem(chip, self.nb)
        self.a = lax.div(chip, self.nb)

    def am(self, d):
        return lax.rem(self.a + (d + self.na), self.na)

    def bm(self, d):
        return lax.rem(self.b + (d + self.nb), self.nb)

    def pm(self, d):
        return lax.rem(self.p + (d + self.nm), self.nm)

    def dev(self, p, a, b, core):
        return (p, (a * self.nb + b) * 2 + core)

    def along(self, da):
        return self.dev(self.p, self.am(da), self.b, self.core)

    def other(self, dc):
        return 1 - self.core if dc else self.core

    def across(self, dp, db, dc):
        return self.dev(self.pm(dp), self.a, self.bm(db), self.other(dc))

    def plane(self):
        keys = [(dp, db) for dp in range(self.nm) for db in range(self.nb)]
        return sorted((key for key in keys if any(key)), key=lambda key: -bool(key[0]) - bool(key[1]))

    def mates(self):
        return [(dp, da) for dp in range(self.nm) for da in range(self.na) if dp or da]

    def mate(self, dp, da):
        return self.dev(self.pm(dp), self.am(da), self.b, self.core)

    def slot(self, dp, db, dc):
        return (self.pm(dp) * self.nb + self.bm(db)) * 2 + self.other(dc)

    def greet(self, lists=False):
        sem = pltpu.get_barrier_semaphore()
        peers = [self.along(d) for d in range(1, self.na)] + [self.across(0, 0, 1)]
        peers += [self.across(dp, db, 0) for dp, db in self.plane()]
        if lists:
            peers += [self.mate(dp, da) for dp, da in self.mates() if dp and da]
        for peer in peers:
            pl.semaphore_signal(sem, inc=1, device_id=peer, device_id_type=MESH)
        return sem, len(peers)


def remote(src, dst, sems, index, device):
    copy = pltpu.make_async_remote_copy(
        src_ref=src, dst_ref=dst, send_sem=sems[0].at[index], recv_sem=sems[1].at[index],
        device_id=device, device_id_type=MESH,
    )
    copy.start()
    return copy


def split2(x):
    high = x.astype(BF16).astype(F32)
    return high, x - high


def split3(x):
    high, rest = split2(x)
    mid, low = split2(rest)
    return high, mid, low


def rows_x(x):
    (xh, xm), (yh, ym), (zh, zm) = [split2(x[j]) for j in range(3)]
    norm = split3(-(x[0] * x[0] + x[1] * x[1] + x[2] * x[2]))
    one = jnp.ones_like(x[0])
    return [xh, yh, zh, xh, yh, zh, xm, ym, zm, *norm, one, one, one, jnp.zeros_like(one)]


def rows_y(y):
    (xh, xm), (yh, ym), (zh, zm) = [split2(2.0 * y[j]) for j in range(3)]
    norm = split3(-(y[0] * y[0] + y[1] * y[1] + y[2] * y[2]))
    one = jnp.ones_like(y[0])
    return [xh, yh, zh, xm, ym, zm, xh, yh, zh, one, one, one, *norm, jnp.zeros_like(one)]


def fill(stage, rows):
    cells = rows[0].shape[0]
    for j, row in enumerate(rows):
        stage[pl.ds(j, cells, stride=TERMS), :] = row


def build_y(pos, stage, out, slot):
    cells = pos.shape[1]
    fill(stage, rows_y([pos[j] for j in range(3)]))
    out[pl.ds(slot * cells, cells)] = stage[...].reshape(cells, TERMS, 128).astype(BF16)


def build_x(pos, stage, out, slot):
    cells = pos.shape[1]
    fill(stage, rows_x([pos[j] for j in range(3)]))
    for group in range(0, cells, 128 // TERMS):
        block = stage[group * TERMS : group * TERMS + 128, :].T.astype(BF16)
        for j in range(128 // TERMS):
            out[slot * cells + group + j, :, :TERMS] = block[:, j * TERMS : (j + 1) * TERMS]


def count_list(at, mc, ic, lists, keep_m, keep_i, keep_rank, first, last, total):
    lists_n = lists.shape[0]
    cells_m = at.na * mc
    shift_m, shift_i, shift_b = [int(math.log2(n)) for n in (mc, ic, at.nb)]
    mine = lax.broadcasted_iota(jnp.int32, (cells_m, 128), 0)
    column = lax.broadcasted_iota(jnp.int32, (128, 256), 1)
    upper = jnp.where(
        (lax.broadcasted_iota(jnp.int32, (128, 256), 0) <= column) | (column >= 128), 1.0, 0.0
    ).astype(BF16)
    home = at.p * at.na + at.a

    def count(chunk, total):
        which, part = lax.rem(lax.div(chunk, 4) + home, lists_n), lax.rem(chunk, 4)
        r = lists[which, pl.ds(part, 1), :]
        c = lists[which, pl.ds(4 + part, 1), :]
        owner = jnp.right_shift(r, shift_i)
        ok = (
            (r >= 0)
            & (jnp.right_shift(owner, 1 + shift_b) == at.a)
            & (jnp.right_shift(c, shift_m) == at.p)
        )
        m = lax.rem(which, at.na) * mc + jnp.bitwise_and(c, mc - 1)
        m = jnp.where(ok, m, -1)
        spot = lax.div(which, at.na) * (at.nb * 2) + jnp.bitwise_and(owner, at.nb * 2 - 1)
        i = spot * ic + jnp.bitwise_and(r, ic - 1)
        hot = jnp.where(mine == m, 1.0, 0.0).astype(F32)
        rank = jnp.dot(hot.astype(BF16), upper, preferred_element_type=F32)
        keep_m[pl.ds(chunk, 1), :] = m
        keep_i[pl.ds(chunk, 1), :] = i + 1
        keep_rank[pl.ds(chunk, 1), :] = jnp.sum(hot * (rank[:, :128] + total), axis=0, keepdims=True) - 1.0
        return total + rank[:, 128:]

    return lax.fori_loop(first, last, count, total, unroll=7)


def place_list(at, mc, ic, lists, keep_m, keep_i, keep_rank, total, out):
    lists_n, chunks = lists.shape[0], lists.shape[0] * 4
    cells_m = at.na * mc
    lines = -(-(out.shape[0] // 3) // 8) * 8
    dummy = at.nm * at.nb * 2 * ic
    wide = dummy > 255
    groups = 5 if wide else 3
    mine = lax.broadcasted_iota(jnp.int32, (cells_m, 128), 0)
    lower = jnp.where(
        lax.broadcasted_iota(jnp.int32, (cells_m, cells_m), 0)
        > lax.broadcasted_iota(jnp.int32, (cells_m, cells_m), 1), 1.0, 0.0
    ).astype(F32)
    even = 2.0 * jnp.floor((total + 1.0) * 0.5)
    start = jnp.dot(lower, even, preferred_element_type=F32, precision=lax.Precision.HIGHEST)
    doubles = jnp.sum(even, axis=0, keepdims=True) * 0.5
    line = lax.broadcasted_iota(jnp.int32, (lines, 128), 0)
    column = lax.broadcasted_iota(jnp.int32, (128, 128), 0)

    def place(chunk, acc):
        m = keep_m[pl.ds(chunk, 1), :]
        i = keep_i[pl.ds(chunk, 1), :]
        hot = jnp.where(mine == m, 1.0, 0.0).astype(F32)
        spot = jnp.sum(hot * start, axis=0, keepdims=True) + keep_rank[pl.ds(chunk, 1), :]
        spot = jnp.where(m >= 0, spot.astype(jnp.int32), -1)
        double = jnp.right_shift(spot, 1)
        second = jnp.bitwise_and(spot, 1) == 1
        here = (line == jnp.right_shift(double, 7)) & (m >= 0)
        lane_hot = jnp.where(column == jnp.bitwise_and(double, 127), 1.0, 0.0).astype(BF16)
        zero = jnp.zeros((1, 128), F32)
        parts = [jnp.bitwise_and(i, 63), jnp.right_shift(i, 6)] if wide else [i]
        parts = [x.astype(F32) for x in parts]
        values = [jnp.where(second, zero, m.astype(F32))]
        values += [jnp.where(second, zero, x) for x in parts] + [jnp.where(second, x, zero) for x in parts]
        left = jnp.concatenate([jnp.where(here, v, 0.0) for v in values], axis=0).astype(BF16)
        return acc + lax.dot_general(left, lane_hot, (((1,), (1,)), ((), ())), preferred_element_type=F32)

    acc = lax.fori_loop(0, chunks, place, jnp.zeros((groups * lines, 128), F32), unroll=8)
    found = [acc[j * lines : (j + 1) * lines].astype(jnp.int32) for j in range(groups)]
    size = out.shape[0] // 3
    out[0:size, :] = found[0][0:size]
    for j in range(2):
        i = found[1 + 2 * j] + 64 * found[2 + 2 * j] if wide else found[1 + j]
        out[(j + 1) * size : (j + 2) * size, :] = jnp.where(i == 0, dummy, i - 1)[0:size]
    out[out.shape[0] - 1 :, :] = doubles.astype(jnp.int32)


def conc_rows(conc):
    conc = conc * RATE
    high = conc.astype(BF16).astype(F32)
    ones = jnp.full_like(conc, RATE)
    return jnp.concatenate([high, conc - high, ones, ones], axis=1).astype(BF16)


def fill_rows(conc, rows, slot):
    cells = conc.shape[1]
    rows[pl.ds(slot * cells, cells)] = conc_rows(conc[slot])


def share_plane(at, src, dst, sems, pass_sems):
    me = at.slot(0, 0, 0)
    copies = {
        (dp, db): remote(src, dst.at[me], sems, (dp, db), at.across(dp, db, 0)) for dp, db in at.plane()
    }
    return copies, {(0, 0): remote(src, dst.at[me], pass_sems, (0, 0), at.across(0, 0, 1))}


def pass_on(at, copies, passed, dst, pass_sems):
    for (dp, db), copy in copies.items():
        copy.wait_recv()
        block = dst.at[at.slot(-dp, -db, 0)]
        passed[dp, db] = remote(block, block, pass_sems, (dp, db), at.across(0, 0, 1))


def share_along(at, src, dst, sems):
    return {da: remote(src, dst.at[at.a], sems, da, at.along(da)) for da in range(1, at.na)}


def take_plane(at, copies, passed, conc, rows):
    for dp, db in copies:
        fill_rows(conc, rows, at.slot(-dp, -db, 0))
    for (dp, db), copy in passed.items():
        copy.wait_recv()
        fill_rows(conc, rows, at.slot(-dp, -db, 1))


def take_along(at, copies, conc, rows):
    for da, copy in copies.items():
        copy.wait_recv()
        fill_rows(conc, rows, at.am(-da))


def finish_sends(*groups):
    for group in groups:
        for copy in group.values():
            copy.wait_send()


def first_gather(n_mob, n_imm, mpos, walk, mconc, ipos, iconc, rows, cols, count,
                 g_conc, h_conc, m_rows, i_rows, x_all, y_one, pair_list, h_pos,
                 g_pos, lists, in_m, in_w, in_i, in_r, in_c, in_n, stage, keep_m, keep_i, keep_rank, *sems):
    at = Place(n_mob, n_imm)
    local = sems[0]
    z_pos, z_conc, p_pos, p_conc, c_pos, c_conc, l_sem = [sems[j : j + 2] for j in range(1, 15, 2)]
    me = at.slot(0, 0, 0)
    reads = [
        pltpu.make_async_copy(src, dst, local.at[j])
        for j, (src, dst) in enumerate((
            (mpos, in_m), (walk, in_w), (ipos, in_i), (rows, in_r), (cols, in_c), (count, in_n),
            (iconc, g_conc.at[at.a]), (mconc, h_conc.at[me]),
        ))
    ]
    for read in reads:
        read.start()
    sem, peers = at.greet(lists=True)
    clear_spare(h_conc, i_rows, y_one)
    reads[0].wait()
    reads[1].wait()
    moved = in_m[...] + in_w[0]
    h_pos[me, 0] = (moved - CENTRE) * SCALE
    h_pos[me, 1] = ((moved + in_w[1]) - CENTRE) * SCALE
    reads[2].wait()
    g_pos[at.a] = (in_i[...] - CENTRE) * SCALE
    for read in reads[3:6]:
        read.wait()
    home = at.p * at.na + at.a
    lane = lax.broadcasted_iota(jnp.int32, (1, 128), 1)
    for j in range(4):
        r = in_r[0, :, j * 128 : (j + 1) * 128]
        lists[home, j : j + 1, :] = jnp.where(j * 128 + lane < in_n[...], r, -1)
        lists[home, 4 + j : 5 + j, :] = in_c[0, :, j * 128 : (j + 1) * 128]
    build_x(g_pos.at[at.a], stage, x_all, at.a)
    build_y(h_pos.at[me, 0], stage, y_one, me)
    for read in reads[6:]:
        read.wait()
    fill_rows(g_conc, m_rows, at.a)
    fill_rows(h_conc, i_rows, me)
    mc, ic = iconc.shape[0], mconc.shape[0]
    total = count_list(at, mc, ic, lists, keep_m, keep_i, keep_rank, 0, 4, jnp.zeros((at.na * mc, 128), F32))
    pl.semaphore_wait(sem, peers)
    shared = {
        (dp, da): remote(lists.at[home], lists.at[home], l_sem, (dp, da), at.mate(dp, da)) for dp, da in at.mates()
    }
    z_far = share_along(at, g_pos.at[at.a], g_pos, z_pos)
    z_conc = share_along(at, g_conc.at[at.a], g_conc, z_conc)
    p_far, p_near = share_plane(at, h_pos.at[me], h_pos, p_pos, c_pos)
    p_conc, p_near_conc = share_plane(at, h_conc.at[me], h_conc, p_conc, c_conc)
    for copy in shared.values():
        copy.wait_recv()
    total = count_list(at, mc, ic, lists, keep_m, keep_i, keep_rank, 4, lists.shape[0] * 4, total)
    pass_on(at, p_far, p_near, h_pos, c_pos)
    place_list(at, mc, ic, lists, keep_m, keep_i, keep_rank, total, pair_list)
    pass_on(at, p_conc, p_near_conc, h_conc, c_conc)
    for dp, db in p_far:
        here = at.slot(-dp, -db, 0)
        build_y(h_pos.at[here, 0], stage, y_one, here)
    for (dp, db), copy in p_near.items():
        copy.wait_recv()
        here = at.slot(-dp, -db, 1)
        build_y(h_pos.at[here, 0], stage, y_one, here)
    for da, copy in z_far.items():
        copy.wait_recv()
        build_x(g_pos.at[at.am(-da)], stage, x_all, at.am(-da))
    take_plane(at, p_conc, p_near_conc, h_conc, i_rows)
    take_along(at, z_conc, g_conc, m_rows)
    finish_sends(z_far, z_conc, shared, p_far, p_near, p_conc, p_near_conc)


def clear_spare(h_conc, i_rows, y_all):
    h_conc[h_conc.shape[0] - 1] = jnp.zeros(h_conc.shape[1:], F32)
    i_rows[i_rows.shape[0] - 16 :] = jnp.zeros((16,) + i_rows.shape[1:], BF16)
    row = lax.broadcasted_iota(jnp.int32, (8, TERMS, 128), 1)
    y_all[y_all.shape[0] - 8 :] = jnp.where(row == 12, FAR, 0.0).astype(BF16)


def reduce_start(at, part_m, part_i, land_m, land_c, out_b, land_b, z_sem, c_sem, b_sem):
    mc, ic = land_m.shape[1], land_c.shape[2]
    c_copies = {
        (dp, db): remote(
            part_i.at[pl.ds(at.slot(dp, db, 1) * ic, ic)], land_c.at[dp, db], c_sem, (dp, db), at.across(0, 0, 1))
        for dp, db in at.plane() + [(0, 0)]
    }
    z_copies = {
        da: remote(part_m.at[pl.ds(at.am(da) * mc, mc)], land_m.at[da], z_sem, da, at.along(da))
        for da in range(1, at.na)
    }
    b_copies = {}
    for dp, db in at.plane():
        c_copies[dp, db].wait_recv()
        out_b[dp, db] = part_i[pl.ds(at.slot(dp, db, 0) * ic, ic)] + land_c[dp, db]
        b_copies[dp, db] = remote(out_b.at[dp, db], land_b.at[dp, db], b_sem, (dp, db), at.across(dp, db, 0))
    return z_copies, c_copies, b_copies


def reduce_end(base, part, slot, land, copies):
    cells = base.shape[0]
    total = base[...] + part[pl.ds(slot * cells, cells)]
    for key, copy in copies.items():
        copy.wait_recv()
        total = total + land[key]
    return total


def reduce_plane_end(at, base, part, land_c, land_b, c_copies, b_copies):
    c_copies[0, 0].wait_recv()
    return reduce_end(base, part, at.slot(0, 0, 0), land_b, b_copies) + land_c[0, 0]


def exchange(n_mob, n_imm, part_m, part_i, conc_m, conc_i, h_pos, own_m, own_i, g_conc, h_conc, m_rows, i_rows,
             y_two, land_m, land_c, out_b, land_b, stage, *sems):
    at = Place(n_mob, n_imm)
    z_sem, c_sem, b_sem, z_conc, p_conc, c_conc = [sems[j : j + 2] for j in range(0, 12, 2)]
    sem, peers = at.greet()
    clear_spare(h_conc, i_rows, y_two)
    pl.semaphore_wait(sem, peers)
    z_copies, c_copies, b_copies = reduce_start(
        at, part_m, part_i, land_m, land_c, out_b, land_b, z_sem, c_sem, b_sem)
    for slot in range(h_pos.shape[0]):
        build_y(h_pos.at[slot, 1], stage, y_two, slot)
    me = at.slot(0, 0, 0)
    own_i[...] = reduce_plane_end(at, conc_i, part_i, land_c, land_b, c_copies, b_copies)
    p_conc, p_near = share_plane(at, own_i, h_conc, p_conc, c_conc)
    own_m[...] = reduce_end(conc_m, part_m, at.a, land_m, z_copies)
    z_conc = share_along(at, own_m, g_conc, z_conc)
    g_conc[at.a] = own_m[...]
    h_conc[me] = own_i[...]
    fill_rows(g_conc, m_rows, at.a)
    fill_rows(h_conc, i_rows, me)
    pass_on(at, p_conc, p_near, h_conc, c_conc)
    take_plane(at, p_conc, p_near, h_conc, i_rows)
    take_along(at, z_conc, g_conc, m_rows)
    finish_sends(z_copies, c_copies, b_copies, z_conc, p_conc, p_near)


def last_reduce(n_mob, n_imm, part_m, part_i, conc_m, conc_i, own_m, own_i, land_m, land_c, out_b, land_b, *sems):
    at = Place(n_mob, n_imm)
    sem, peers = at.greet()
    pl.semaphore_wait(sem, peers)
    z_copies, c_copies, b_copies = reduce_start(
        at, part_m, part_i, land_m, land_c, out_b, land_b, sems[0:2], sems[2:4], sems[4:6])
    own_i[...] = reduce_plane_end(at, conc_i, part_i, land_c, land_b, c_copies, b_copies)
    own_m[...] = reduce_end(conc_m, part_m, at.a, land_m, z_copies)
    finish_sends(z_copies, c_copies, b_copies)


def pair_loop(pair_list, x_all, y_all, x_conc, y_conc, m_rows, i_rows, gain_m, gain_i,
              lst, p_even, p_odd, w_even, w_odd, sem):
    read = pltpu.make_async_copy(pair_list, lst, sem)
    read.start()
    gain_m[...] = jnp.zeros_like(gain_m)
    gain_i[...] = jnp.zeros_like(gain_i)
    read.wait()
    size = lst.shape[0] // 3 // 128 * 128
    used = lst[lst.shape[0] - 128]

    def entry(block, u):
        spot = block * UNROLL
        return lst[spot + u], lst[spot + (size + u)], lst[spot + (2 * size + u)]

    def measure(block, u, powers):
        m, i, k = entry(block, u)
        right = jnp.concatenate([y_all[i], y_all[k]], axis=1)
        powers[u] = jnp.dot(x_all[m][:, :TERMS], right, preferred_element_type=F32)

    def weigh(u, powers, weights):
        weights[u] = jnp.exp2(powers[u]).astype(BF16)

    def transfer(block, u, weights):
        m, i, k = entry(block, u)
        weight = weights[u]
        to_i = jnp.dot(m_rows[m], weight, preferred_element_type=F32)
        right = jnp.concatenate([i_rows[i], i_rows[k]], axis=1)
        to_m = lax.dot_general(right, weight, (((1,), (1,)), ((), ())), preferred_element_type=F32)
        return m, i, k, to_i, to_m

    def finish(m, i, k, to_i, to_m):
        gain_m[m] += to_m[0:8] + to_m[8:16] - to_m[16:24] * x_conc[m]
        gain_i[i] += to_i[0:8, :128] + to_i[8:16, :128] - to_i[16:24, :128] * y_conc[i]
        gain_i[k] += to_i[0:8, 128:] + to_i[8:16, 128:] - to_i[16:24, 128:] * y_conc[k]

    def step(block, first=None, second=None, third=None):
        moved = []
        for u in range(UNROLL):
            if second is not None:
                weigh(u, *second)
            if first is not None:
                measure(block, u, first)
            if third is not None:
                moved.append(transfer(block - 2, u, third))
        for item in moved:
            finish(*item)

    pairs = jnp.maximum(lax.div(used + (2 * UNROLL - 1), 2 * UNROLL), 1)
    step(0, p_even)
    step(1, p_odd, (p_even, w_even))

    def body(t, carry):
        step(2 * t, p_even, (p_odd, w_odd), w_even)
        step(2 * t + 1, p_odd, (p_even, w_even), w_odd)
        return carry

    lax.fori_loop(1, pairs, body, 0)
    step(2 * pairs, None, (p_odd, w_odd), w_even)
    step(2 * pairs + 1, None, None, w_odd)


def write_out(own_m, own_i, out_m, out_i, sems):
    copies = [
        pltpu.make_async_copy(src, dst, sems.at[j]) for j, (src, dst) in enumerate(((own_m, out_m), (own_i, out_i)))
    ]
    for copy in copies:
        copy.start()
    for copy in copies:
        copy.wait()


def on_device(n_mob, n_imm, mpos, walk, mconc, ipos, iconc, rows, cols, counts):
    nm, nb, na = sizes(n_mob, n_imm)
    mc, solutes, part = iconc.shape
    ic = mconc.shape[0]
    slots = nm * nb * 2
    cells_m, cells_i = na * mc, slots * ic
    tiles = nm * na
    chunks = tiles * 4
    lines = -(-(chunks * 64 + cells_m // 2 + 2 * UNROLL) // 128)
    list_rows = -(-(3 * lines + 1) // 8) * 8
    vmem = pl.BlockSpec(memory_space=pltpu.VMEM)
    anywhere = pl.BlockSpec(memory_space=pl.ANY)
    hbm = pl.BlockSpec(memory_space=pltpu.HBM)
    dma = pltpu.SemaphoreType.DMA

    def params(ident):
        return pltpu.CompilerParams(collective_id=ident, has_side_effects=True, vmem_limit_bytes=VMEM_LIMIT)

    def shape(dims, dtype=F32):
        return jax.ShapeDtypeStruct(dims, dtype)

    def pairs(*dims):
        return [dma(dims)] * 2

    cell_m, cell_i = (mc, solutes, part), (ic, solutes, part)
    all_m, all_i = (na,) + cell_m, (slots + 1,) + cell_i
    pos_m, pos_i = (3, mc, part), (3, ic, part)
    stage = pltpu.VMEM((max(mc, ic) * TERMS, part), F32)
    x_shape = shape((cells_m, part, 128), BF16)
    concs = (
        shape(all_m), shape(all_i),
        shape((cells_m, 4 * solutes, part), BF16), shape((cells_i + 16, 4 * solutes, part), BF16),
    )
    plane = (nm, nb)
    y_shape = shape((cells_i + 8, TERMS, part), BF16)
    *concs_one, x_all, y_one, pair_list, h_pos = pl.pallas_call(
        functools.partial(first_gather, n_mob, n_imm),
        out_shape=concs + (
            x_shape, y_shape, shape((list_rows, 128), jnp.int32), shape((slots, 2) + pos_i),
        ),
        in_specs=[hbm] * 8,
        out_specs=(vmem,) * 8,
        scratch_shapes=[
            pltpu.VMEM((na,) + pos_m, F32), pltpu.VMEM((tiles, 8, 128), jnp.int32),
            pltpu.VMEM(pos_i, F32), pltpu.VMEM((2,) + pos_i, F32), pltpu.VMEM(pos_m, F32),
            pltpu.VMEM(rows.shape, jnp.int32), pltpu.VMEM(cols.shape, jnp.int32), pltpu.VMEM((1, 1), jnp.int32),
            stage, pltpu.VMEM((chunks, 128), jnp.int32), pltpu.VMEM((chunks, 128), jnp.int32),
            pltpu.VMEM((chunks, 128), F32),
            dma((8,)), *pairs(na), *pairs(na), *pairs(*plane), *pairs(*plane), *pairs(*plane), *pairs(*plane),
            *pairs(nm, na),
        ],
        compiler_params=params(0),
    )(*[
        pltpu.with_memory_space_constraint(x, pltpu.HBM)
        for x in (jnp.transpose(mpos, (1, 0, 2)), jnp.transpose(walk, (0, 2, 1, 3)), mconc,
                  jnp.transpose(ipos, (1, 0, 2)), iconc, rows, cols)
    ], counts)
    flat_list = pair_list.reshape(-1)

    def gains(y_all, x_conc, y_conc, m_rows, i_rows):
        return pl.pallas_call(
            pair_loop,
            out_shape=(shape((cells_m, solutes, part)), shape((cells_i + 1, solutes, part))),
            in_specs=[anywhere] + [vmem] * 6,
            out_specs=(vmem,) * 2,
            scratch_shapes=[
                pltpu.SMEM((flat_list.shape[0],), jnp.int32),
                pltpu.VMEM((UNROLL, part, 256), F32), pltpu.VMEM((UNROLL, part, 256), F32),
                pltpu.VMEM((UNROLL, part, 256), BF16), pltpu.VMEM((UNROLL, part, 256), BF16),
                dma,
            ],
            compiler_params=pltpu.CompilerParams(vmem_limit_bytes=VMEM_LIMIT),
        )(flat_list, x_all, y_all, x_conc.reshape((cells_m, solutes, part)),
          y_conc.reshape((cells_i + ic, solutes, part)), m_rows, i_rows)

    lands = [pltpu.VMEM((na,) + cell_m, F32)] + [pltpu.VMEM(plane + cell_i, F32)] * 3
    own = (shape(cell_m), shape(cell_i))
    part_m, part_i = gains(y_one, *concs_one)
    own_m, own_i, *concs_two, y_two = pl.pallas_call(
        functools.partial(exchange, n_mob, n_imm),
        out_shape=own + concs + (y_shape,),
        in_specs=[vmem] * 5,
        out_specs=(vmem,) * 7,
        scratch_shapes=lands + [stage, *pairs(na), *pairs(*plane), *pairs(*plane),
                                *pairs(na), *pairs(*plane), *pairs(*plane)],
        compiler_params=params(1),
    )(part_m, part_i, iconc, mconc, h_pos)
    part_m, part_i = gains(y_two, *concs_two)
    own_m, own_i = pl.pallas_call(
        functools.partial(last_reduce, n_mob, n_imm),
        out_shape=own,
        in_specs=[vmem] * 4,
        out_specs=(vmem,) * 2,
        scratch_shapes=lands + [*pairs(na), *pairs(*plane), *pairs(*plane)],
        compiler_params=params(2),
    )(part_m, part_i, own_m, own_i)
    return pl.pallas_call(
        write_out,
        out_shape=own[::-1],
        in_specs=[vmem] * 2,
        out_specs=(anywhere,) * 2,
        scratch_shapes=[dma((2,))],
        compiler_params=pltpu.CompilerParams(vmem_limit_bytes=VMEM_LIMIT),
    )(own_i, own_m)


def solution(mesh):
    return jax.shard_map(
        functools.partial(on_device, mesh.shape["mob"], mesh.shape["imm"]),
        mesh=mesh,
        in_specs=(
            P(("mob", "imm"), None, None),
            P(None, ("mob", "imm"), None, None),
            P(("mob", "imm"), None, None),
            P(("mob", "imm"), None, None),
            P(("mob", "imm"), None, None),
            P("mob", "imm", None),
            P("mob", "imm", None),
            P("mob", "imm"),
        ),
        out_specs=(P(("mob", "imm"), None, None), P(("mob", "imm"), None, None)),
        check_vma=False,
    )
```

```python
import functools
import math

import jax
import jax.numpy as jnp
from jax import lax
from jax.experimental import pallas as pl
from jax.experimental.pallas import tpu as pltpu
from jax.sharding import PartitionSpec as P

RATE = 1.0 / 512.0
SCALE = math.sqrt(0.5 * math.log2(math.e))
CENTRE = 2.0
FAR = -30000.0
MESH = pl.DeviceIdType.MESH
VMEM_LIMIT = 20 * 1024 * 1024
UNROLL = 12
TERMS = 16
F32 = jnp.float32
BF16 = jnp.bfloat16


def sizes(n_mob, n_imm):
    rest = n_imm // 2
    nb = 1
    while nb * nb * 4 <= rest:
        nb *= 2
    return n_mob, nb, rest // nb


class Place:
    def __init__(self, n_mob, n_imm):
        self.nm, self.nb, self.na = sizes(n_mob, n_imm)
        self.p = lax.axis_index("mob")
        q = lax.axis_index("imm")
        self.core = lax.rem(q, 2)
        chip = lax.div(q, 2)
        self.b = lax.rem(chip, self.nb)
        self.a = lax.div(chip, self.nb)

    def am(self, d):
        return lax.rem(self.a + (d + self.na), self.na)

    def bm(self, d):
        return lax.rem(self.b + (d + self.nb), self.nb)

    def pm(self, d):
        return lax.rem(self.p + (d + self.nm), self.nm)

    def dev(self, p, a, b, core):
        return (p, (a * self.nb + b) * 2 + core)

    def along(self, da):
        return self.dev(self.p, self.am(da), self.b, self.core)

    def other(self, dc):
        return 1 - self.core if dc else self.core

    def across(self, dp, db, dc):
        return self.dev(self.pm(dp), self.a, self.bm(db), self.other(dc))

    def plane(self):
        keys = [(dp, db) for dp in range(self.nm) for db in range(self.nb)]
        return sorted((key for key in keys if any(key)), key=lambda key: -bool(key[0]) - bool(key[1]))

    def mates(self):
        return [(dp, da) for dp in range(self.nm) for da in range(self.na) if dp or da]

    def mate(self, dp, da):
        return self.dev(self.pm(dp), self.am(da), self.b, self.core)

    def slot(self, dp, db, dc):
        return (self.pm(dp) * self.nb + self.bm(db)) * 2 + self.other(dc)

    def greet(self, lists=False):
        sem = pltpu.get_barrier_semaphore()
        peers = [self.along(d) for d in range(1, self.na)] + [self.across(0, 0, 1)]
        peers += [self.across(dp, db, 0) for dp, db in self.plane()]
        if lists:
            peers += [self.mate(dp, da) for dp, da in self.mates() if dp and da]
        for peer in peers:
            pl.semaphore_signal(sem, inc=1, device_id=peer, device_id_type=MESH)
        return sem, len(peers)


def remote(src, dst, sems, index, device):
    copy = pltpu.make_async_remote_copy(
        src_ref=src, dst_ref=dst, send_sem=sems[0].at[index], recv_sem=sems[1].at[index],
        device_id=device, device_id_type=MESH,
    )
    copy.start()
    return copy


def split2(x):
    high = x.astype(BF16).astype(F32)
    return high, x - high


def split3(x):
    high, rest = split2(x)
    mid, low = split2(rest)
    return high, mid, low


def rows_x(x):
    (xh, xm), (yh, ym), (zh, zm) = [split2(x[j]) for j in range(3)]
    norm = split3(-(x[0] * x[0] + x[1] * x[1] + x[2] * x[2]))
    one = jnp.ones_like(x[0])
    return [xh, yh, zh, xh, yh, zh, xm, ym, zm, *norm, one, one, one, jnp.zeros_like(one)]


def rows_y(y):
    (xh, xm), (yh, ym), (zh, zm) = [split2(2.0 * y[j]) for j in range(3)]
    norm = split3(-(y[0] * y[0] + y[1] * y[1] + y[2] * y[2]))
    one = jnp.ones_like(y[0])
    return [xh, yh, zh, xm, ym, zm, xh, yh, zh, one, one, one, *norm, jnp.zeros_like(one)]


def fill(stage, rows):
    cells = rows[0].shape[0]
    for j, row in enumerate(rows):
        stage[pl.ds(j, cells, stride=TERMS), :] = row


def build_y(pos, stage, out, slot):
    cells = pos.shape[1]
    fill(stage, rows_y([pos[j] for j in range(3)]))
    out[pl.ds(slot * cells, cells)] = stage[...].reshape(cells, TERMS, 128).astype(BF16)


def build_x(pos, stage, out, slot):
    cells = pos.shape[1]
    fill(stage, rows_x([pos[j] for j in range(3)]))
    for group in range(0, cells, 128 // TERMS):
        block = stage[group * TERMS : group * TERMS + 128, :].T.astype(BF16)
        for j in range(128 // TERMS):
            out[slot * cells + group + j, :, :TERMS] = block[:, j * TERMS : (j + 1) * TERMS]


def count_list(at, mc, ic, lists, keep_m, keep_i, keep_rank, first, last, total):
    lists_n = lists.shape[0]
    cells_m = at.na * mc
    shift_m, shift_i, shift_b = [int(math.log2(n)) for n in (mc, ic, at.nb)]
    mine = lax.broadcasted_iota(jnp.int32, (cells_m, 128), 0)
    column = lax.broadcasted_iota(jnp.int32, (128, 256), 1)
    upper = jnp.where(
        (lax.broadcasted_iota(jnp.int32, (128, 256), 0) <= column) | (column >= 128), 1.0, 0.0
    ).astype(BF16)
    home = at.p * at.na + at.a

    def count(chunk, total):
        which, part = lax.rem(lax.div(chunk, 4) + home, lists_n), lax.rem(chunk, 4)
        r = lists[which, pl.ds(part, 1), :]
        c = lists[which, pl.ds(4 + part, 1), :]
        owner = jnp.right_shift(r, shift_i)
        ok = (
            (r >= 0)
            & (jnp.right_shift(owner, 1 + shift_b) == at.a)
            & (jnp.right_shift(c, shift_m) == at.p)
        )
        m = lax.rem(which, at.na) * mc + jnp.bitwise_and(c, mc - 1)
        m = jnp.where(ok, m, -1)
        spot = lax.div(which, at.na) * (at.nb * 2) + jnp.bitwise_and(owner, at.nb * 2 - 1)
        i = spot * ic + jnp.bitwise_and(r, ic - 1)
        hot = jnp.where(mine == m, 1.0, 0.0).astype(F32)
        rank = jnp.dot(hot.astype(BF16), upper, preferred_element_type=F32)
        keep_m[pl.ds(chunk, 1), :] = m
        keep_i[pl.ds(chunk, 1), :] = i + 1
        keep_rank[pl.ds(chunk, 1), :] = jnp.sum(hot * (rank[:, :128] + total), axis=0, keepdims=True) - 1.0
        return total + rank[:, 128:]

    return lax.fori_loop(first, last, count, total, unroll=7)


def place_list(at, mc, ic, lists, keep_m, keep_i, keep_rank, total, out):
    lists_n, chunks = lists.shape[0], lists.shape[0] * 4
    cells_m = at.na * mc
    lines = -(-(out.shape[0] // 3) // 8) * 8
    dummy = at.nm * at.nb * 2 * ic
    wide = dummy > 255
    groups = 5 if wide else 3
    mine = lax.broadcasted_iota(jnp.int32, (cells_m, 128), 0)
    lower = jnp.where(
        lax.broadcasted_iota(jnp.int32, (cells_m, cells_m), 0)
        > lax.broadcasted_iota(jnp.int32, (cells_m, cells_m), 1), 1.0, 0.0
    ).astype(F32)
    even = 2.0 * jnp.floor((total + 1.0) * 0.5)
    start = jnp.dot(lower, even, preferred_element_type=F32, precision=lax.Precision.HIGHEST)
    doubles = jnp.sum(even, axis=0, keepdims=True) * 0.5
    line = lax.broadcasted_iota(jnp.int32, (lines, 128), 0)
    column = lax.broadcasted_iota(jnp.int32, (128, 128), 0)

    def place(chunk, acc):
        m = keep_m[pl.ds(chunk, 1), :]
        i = keep_i[pl.ds(chunk, 1), :]
        hot = jnp.where(mine == m, 1.0, 0.0).astype(F32)
        spot = jnp.sum(hot * start, axis=0, keepdims=True) + keep_rank[pl.ds(chunk, 1), :]
        spot = jnp.where(m >= 0, spot.astype(jnp.int32), -1)
        double = jnp.right_shift(spot, 1)
        second = jnp.bitwise_and(spot, 1) == 1
        here = (line == jnp.right_shift(double, 7)) & (m >= 0)
        lane_hot = jnp.where(column == jnp.bitwise_and(double, 127), 1.0, 0.0).astype(BF16)
        zero = jnp.zeros((1, 128), F32)
        parts = [jnp.bitwise_and(i, 63), jnp.right_shift(i, 6)] if wide else [i]
        parts = [x.astype(F32) for x in parts]
        values = [jnp.where(second, zero, m.astype(F32))]
        values += [jnp.where(second, zero, x) for x in parts] + [jnp.where(second, x, zero) for x in parts]
        left = jnp.concatenate([jnp.where(here, v, 0.0) for v in values], axis=0).astype(BF16)
        return acc + lax.dot_general(left, lane_hot, (((1,), (1,)), ((), ())), preferred_element_type=F32)

    acc = lax.fori_loop(0, chunks, place, jnp.zeros((groups * lines, 128), F32), unroll=8)
    found = [acc[j * lines : (j + 1) * lines].astype(jnp.int32) for j in range(groups)]
    size = out.shape[0] // 3
    out[0:size, :] = found[0][0:size]
    for j in range(2):
        i = found[1 + 2 * j] + 64 * found[2 + 2 * j] if wide else found[1 + j]
        out[(j + 1) * size : (j + 2) * size, :] = jnp.where(i == 0, dummy, i - 1)[0:size]
    out[out.shape[0] - 1 :, :] = doubles.astype(jnp.int32)


def conc_rows(conc):
    conc = conc * RATE
    high = conc.astype(BF16).astype(F32)
    ones = jnp.full_like(conc, RATE)
    return jnp.concatenate([high, conc - high, ones, ones], axis=1).astype(BF16)


def fill_rows(conc, rows, slot):
    cells = conc.shape[1]
    rows[pl.ds(slot * cells, cells)] = conc_rows(conc[slot])


def share_plane(at, src, dst, sems, pass_sems):
    me = at.slot(0, 0, 0)
    copies = {
        (dp, db): remote(src, dst.at[me], sems, (dp, db), at.across(dp, db, 0)) for dp, db in at.plane()
    }
    return copies, {(0, 0): remote(src, dst.at[me], pass_sems, (0, 0), at.across(0, 0, 1))}


def pass_on(at, copies, passed, dst, pass_sems):
    for (dp, db), copy in copies.items():
        copy.wait_recv()
        block = dst.at[at.slot(-dp, -db, 0)]
        passed[dp, db] = remote(block, block, pass_sems, (dp, db), at.across(0, 0, 1))


def share_along(at, src, dst, sems):
    return {da: remote(src, dst.at[at.a], sems, da, at.along(da)) for da in range(1, at.na)}


def take_plane(at, copies, passed, conc, rows):
    for dp, db in copies:
        fill_rows(conc, rows, at.slot(-dp, -db, 0))
    for (dp, db), copy in passed.items():
        copy.wait_recv()
        fill_rows(conc, rows, at.slot(-dp, -db, 1))


def take_along(at, copies, conc, rows):
    for da, copy in copies.items():
        copy.wait_recv()
        fill_rows(conc, rows, at.am(-da))


def finish_sends(*groups):
    for group in groups:
        for copy in group.values():
            copy.wait_send()


def first_gather(n_mob, n_imm, mpos, walk, mconc, ipos, iconc, rows, cols, count,
                 g_conc, h_conc, m_rows, i_rows, x_all, y_one, pair_list, h_pos,
                 g_pos, lists, in_m, in_w, in_i, in_r, in_c, in_n, stage, keep_m, keep_i, keep_rank, *sems):
    at = Place(n_mob, n_imm)
    local = sems[0]
    z_pos, z_conc, p_pos, p_conc, c_pos, c_conc, l_sem = [sems[j : j + 2] for j in range(1, 15, 2)]
    me = at.slot(0, 0, 0)
    reads = [
        pltpu.make_async_copy(src, dst, local.at[j])
        for j, (src, dst) in enumerate((
            (mpos, in_m), (walk, in_w), (ipos, in_i), (rows, in_r), (cols, in_c), (count, in_n),
            (iconc, g_conc.at[at.a]), (mconc, h_conc.at[me]),
        ))
    ]
    for read in reads:
        read.start()
    sem, peers = at.greet(lists=True)
    clear_spare(h_conc, i_rows, y_one)
    reads[0].wait()
    reads[1].wait()
    moved = in_m[...] + in_w[0]
    h_pos[me, 0] = (moved - CENTRE) * SCALE
    h_pos[me, 1] = ((moved + in_w[1]) - CENTRE) * SCALE
    reads[2].wait()
    g_pos[at.a] = (in_i[...] - CENTRE) * SCALE
    for read in reads[3:6]:
        read.wait()
    home = at.p * at.na + at.a
    lane = lax.broadcasted_iota(jnp.int32, (1, 128), 1)
    for j in range(4):
        r = in_r[0, :, j * 128 : (j + 1) * 128]
        lists[home, j : j + 1, :] = jnp.where(j * 128 + lane < in_n[...], r, -1)
        lists[home, 4 + j : 5 + j, :] = in_c[0, :, j * 128 : (j + 1) * 128]
    build_x(g_pos.at[at.a], stage, x_all, at.a)
    build_y(h_pos.at[me, 0], stage, y_one, me)
    for read in reads[6:]:
        read.wait()
    fill_rows(g_conc, m_rows, at.a)
    fill_rows(h_conc, i_rows, me)
    mc, ic = iconc.shape[0], mconc.shape[0]
    total = count_list(at, mc, ic, lists, keep_m, keep_i, keep_rank, 0, 4, jnp.zeros((at.na * mc, 128), F32))
    pl.semaphore_wait(sem, peers)
    shared = {
        (dp, da): remote(lists.at[home], lists.at[home], l_sem, (dp, da), at.mate(dp, da)) for dp, da in at.mates()
    }
    z_far = share_along(at, g_pos.at[at.a], g_pos, z_pos)
    z_conc = share_along(at, g_conc.at[at.a], g_conc, z_conc)
    p_far, p_near = share_plane(at, h_pos.at[me], h_pos, p_pos, c_pos)
    p_conc, p_near_conc = share_plane(at, h_conc.at[me], h_conc, p_conc, c_conc)
    for copy in shared.values():
        copy.wait_recv()
    total = count_list(at, mc, ic, lists, keep_m, keep_i, keep_rank, 4, lists.shape[0] * 4, total)
    pass_on(at, p_far, p_near, h_pos, c_pos)
    place_list(at, mc, ic, lists, keep_m, keep_i, keep_rank, total, pair_list)
    pass_on(at, p_conc, p_near_conc, h_conc, c_conc)
    for dp, db in p_far:
        here = at.slot(-dp, -db, 0)
        build_y(h_pos.at[here, 0], stage, y_one, here)
    for (dp, db), copy in p_near.items():
        copy.wait_recv()
        here = at.slot(-dp, -db, 1)
        build_y(h_pos.at[here, 0], stage, y_one, here)
    for da, copy in z_far.items():
        copy.wait_recv()
        build_x(g_pos.at[at.am(-da)], stage, x_all, at.am(-da))
    take_plane(at, p_conc, p_near_conc, h_conc, i_rows)
    take_along(at, z_conc, g_conc, m_rows)
    finish_sends(z_far, z_conc, shared, p_far, p_near, p_conc, p_near_conc)


def clear_spare(h_conc, i_rows, y_all):
    h_conc[h_conc.shape[0] - 1] = jnp.zeros(h_conc.shape[1:], F32)
    i_rows[i_rows.shape[0] - 16 :] = jnp.zeros((16,) + i_rows.shape[1:], BF16)
    row = lax.broadcasted_iota(jnp.int32, (8, TERMS, 128), 1)
    y_all[y_all.shape[0] - 8 :] = jnp.where(row == 12, FAR, 0.0).astype(BF16)


def reduce_start(at, part_m, part_i, land_m, land_c, out_b, land_b, z_sem, c_sem, b_sem):
    mc, ic = land_m.shape[1], land_c.shape[2]
    c_copies = {
        (dp, db): remote(
            part_i.at[pl.ds(at.slot(dp, db, 1) * ic, ic)], land_c.at[dp, db], c_sem, (dp, db), at.across(0, 0, 1))
        for dp, db in at.plane() + [(0, 0)]
    }
    z_copies = {
        da: remote(part_m.at[pl.ds(at.am(da) * mc, mc)], land_m.at[da], z_sem, da, at.along(da))
        for da in range(1, at.na)
    }
    b_copies = {}
    for dp, db in at.plane():
        c_copies[dp, db].wait_recv()
        out_b[dp, db] = part_i[pl.ds(at.slot(dp, db, 0) * ic, ic)] + land_c[dp, db]
        b_copies[dp, db] = remote(out_b.at[dp, db], land_b.at[dp, db], b_sem, (dp, db), at.across(dp, db, 0))
    return z_copies, c_copies, b_copies


def reduce_end(base, part, slot, land, copies):
    cells = base.shape[0]
    total = base[...] + part[pl.ds(slot * cells, cells)]
    for key, copy in copies.items():
        copy.wait_recv()
        total = total + land[key]
    return total


def reduce_plane_end(at, base, part, land_c, land_b, c_copies, b_copies):
    c_copies[0, 0].wait_recv()
    return reduce_end(base, part, at.slot(0, 0, 0), land_b, b_copies) + land_c[0, 0]


def exchange(n_mob, n_imm, part_m, part_i, conc_m, conc_i, h_pos, own_m, own_i, g_conc, h_conc, m_rows, i_rows,
             y_two, land_m, land_c, out_b, land_b, stage, *sems):
    at = Place(n_mob, n_imm)
    z_sem, c_sem, b_sem, z_conc, p_conc, c_conc = [sems[j : j + 2] for j in range(0, 12, 2)]
    sem, peers = at.greet()
    clear_spare(h_conc, i_rows, y_two)
    pl.semaphore_wait(sem, peers)
    z_copies, c_copies, b_copies = reduce_start(
        at, part_m, part_i, land_m, land_c, out_b, land_b, z_sem, c_sem, b_sem)
    for slot in range(h_pos.shape[0]):
        build_y(h_pos.at[slot, 1], stage, y_two, slot)
    me = at.slot(0, 0, 0)
    own_i[...] = reduce_plane_end(at, conc_i, part_i, land_c, land_b, c_copies, b_copies)
    p_conc, p_near = share_plane(at, own_i, h_conc, p_conc, c_conc)
    own_m[...] = reduce_end(conc_m, part_m, at.a, land_m, z_copies)
    z_conc = share_along(at, own_m, g_conc, z_conc)
    g_conc[at.a] = own_m[...]
    h_conc[me] = own_i[...]
    fill_rows(g_conc, m_rows, at.a)
    fill_rows(h_conc, i_rows, me)
    pass_on(at, p_conc, p_near, h_conc, c_conc)
    take_plane(at, p_conc, p_near, h_conc, i_rows)
    take_along(at, z_conc, g_conc, m_rows)
    finish_sends(z_copies, c_copies, b_copies, z_conc, p_conc, p_near)


def last_reduce(n_mob, n_imm, part_m, part_i, conc_m, conc_i, own_m, own_i, land_m, land_c, out_b, land_b, *sems):
    at = Place(n_mob, n_imm)
    sem, peers = at.greet()
    pl.semaphore_wait(sem, peers)
    z_copies, c_copies, b_copies = reduce_start(
        at, part_m, part_i, land_m, land_c, out_b, land_b, sems[0:2], sems[2:4], sems[4:6])
    own_i[...] = reduce_plane_end(at, conc_i, part_i, land_c, land_b, c_copies, b_copies)
    own_m[...] = reduce_end(conc_m, part_m, at.a, land_m, z_copies)
    finish_sends(z_copies, c_copies, b_copies)


def pair_loop(pair_list, x_all, y_all, x_conc, y_conc, m_rows, i_rows, gain_m, gain_i,
              lst, p_even, p_odd, w_even, w_odd, sem):
    read = pltpu.make_async_copy(pair_list, lst, sem)
    read.start()
    gain_m[...] = jnp.zeros_like(gain_m)
    gain_i[...] = jnp.zeros_like(gain_i)
    read.wait()
    size = lst.shape[0] // 3 // 128 * 128
    used = lst[lst.shape[0] - 128]

    def entry(block, u):
        spot = block * UNROLL
        return lst[spot + u], lst[spot + (size + u)], lst[spot + (2 * size + u)]

    def measure(block, u, powers):
        m, i, k = entry(block, u)
        right = jnp.concatenate([y_all[i], y_all[k]], axis=1)
        powers[u] = jnp.dot(x_all[m][:, :TERMS], right, preferred_element_type=F32)

    def weigh(u, powers, weights):
        weights[u] = jnp.exp2(powers[u]).astype(BF16)

    def transfer(block, u, weights):
        m, i, k = entry(block, u)
        weight = weights[u]
        to_i = jnp.dot(m_rows[m], weight, preferred_element_type=F32)
        right = jnp.concatenate([i_rows[i], i_rows[k]], axis=1)
        to_m = lax.dot_general(right, weight, (((1,), (1,)), ((), ())), preferred_element_type=F32)
        return m, i, k, to_i, to_m

    def finish(m, i, k, to_i, to_m):
        gain_m[m] += to_m[0:8] + to_m[8:16] - to_m[16:24] * x_conc[m]
        gain_i[i] += to_i[0:8, :128] + to_i[8:16, :128] - to_i[16:24, :128] * y_conc[i]
        gain_i[k] += to_i[0:8, 128:] + to_i[8:16, 128:] - to_i[16:24, 128:] * y_conc[k]

    def step(block, first=None, second=None, third=None):
        moved = []
        for u in range(UNROLL):
            if second is not None:
                weigh(u, *second)
            if first is not None:
                measure(block, u, first)
            if third is not None:
                moved.append(transfer(block - 2, u, third))
        for item in moved:
            finish(*item)

    pairs = jnp.maximum(lax.div(used + (2 * UNROLL - 1), 2 * UNROLL), 1)
    step(0, p_even)
    step(1, p_odd, (p_even, w_even))

    def body(t, carry):
        step(2 * t, p_even, (p_odd, w_odd), w_even)
        step(2 * t + 1, p_odd, (p_even, w_even), w_odd)
        return carry

    lax.fori_loop(1, pairs, body, 0)
    step(2 * pairs, None, (p_odd, w_odd), w_even)
    step(2 * pairs + 1, None, None, w_odd)


def write_out(own_m, own_i, out_m, out_i, sems):
    copies = [
        pltpu.make_async_copy(src, dst, sems.at[j]) for j, (src, dst) in enumerate(((own_m, out_m), (own_i, out_i)))
    ]
    for copy in copies:
        copy.start()
    for copy in copies:
        copy.wait()


def on_device(n_mob, n_imm, mpos, walk, mconc, ipos, iconc, rows, cols, counts):
    nm, nb, na = sizes(n_mob, n_imm)
    mc, solutes, part = iconc.shape
    ic = mconc.shape[0]
    slots = nm * nb * 2
    cells_m, cells_i = na * mc, slots * ic
    tiles = nm * na
    chunks = tiles * 4
    lines = -(-(chunks * 64 + cells_m // 2 + 2 * UNROLL) // 128)
    list_rows = -(-(3 * lines + 1) // 8) * 8
    vmem = pl.BlockSpec(memory_space=pltpu.VMEM)
    anywhere = pl.BlockSpec(memory_space=pl.ANY)
    hbm = pl.BlockSpec(memory_space=pltpu.HBM)
    dma = pltpu.SemaphoreType.DMA

    def params(ident):
        return pltpu.CompilerParams(collective_id=ident, has_side_effects=True, vmem_limit_bytes=VMEM_LIMIT)

    def shape(dims, dtype=F32):
        return jax.ShapeDtypeStruct(dims, dtype)

    def pairs(*dims):
        return [dma(dims)] * 2

    cell_m, cell_i = (mc, solutes, part), (ic, solutes, part)
    all_m, all_i = (na,) + cell_m, (slots + 1,) + cell_i
    pos_m, pos_i = (3, mc, part), (3, ic, part)
    stage = pltpu.VMEM((max(mc, ic) * TERMS, part), F32)
    x_shape = shape((cells_m, part, 128), BF16)
    concs = (
        shape(all_m), shape(all_i),
        shape((cells_m, 4 * solutes, part), BF16), shape((cells_i + 16, 4 * solutes, part), BF16),
    )
    plane = (nm, nb)
    y_shape = shape((cells_i + 8, TERMS, part), BF16)
    *concs_one, x_all, y_one, pair_list, h_pos = pl.pallas_call(
        functools.partial(first_gather, n_mob, n_imm),
        out_shape=concs + (
            x_shape, y_shape, shape((list_rows, 128), jnp.int32), shape((slots, 2) + pos_i),
        ),
        in_specs=[hbm] * 8,
        out_specs=(vmem,) * 8,
        scratch_shapes=[
            pltpu.VMEM((na,) + pos_m, F32), pltpu.VMEM((tiles, 8, 128), jnp.int32),
            pltpu.VMEM(pos_i, F32), pltpu.VMEM((2,) + pos_i, F32), pltpu.VMEM(pos_m, F32),
            pltpu.VMEM(rows.shape, jnp.int32), pltpu.VMEM(cols.shape, jnp.int32), pltpu.VMEM((1, 1), jnp.int32),
            stage, pltpu.VMEM((chunks, 128), jnp.int32), pltpu.VMEM((chunks, 128), jnp.int32),
            pltpu.VMEM((chunks, 128), F32),
            dma((8,)), *pairs(na), *pairs(na), *pairs(*plane), *pairs(*plane), *pairs(*plane), *pairs(*plane),
            *pairs(nm, na),
        ],
        compiler_params=params(0),
    )(*[
        pltpu.with_memory_space_constraint(x, pltpu.HBM)
        for x in (jnp.transpose(mpos, (1, 0, 2)), jnp.transpose(walk, (0, 2, 1, 3)), mconc,
                  jnp.transpose(ipos, (1, 0, 2)), iconc, rows, cols)
    ], counts)
    flat_list = pair_list.reshape(-1)

    def gains(y_all, x_conc, y_conc, m_rows, i_rows):
        return pl.pallas_call(
            pair_loop,
            out_shape=(shape((cells_m, solutes, part)), shape((cells_i + 1, solutes, part))),
            in_specs=[anywhere] + [vmem] * 6,
            out_specs=(vmem,) * 2,
            scratch_shapes=[
                pltpu.SMEM((flat_list.shape[0],), jnp.int32),
                pltpu.VMEM((UNROLL, part, 256), F32), pltpu.VMEM((UNROLL, part, 256), F32),
                pltpu.VMEM((UNROLL, part, 256), BF16), pltpu.VMEM((UNROLL, part, 256), BF16),
                dma,
            ],
            compiler_params=pltpu.CompilerParams(vmem_limit_bytes=VMEM_LIMIT),
        )(flat_list, x_all, y_all, x_conc.reshape((cells_m, solutes, part)),
          y_conc.reshape((cells_i + ic, solutes, part)), m_rows, i_rows)

    lands = [pltpu.VMEM((na,) + cell_m, F32)] + [pltpu.VMEM(plane + cell_i, F32)] * 3
    own = (shape(cell_m), shape(cell_i))
    part_m, part_i = gains(y_one, *concs_one)
    own_m, own_i, *concs_two, y_two = pl.pallas_call(
        functools.partial(exchange, n_mob, n_imm),
        out_shape=own + concs + (y_shape,),
        in_specs=[vmem] * 5,
        out_specs=(vmem,) * 7,
        scratch_shapes=lands + [stage, *pairs(na), *pairs(*plane), *pairs(*plane),
                                *pairs(na), *pairs(*plane), *pairs(*plane)],
        compiler_params=params(1),
    )(part_m, part_i, iconc, mconc, h_pos)
    part_m, part_i = gains(y_two, *concs_two)
    own_m, own_i = pl.pallas_call(
        functools.partial(last_reduce, n_mob, n_imm),
        out_shape=own,
        in_specs=[vmem] * 4,
        out_specs=(vmem,) * 2,
        scratch_shapes=lands + [*pairs(na), *pairs(*plane), *pairs(*plane)],
        compiler_params=params(2),
    )(part_m, part_i, own_m, own_i)
    return pl.pallas_call(
        write_out,
        out_shape=own[::-1],
        in_specs=[vmem] * 2,
        out_specs=(anywhere,) * 2,
        scratch_shapes=[dma((2,))],
        compiler_params=pltpu.CompilerParams(vmem_limit_bytes=VMEM_LIMIT),
    )(own_i, own_m)


def solution(mesh):
    return jax.shard_map(
        functools.partial(on_device, mesh.shape["mob"], mesh.shape["imm"]),
        mesh=mesh,
        in_specs=(
            P(("mob", "imm"), None, None),
            P(None, ("mob", "imm"), None, None),
            P(("mob", "imm"), None, None),
            P(("mob", "imm"), None, None),
            P(("mob", "imm"), None, None),
            P("mob", "imm", None),
            P("mob", "imm", None),
            P("mob", "imm"),
        ),
        out_specs=(P(("mob", "imm"), None, None), P(("mob", "imm"), None, None)),
        check_vma=False,
    )
```

```python
import functools
import math

import jax
import jax.numpy as jnp
from jax import lax
from jax.experimental import pallas as pl
from jax.experimental.pallas import tpu as pltpu
from jax.sharding import PartitionSpec as P

RATE = 1.0 / 512.0
SCALE = math.sqrt(0.5 * math.log2(math.e))
CENTRE = 2.0
FAR = -30000.0
MESH = pl.DeviceIdType.MESH
VMEM_LIMIT = 20 * 1024 * 1024
UNROLL = 16
TERMS = 16
F32 = jnp.float32
BF16 = jnp.bfloat16


def sizes(n_mob, n_imm):
    rest = n_imm // 2
    nb = 1
    while nb * nb * 4 <= rest:
        nb *= 2
    return n_mob, nb, rest // nb


class Place:
    def __init__(self, n_mob, n_imm):
        self.nm, self.nb, self.na = sizes(n_mob, n_imm)
        self.p = lax.axis_index("mob")
        q = lax.axis_index("imm")
        self.core = lax.rem(q, 2)
        chip = lax.div(q, 2)
        self.b = lax.rem(chip, self.nb)
        self.a = lax.div(chip, self.nb)

    def am(self, d):
        return lax.rem(self.a + (d + self.na), self.na)

    def bm(self, d):
        return lax.rem(self.b + (d + self.nb), self.nb)

    def pm(self, d):
        return lax.rem(self.p + (d + self.nm), self.nm)

    def dev(self, p, a, b, core):
        return (p, (a * self.nb + b) * 2 + core)

    def along(self, da):
        return self.dev(self.p, self.am(da), self.b, self.core)

    def other(self, dc):
        return 1 - self.core if dc else self.core

    def across(self, dp, db, dc):
        return self.dev(self.pm(dp), self.a, self.bm(db), self.other(dc))

    def plane(self):
        keys = [(dp, db) for dp in range(self.nm) for db in range(self.nb)]
        return sorted((key for key in keys if any(key)), key=lambda key: -bool(key[0]) - bool(key[1]))

    def mates(self):
        return [(dp, da) for dp in range(self.nm) for da in range(self.na) if dp or da]

    def mate(self, dp, da):
        return self.dev(self.pm(dp), self.am(da), self.b, self.core)

    def slot(self, dp, db, dc):
        return (self.pm(dp) * self.nb + self.bm(db)) * 2 + self.other(dc)

    def greet(self, lists=False):
        sem = pltpu.get_barrier_semaphore()
        peers = [self.along(d) for d in range(1, self.na)] + [self.across(0, 0, 1)]
        peers += [self.across(dp, db, 0) for dp, db in self.plane()]
        if lists:
            peers += [self.mate(dp, da) for dp, da in self.mates() if dp and da]
        for peer in peers:
            pl.semaphore_signal(sem, inc=1, device_id=peer, device_id_type=MESH)
        return sem, len(peers)


def remote(src, dst, sems, index, device):
    copy = pltpu.make_async_remote_copy(
        src_ref=src, dst_ref=dst, send_sem=sems[0].at[index], recv_sem=sems[1].at[index],
        device_id=device, device_id_type=MESH,
    )
    copy.start()
    return copy


def split2(x):
    high = x.astype(BF16).astype(F32)
    return high, x - high


def split3(x):
    high, rest = split2(x)
    mid, low = split2(rest)
    return high, mid, low


def rows_x(x):
    (xh, xm), (yh, ym), (zh, zm) = [split2(x[j]) for j in range(3)]
    norm = split3(-(x[0] * x[0] + x[1] * x[1] + x[2] * x[2]))
    one = jnp.ones_like(x[0])
    return [xh, yh, zh, xh, yh, zh, xm, ym, zm, *norm, one, one, one, jnp.zeros_like(one)]


def rows_y(y):
    (xh, xm), (yh, ym), (zh, zm) = [split2(2.0 * y[j]) for j in range(3)]
    norm = split3(-(y[0] * y[0] + y[1] * y[1] + y[2] * y[2]))
    one = jnp.ones_like(y[0])
    return [xh, yh, zh, xm, ym, zm, xh, yh, zh, one, one, one, *norm, jnp.zeros_like(one)]


def fill(stage, rows):
    cells = rows[0].shape[0]
    for j, row in enumerate(rows):
        stage[pl.ds(j, cells, stride=TERMS), :] = row


def build_y(pos, stage, out, slot):
    cells = pos.shape[1]
    fill(stage, rows_y([pos[j] for j in range(3)]))
    out[pl.ds(slot * cells, cells)] = stage[...].reshape(cells, TERMS, 128).astype(BF16)


def build_x(pos, stage, out, slot):
    cells = pos.shape[1]
    fill(stage, rows_x([pos[j] for j in range(3)]))
    for group in range(0, cells, 128 // TERMS):
        block = stage[group * TERMS : group * TERMS + 128, :].T.astype(BF16)
        for j in range(128 // TERMS):
            out[slot * cells + group + j, :, :TERMS] = block[:, j * TERMS : (j + 1) * TERMS]


def count_list(at, mc, ic, lists, keep_m, keep_i, keep_rank, first, last, total):
    lists_n = lists.shape[0]
    cells_m = at.na * mc
    shift_m, shift_i, shift_b = [int(math.log2(n)) for n in (mc, ic, at.nb)]
    mine = lax.broadcasted_iota(jnp.int32, (cells_m, 128), 0)
    column = lax.broadcasted_iota(jnp.int32, (128, 256), 1)
    upper = jnp.where(
        (lax.broadcasted_iota(jnp.int32, (128, 256), 0) <= column) | (column >= 128), 1.0, 0.0
    ).astype(BF16)
    home = at.p * at.na + at.a

    def count(chunk, total):
        which, part = lax.rem(lax.div(chunk, 4) + home, lists_n), lax.rem(chunk, 4)
        r = lists[which, pl.ds(part, 1), :]
        c = lists[which, pl.ds(4 + part, 1), :]
        owner = jnp.right_shift(r, shift_i)
        ok = (
            (r >= 0)
            & (jnp.right_shift(owner, 1 + shift_b) == at.a)
            & (jnp.right_shift(c, shift_m) == at.p)
        )
        m = lax.rem(which, at.na) * mc + jnp.bitwise_and(c, mc - 1)
        m = jnp.where(ok, m, -1)
        spot = lax.div(which, at.na) * (at.nb * 2) + jnp.bitwise_and(owner, at.nb * 2 - 1)
        i = spot * ic + jnp.bitwise_and(r, ic - 1)
        hot = jnp.where(mine == m, 1.0, 0.0).astype(F32)
        rank = jnp.dot(hot.astype(BF16), upper, preferred_element_type=F32)
        keep_m[pl.ds(chunk, 1), :] = m
        keep_i[pl.ds(chunk, 1), :] = i + 1
        keep_rank[pl.ds(chunk, 1), :] = jnp.sum(hot * (rank[:, :128] + total), axis=0, keepdims=True) - 1.0
        return total + rank[:, 128:]

    return lax.fori_loop(first, last, count, total, unroll=7)


def place_list(at, mc, ic, lists, keep_m, keep_i, keep_rank, total, out):
    lists_n, chunks = lists.shape[0], lists.shape[0] * 4
    cells_m = at.na * mc
    lines = -(-(out.shape[0] // 3) // 8) * 8
    dummy = at.nm * at.nb * 2 * ic
    wide = dummy > 255
    groups = 5 if wide else 3
    mine = lax.broadcasted_iota(jnp.int32, (cells_m, 128), 0)
    lower = jnp.where(
        lax.broadcasted_iota(jnp.int32, (cells_m, cells_m), 0)
        > lax.broadcasted_iota(jnp.int32, (cells_m, cells_m), 1), 1.0, 0.0
    ).astype(F32)
    even = 2.0 * jnp.floor((total + 1.0) * 0.5)
    start = jnp.dot(lower, even, preferred_element_type=F32, precision=lax.Precision.HIGHEST)
    doubles = jnp.sum(even, axis=0, keepdims=True) * 0.5
    line = lax.broadcasted_iota(jnp.int32, (lines, 128), 0)
    column = lax.broadcasted_iota(jnp.int32, (128, 128), 0)

    def place(chunk, acc):
        m = keep_m[pl.ds(chunk, 1), :]
        i = keep_i[pl.ds(chunk, 1), :]
        hot = jnp.where(mine == m, 1.0, 0.0).astype(F32)
        spot = jnp.sum(hot * start, axis=0, keepdims=True) + keep_rank[pl.ds(chunk, 1), :]
        spot = jnp.where(m >= 0, spot.astype(jnp.int32), -1)
        double = jnp.right_shift(spot, 1)
        second = jnp.bitwise_and(spot, 1) == 1
        here = (line == jnp.right_shift(double, 7)) & (m >= 0)
        lane_hot = jnp.where(column == jnp.bitwise_and(double, 127), 1.0, 0.0).astype(BF16)
        zero = jnp.zeros((1, 128), F32)
        parts = [jnp.bitwise_and(i, 63), jnp.right_shift(i, 6)] if wide else [i]
        parts = [x.astype(F32) for x in parts]
        values = [jnp.where(second, zero, m.astype(F32))]
        values += [jnp.where(second, zero, x) for x in parts] + [jnp.where(second, x, zero) for x in parts]
        left = jnp.concatenate([jnp.where(here, v, 0.0) for v in values], axis=0).astype(BF16)
        return acc + lax.dot_general(left, lane_hot, (((1,), (1,)), ((), ())), preferred_element_type=F32)

    acc = lax.fori_loop(0, chunks, place, jnp.zeros((groups * lines, 128), F32), unroll=8)
    found = [acc[j * lines : (j + 1) * lines].astype(jnp.int32) for j in range(groups)]
    size = out.shape[0] // 3
    out[0:size, :] = found[0][0:size]
    for j in range(2):
        i = found[1 + 2 * j] + 64 * found[2 + 2 * j] if wide else found[1 + j]
        out[(j + 1) * size : (j + 2) * size, :] = jnp.where(i == 0, dummy, i - 1)[0:size]
    out[out.shape[0] - 1 :, :] = doubles.astype(jnp.int32)


def conc_rows(conc):
    conc = conc * RATE
    high = conc.astype(BF16).astype(F32)
    ones = jnp.full_like(conc, RATE)
    return jnp.concatenate([high, conc - high, ones, ones], axis=1).astype(BF16)


def fill_rows(conc, rows, slot):
    cells = conc.shape[1]
    rows[pl.ds(slot * cells, cells)] = conc_rows(conc[slot])


def share_plane(at, src, dst, sems, pass_sems):
    me = at.slot(0, 0, 0)
    copies = {
        (dp, db): remote(src, dst.at[me], sems, (dp, db), at.across(dp, db, 0)) for dp, db in at.plane()
    }
    return copies, {(0, 0): remote(src, dst.at[me], pass_sems, (0, 0), at.across(0, 0, 1))}


def pass_on(at, copies, passed, dst, pass_sems):
    for (dp, db), copy in copies.items():
        copy.wait_recv()
        block = dst.at[at.slot(-dp, -db, 0)]
        passed[dp, db] = remote(block, block, pass_sems, (dp, db), at.across(0, 0, 1))


def share_along(at, src, dst, sems):
    return {da: remote(src, dst.at[at.a], sems, da, at.along(da)) for da in range(1, at.na)}


def take_plane(at, copies, passed, conc, rows):
    for dp, db in copies:
        fill_rows(conc, rows, at.slot(-dp, -db, 0))
    for (dp, db), copy in passed.items():
        copy.wait_recv()
        fill_rows(conc, rows, at.slot(-dp, -db, 1))


def take_along(at, copies, conc, rows):
    for da, copy in copies.items():
        copy.wait_recv()
        fill_rows(conc, rows, at.am(-da))


def finish_sends(*groups):
    for group in groups:
        for copy in group.values():
            copy.wait_send()


def first_gather(n_mob, n_imm, mpos, walk, mconc, ipos, iconc, rows, cols, count,
                 g_conc, h_conc, m_rows, i_rows, x_all, y_one, pair_list, h_pos,
                 g_pos, lists, in_m, in_w, in_i, in_r, in_c, in_n, stage, keep_m, keep_i, keep_rank, *sems):
    at = Place(n_mob, n_imm)
    local = sems[0]
    z_pos, z_conc, p_pos, p_conc, c_pos, c_conc, l_sem = [sems[j : j + 2] for j in range(1, 15, 2)]
    me = at.slot(0, 0, 0)
    reads = [
        pltpu.make_async_copy(src, dst, local.at[j])
        for j, (src, dst) in enumerate((
            (mpos, in_m), (walk, in_w), (ipos, in_i), (rows, in_r), (cols, in_c), (count, in_n),
            (iconc, g_conc.at[at.a]), (mconc, h_conc.at[me]),
        ))
    ]
    for read in reads:
        read.start()
    sem, peers = at.greet(lists=True)
    clear_spare(h_conc, i_rows, y_one)
    reads[0].wait()
    reads[1].wait()
    moved = in_m[...] + in_w[0]
    h_pos[me, 0] = (moved - CENTRE) * SCALE
    h_pos[me, 1] = ((moved + in_w[1]) - CENTRE) * SCALE
    reads[2].wait()
    g_pos[at.a] = (in_i[...] - CENTRE) * SCALE
    for read in reads[3:6]:
        read.wait()
    home = at.p * at.na + at.a
    lane = lax.broadcasted_iota(jnp.int32, (1, 128), 1)
    for j in range(4):
        r = in_r[0, :, j * 128 : (j + 1) * 128]
        lists[home, j : j + 1, :] = jnp.where(j * 128 + lane < in_n[...], r, -1)
        lists[home, 4 + j : 5 + j, :] = in_c[0, :, j * 128 : (j + 1) * 128]
    build_x(g_pos.at[at.a], stage, x_all, at.a)
    build_y(h_pos.at[me, 0], stage, y_one, me)
    for read in reads[6:]:
        read.wait()
    fill_rows(g_conc, m_rows, at.a)
    fill_rows(h_conc, i_rows, me)
    mc, ic = iconc.shape[0], mconc.shape[0]
    total = count_list(at, mc, ic, lists, keep_m, keep_i, keep_rank, 0, 4, jnp.zeros((at.na * mc, 128), F32))
    pl.semaphore_wait(sem, peers)
    shared = {
        (dp, da): remote(lists.at[home], lists.at[home], l_sem, (dp, da), at.mate(dp, da)) for dp, da in at.mates()
    }
    z_far = share_along(at, g_pos.at[at.a], g_pos, z_pos)
    z_conc = share_along(at, g_conc.at[at.a], g_conc, z_conc)
    p_far, p_near = share_plane(at, h_pos.at[me], h_pos, p_pos, c_pos)
    p_conc, p_near_conc = share_plane(at, h_conc.at[me], h_conc, p_conc, c_conc)
    for copy in shared.values():
        copy.wait_recv()
    total = count_list(at, mc, ic, lists, keep_m, keep_i, keep_rank, 4, lists.shape[0] * 4, total)
    pass_on(at, p_far, p_near, h_pos, c_pos)
    place_list(at, mc, ic, lists, keep_m, keep_i, keep_rank, total, pair_list)
    pass_on(at, p_conc, p_near_conc, h_conc, c_conc)
    for dp, db in p_far:
        here = at.slot(-dp, -db, 0)
        build_y(h_pos.at[here, 0], stage, y_one, here)
    for (dp, db), copy in p_near.items():
        copy.wait_recv()
        here = at.slot(-dp, -db, 1)
        build_y(h_pos.at[here, 0], stage, y_one, here)
    for da, copy in z_far.items():
        copy.wait_recv()
        build_x(g_pos.at[at.am(-da)], stage, x_all, at.am(-da))
    take_plane(at, p_conc, p_near_conc, h_conc, i_rows)
    take_along(at, z_conc, g_conc, m_rows)
    finish_sends(z_far, z_conc, shared, p_far, p_near, p_conc, p_near_conc)


def clear_spare(h_conc, i_rows, y_all):
    h_conc[h_conc.shape[0] - 1] = jnp.zeros(h_conc.shape[1:], F32)
    i_rows[i_rows.shape[0] - 16 :] = jnp.zeros((16,) + i_rows.shape[1:], BF16)
    row = lax.broadcasted_iota(jnp.int32, (8, TERMS, 128), 1)
    y_all[y_all.shape[0] - 8 :] = jnp.where(row == 12, FAR, 0.0).astype(BF16)


def reduce_start(at, part_m, part_i, land_m, land_c, out_b, land_b, z_sem, c_sem, b_sem):
    mc, ic = land_m.shape[1], land_c.shape[2]
    c_copies = {
        (dp, db): remote(
            part_i.at[pl.ds(at.slot(dp, db, 1) * ic, ic)], land_c.at[dp, db], c_sem, (dp, db), at.across(0, 0, 1))
        for dp, db in at.plane() + [(0, 0)]
    }
    z_copies = {
        da: remote(part_m.at[pl.ds(at.am(da) * mc, mc)], land_m.at[da], z_sem, da, at.along(da))
        for da in range(1, at.na)
    }
    b_copies = {}
    for dp, db in at.plane():
        c_copies[dp, db].wait_recv()
        out_b[dp, db] = part_i[pl.ds(at.slot(dp, db, 0) * ic, ic)] + land_c[dp, db]
        b_copies[dp, db] = remote(out_b.at[dp, db], land_b.at[dp, db], b_sem, (dp, db), at.across(dp, db, 0))
    return z_copies, c_copies, b_copies


def reduce_end(base, part, slot, land, copies):
    cells = base.shape[0]
    total = base[...] + part[pl.ds(slot * cells, cells)]
    for key, copy in copies.items():
        copy.wait_recv()
        total = total + land[key]
    return total


def reduce_plane_end(at, base, part, land_c, land_b, c_copies, b_copies):
    c_copies[0, 0].wait_recv()
    return reduce_end(base, part, at.slot(0, 0, 0), land_b, b_copies) + land_c[0, 0]


def exchange(n_mob, n_imm, part_m, part_i, conc_m, conc_i, h_pos, own_m, own_i, g_conc, h_conc, m_rows, i_rows,
             y_two, land_m, land_c, out_b, land_b, stage, *sems):
    at = Place(n_mob, n_imm)
    z_sem, c_sem, b_sem, z_conc, p_conc, c_conc = [sems[j : j + 2] for j in range(0, 12, 2)]
    sem, peers = at.greet()
    clear_spare(h_conc, i_rows, y_two)
    pl.semaphore_wait(sem, peers)
    z_copies, c_copies, b_copies = reduce_start(
        at, part_m, part_i, land_m, land_c, out_b, land_b, z_sem, c_sem, b_sem)
    for slot in range(h_pos.shape[0]):
        build_y(h_pos.at[slot, 1], stage, y_two, slot)
    me = at.slot(0, 0, 0)
    own_i[...] = reduce_plane_end(at, conc_i, part_i, land_c, land_b, c_copies, b_copies)
    p_conc, p_near = share_plane(at, own_i, h_conc, p_conc, c_conc)
    own_m[...] = reduce_end(conc_m, part_m, at.a, land_m, z_copies)
    z_conc = share_along(at, own_m, g_conc, z_conc)
    g_conc[at.a] = own_m[...]
    h_conc[me] = own_i[...]
    fill_rows(g_conc, m_rows, at.a)
    fill_rows(h_conc, i_rows, me)
    pass_on(at, p_conc, p_near, h_conc, c_conc)
    take_plane(at, p_conc, p_near, h_conc, i_rows)
    take_along(at, z_conc, g_conc, m_rows)
    finish_sends(z_copies, c_copies, b_copies, z_conc, p_conc, p_near)


def last_reduce(n_mob, n_imm, part_m, part_i, conc_m, conc_i, own_m, own_i, land_m, land_c, out_b, land_b, *sems):
    at = Place(n_mob, n_imm)
    sem, peers = at.greet()
    pl.semaphore_wait(sem, peers)
    z_copies, c_copies, b_copies = reduce_start(
        at, part_m, part_i, land_m, land_c, out_b, land_b, sems[0:2], sems[2:4], sems[4:6])
    own_m[...] = reduce_end(conc_m, part_m, at.a, land_m, z_copies)
    own_i[...] = reduce_plane_end(at, conc_i, part_i, land_c, land_b, c_copies, b_copies)
    finish_sends(z_copies, c_copies, b_copies)


def pair_loop(pair_list, x_all, y_all, x_conc, y_conc, m_rows, i_rows, gain_m, gain_i,
              lst, p_even, p_odd, w_even, w_odd, sem):
    read = pltpu.make_async_copy(pair_list, lst, sem)
    read.start()
    gain_m[...] = jnp.zeros_like(gain_m)
    gain_i[...] = jnp.zeros_like(gain_i)
    read.wait()
    size = lst.shape[0] // 3 // 128 * 128
    used = lst[lst.shape[0] - 128]

    def entry(block, u):
        spot = block * UNROLL
        return lst[spot + u], lst[spot + (size + u)], lst[spot + (2 * size + u)]

    def measure(block, u, powers):
        m, i, k = entry(block, u)
        right = jnp.concatenate([y_all[i], y_all[k]], axis=1)
        powers[u] = jnp.dot(x_all[m][:, :TERMS], right, preferred_element_type=F32)

    def weigh(u, powers, weights):
        weights[u] = jnp.exp2(powers[u]).astype(BF16)

    def transfer(block, u, weights):
        m, i, k = entry(block, u)
        weight = weights[u]
        to_i = jnp.dot(m_rows[m], weight, preferred_element_type=F32)
        right = jnp.concatenate([i_rows[i], i_rows[k]], axis=1)
        to_m = lax.dot_general(right, weight, (((1,), (1,)), ((), ())), preferred_element_type=F32)
        return m, i, k, to_i, to_m

    def finish(m, i, k, to_i, to_m):
        gain_m[m] += to_m[0:8] + to_m[8:16] - to_m[16:24] * x_conc[m]
        gain_i[i] += to_i[0:8, :128] + to_i[8:16, :128] - to_i[16:24, :128] * y_conc[i]
        gain_i[k] += to_i[0:8, 128:] + to_i[8:16, 128:] - to_i[16:24, 128:] * y_conc[k]

    def step(block, first=None, second=None, third=None):
        moved = []
        for u in range(UNROLL):
            if second is not None:
                weigh(u, *second)
            if first is not None:
                measure(block, u, first)
            if third is not None:
                moved.append(transfer(block - 2, u, third))
        for item in moved:
            finish(*item)

    pairs = jnp.maximum(lax.div(used + (2 * UNROLL - 1), 2 * UNROLL), 1)
    step(0, p_even)
    step(1, p_odd, (p_even, w_even))

    def body(t, carry):
        step(2 * t, p_even, (p_odd, w_odd), w_even)
        step(2 * t + 1, p_odd, (p_even, w_even), w_odd)
        return carry

    lax.fori_loop(1, pairs, body, 0)
    step(2 * pairs, None, (p_odd, w_odd), w_even)
    step(2 * pairs + 1, None, None, w_odd)


def write_out(own_m, own_i, out_m, out_i, sems):
    copies = [
        pltpu.make_async_copy(src, dst, sems.at[j]) for j, (src, dst) in enumerate(((own_m, out_m), (own_i, out_i)))
    ]
    for copy in copies:
        copy.start()
    for copy in copies:
        copy.wait()


def on_device(n_mob, n_imm, mpos, walk, mconc, ipos, iconc, rows, cols, counts):
    nm, nb, na = sizes(n_mob, n_imm)
    mc, solutes, part = iconc.shape
    ic = mconc.shape[0]
    slots = nm * nb * 2
    cells_m, cells_i = na * mc, slots * ic
    tiles = nm * na
    chunks = tiles * 4
    lines = -(-(chunks * 64 + cells_m // 2 + 2 * UNROLL) // 128)
    list_rows = -(-(3 * lines + 1) // 8) * 8
    vmem = pl.BlockSpec(memory_space=pltpu.VMEM)
    anywhere = pl.BlockSpec(memory_space=pl.ANY)
    hbm = pl.BlockSpec(memory_space=pltpu.HBM)
    dma = pltpu.SemaphoreType.DMA

    def params(ident):
        return pltpu.CompilerParams(collective_id=ident, has_side_effects=True, vmem_limit_bytes=VMEM_LIMIT)

    def shape(dims, dtype=F32):
        return jax.ShapeDtypeStruct(dims, dtype)

    def pairs(*dims):
        return [dma(dims)] * 2

    cell_m, cell_i = (mc, solutes, part), (ic, solutes, part)
    all_m, all_i = (na,) + cell_m, (slots + 1,) + cell_i
    pos_m, pos_i = (3, mc, part), (3, ic, part)
    stage = pltpu.VMEM((max(mc, ic) * TERMS, part), F32)
    x_shape = shape((cells_m, part, 128), BF16)
    concs = (
        shape(all_m), shape(all_i),
        shape((cells_m, 4 * solutes, part), BF16), shape((cells_i + 16, 4 * solutes, part), BF16),
    )
    plane = (nm, nb)
    y_shape = shape((cells_i + 8, TERMS, part), BF16)
    *concs_one, x_all, y_one, pair_list, h_pos = pl.pallas_call(
        functools.partial(first_gather, n_mob, n_imm),
        out_shape=concs + (
            x_shape, y_shape, shape((list_rows, 128), jnp.int32), shape((slots, 2) + pos_i),
        ),
        in_specs=[hbm] * 8,
        out_specs=(vmem,) * 8,
        scratch_shapes=[
            pltpu.VMEM((na,) + pos_m, F32), pltpu.VMEM((tiles, 8, 128), jnp.int32),
            pltpu.VMEM(pos_i, F32), pltpu.VMEM((2,) + pos_i, F32), pltpu.VMEM(pos_m, F32),
            pltpu.VMEM(rows.shape, jnp.int32), pltpu.VMEM(cols.shape, jnp.int32), pltpu.VMEM((1, 1), jnp.int32),
            stage, pltpu.VMEM((chunks, 128), jnp.int32), pltpu.VMEM((chunks, 128), jnp.int32),
            pltpu.VMEM((chunks, 128), F32),
            dma((8,)), *pairs(na), *pairs(na), *pairs(*plane), *pairs(*plane), *pairs(*plane), *pairs(*plane),
            *pairs(nm, na),
        ],
        compiler_params=params(0),
    )(*[
        pltpu.with_memory_space_constraint(x, pltpu.HBM)
        for x in (jnp.transpose(mpos, (1, 0, 2)), jnp.transpose(walk, (0, 2, 1, 3)), mconc,
                  jnp.transpose(ipos, (1, 0, 2)), iconc, rows, cols)
    ], counts)
    flat_list = pair_list.reshape(-1)

    def gains(y_all, x_conc, y_conc, m_rows, i_rows):
        return pl.pallas_call(
            pair_loop,
            out_shape=(shape((cells_m, solutes, part)), shape((cells_i + 1, solutes, part))),
            in_specs=[anywhere] + [vmem] * 6,
            out_specs=(vmem,) * 2,
            scratch_shapes=[
                pltpu.SMEM((flat_list.shape[0],), jnp.int32),
                pltpu.VMEM((UNROLL, part, 256), F32), pltpu.VMEM((UNROLL, part, 256), F32),
                pltpu.VMEM((UNROLL, part, 256), BF16), pltpu.VMEM((UNROLL, part, 256), BF16),
                dma,
            ],
            compiler_params=pltpu.CompilerParams(vmem_limit_bytes=VMEM_LIMIT),
        )(flat_list, x_all, y_all, x_conc.reshape((cells_m, solutes, part)),
          y_conc.reshape((cells_i + ic, solutes, part)), m_rows, i_rows)

    lands = [pltpu.VMEM((na,) + cell_m, F32)] + [pltpu.VMEM(plane + cell_i, F32)] * 3
    own = (shape(cell_m), shape(cell_i))
    part_m, part_i = gains(y_one, *concs_one)
    own_m, own_i, *concs_two, y_two = pl.pallas_call(
        functools.partial(exchange, n_mob, n_imm),
        out_shape=own + concs + (y_shape,),
        in_specs=[vmem] * 5,
        out_specs=(vmem,) * 7,
        scratch_shapes=lands + [stage, *pairs(na), *pairs(*plane), *pairs(*plane),
                                *pairs(na), *pairs(*plane), *pairs(*plane)],
        compiler_params=params(1),
    )(part_m, part_i, iconc, mconc, h_pos)
    part_m, part_i = gains(y_two, *concs_two)
    own_m, own_i = pl.pallas_call(
        functools.partial(last_reduce, n_mob, n_imm),
        out_shape=own,
        in_specs=[vmem] * 4,
        out_specs=(vmem,) * 2,
        scratch_shapes=lands + [*pairs(na), *pairs(*plane), *pairs(*plane)],
        compiler_params=params(2),
    )(part_m, part_i, own_m, own_i)
    return pl.pallas_call(
        write_out,
        out_shape=own[::-1],
        in_specs=[vmem] * 2,
        out_specs=(anywhere,) * 2,
        scratch_shapes=[dma((2,))],
        compiler_params=pltpu.CompilerParams(vmem_limit_bytes=VMEM_LIMIT),
    )(own_i, own_m)


def solution(mesh):
    return jax.shard_map(
        functools.partial(on_device, mesh.shape["mob"], mesh.shape["imm"]),
        mesh=mesh,
        in_specs=(
            P(("mob", "imm"), None, None),
            P(None, ("mob", "imm"), None, None),
            P(("mob", "imm"), None, None),
            P(("mob", "imm"), None, None),
            P(("mob", "imm"), None, None),
            P("mob", "imm", None),
            P("mob", "imm", None),
            P("mob", "imm"),
        ),
        out_specs=(P(("mob", "imm"), None, None), P(("mob", "imm"), None, None)),
        check_vma=False,
    )
```
